512 devices in a mesh: tile: 32 (over z, y_lo), member: 16 (over y_hi, x, core).
Axes of the slice: x: 4, y: 4 (y_hi: 2, y_lo: 2; y = y_hi * 2 + y_lo), z: 16, core: 2. Of those that a mesh axis runs over, the one named last changes fastest.
Arguments:
- perturbations: bfloat16 [32, 6, 512, 512], P('member', None, 'tile'), may hold values from -6 to 6
- control: float32 [6, 512, 512], P(None, 'tile'), may hold values from -6 to 6
- band_rows: float32 [512, 25], P('tile'), may hold values from 0.5 to 2
- band_cols: float32 [512, 25], replicated, may hold values from 0.5 to 2
- edge_peer: int32 [6, 4], replicated, may hold values from 0 to 23, as said below
- edge_flip: int32 [6, 4], replicated, may hold values from 0 to 1, as said below
Outputs:
- increment: float32 [6, 512, 512], P(None, 'tile')
The draws below stay inside these ranges and needn't reach their ends.
Inputs may be any that keep to these rules, and one draw needn't show every extreme that they name: The faces are those of a cube: edge_peer pairs the 24 face edges two by two (the neighbour of the neighbour is the edge itself, never on the same face), and cells line up one to one along each shared edge. `edge_flip`: equal on both sides of each shared edge.
All inputs are finite; a program needn't handle non-finite values.
Results may differ from the reference program's by a relative error of at most 0.0033.
Values may be sent and summed in bfloat16 or wider, within the bound.
A program may use at most 64 MiB of HBM per device.

```python
import math
import jax
import jax.numpy as jnp
from jax import lax

FACES = 6
HALF = 12
NF = 512
MEMBERS = 32


def cube_links(key):
    key = jax.random.fold_in(key, 11)
    order_key, turn_key = jax.random.split(key)
    order = jax.random.permutation(order_key, 6)
    turns = jax.random.randint(turn_key, (6, 1), 0, 4)
    normals = jnp.array([[1, 0, 0], [-1, 0, 0], [0, 1, 0], [0, -1, 0], [0, 0, 1], [0, 0, -1]], jnp.int32)
    first_axis = jnp.array([[0, 1, 0], [0, 0, 1], [0, 0, 1], [1, 0, 0], [1, 0, 0], [0, 1, 0]], jnp.int32)
    second_axis = jnp.array([[0, 0, 1], [0, 1, 0], [1, 0, 0], [0, 0, 1], [0, 1, 0], [1, 0, 0]], jnp.int32)
    normal = jnp.take(normals, order, axis=0)
    along_a = jnp.take(first_axis, order, axis=0)
    along_b = jnp.take(second_axis, order, axis=0)
    frame_a = jnp.where(turns == 0, along_a, jnp.where(turns == 1, along_b, jnp.where(turns == 2, -along_a, -along_b)))
    frame_b = jnp.where(turns == 0, along_b, jnp.where(turns == 1, -along_a, jnp.where(turns == 2, -along_b, along_a)))
    middles = jnp.stack([normal - frame_a, normal + frame_a, normal - frame_b, normal + frame_b], axis=1).reshape(24, 3)
    directions = jnp.stack([frame_b, frame_b, frame_a, frame_a], axis=1).reshape(24, 3)
    labels = (middles[:, 0] + 1) * 9 + (middles[:, 1] + 1) * 3 + (middles[:, 2] + 1)
    matches = (labels[:, None] == labels[None, :]) & (jnp.arange(24)[:, None] != jnp.arange(24)[None, :])
    partner = jnp.argmax(matches.astype(jnp.int32), axis=1).astype(jnp.int32)
    products = jnp.sum(directions * jnp.take(directions, partner, axis=0), axis=1)
    turned = (products < 0).astype(jnp.int32)
    return (partner.reshape(6, 4), turned.reshape(6, 4))


def draw_edge_peer(key, part):
    return cube_links(key)[0]


def draw_edge_flip(key, part):
    return cube_links(key)[1]


def shard_levels(own_key, shape, cuts, least, largest):
    gain, own = 1.0, jax.random.fold_in(own_key, 6)
    for dim, blocks in cuts:
        draws = jnp.exp(jax.random.uniform(jax.random.fold_in(own, dim), (blocks,), jnp.float32, least / len(cuts), largest / len(cuts)))
        gain = gain * jnp.repeat(draws, shape[dim] // blocks).reshape([-1 if axis == dim else 1 for axis in range(len(shape))])
    return gain


def noise(stream_key, extent, deviation, limit, pieces=(), held_as=jnp.bfloat16):
    values = jax.random.normal(stream_key, extent, jnp.float32) * deviation
    if len(pieces) > 0:
        values = shard_levels(stream_key, extent, pieces, -0.22, 0.18) * values
    return jnp.clip(values, min=-limit, max=limit).astype(held_as)


def setup_inputs(seed: int = 0) -> dict:
    key_of = jax.random.split(jax.random.key(seed), 7)
    perturbations = noise(key_of[0], (MEMBERS, FACES, NF, NF), 1.0, 6.0, ((0, 16), (2, 32)))
    control = noise(key_of[1], (FACES, NF, NF), 1.0, 6.0, ((1, 32),), jnp.float32)
    band_rows = jnp.clip(jnp.exp(math.log(2.0) - 1.3862944 * jax.random.uniform(key_of[2], (NF, 2 * HALF + 1), jnp.float32) ** shard_levels(key_of[2], (NF, 2 * HALF + 1), ((0, 32),), -0.2, 0.2)), 0.5, 2.0)
    band_cols = jnp.clip(jnp.exp(jax.random.uniform(key_of[3], (NF, 2 * HALF + 1), jnp.float32, math.log(0.5), math.log(2.0))), 0.5, 2.0)
    edge_peer = draw_edge_peer(jax.random.fold_in(key_of[6], 71), 0)
    edge_flip = draw_edge_flip(jax.random.fold_in(key_of[6], 71), 0)
    return dict(perturbations=perturbations, control=control, band_rows=band_rows, band_cols=band_cols, edge_peer=edge_peer, edge_flip=edge_flip)


def filter_taps(band, half_width):
    tap_count = 2 * half_width + 1
    offsets = jnp.arange(tap_count, dtype=jnp.float32) - half_width
    taper_curve = jnp.exp(-(offsets / half_width) ** 2)
    normalizer = 1.0 / jnp.sqrt(jnp.sqrt(jnp.sum(taper_curve * taper_curve)) * jnp.sum(taper_curve))
    return (band * (taper_curve * normalizer)[None, :]).astype(jnp.bfloat16)

def edge_strips(field, half_width):
    edge_cells = field.shape[-1]
    first = field[:, :half_width, :]
    second = field[:, edge_cells - half_width:, :][:, ::-1, :]
    third = jnp.swapaxes(field[:, :, :half_width], 1, 2)
    fourth = jnp.swapaxes(field[:, :, edge_cells - half_width:][:, :, ::-1], 1, 2)
    return jnp.stack([first, second, third, fourth], axis=1)

def arriving(strips, edge_peer, edge_flip):
    face_count, half_width, edge_cells = (strips.shape[0], strips.shape[2], strips.shape[3])
    flattened = strips.reshape(face_count * 4, half_width, edge_cells)
    picked = jnp.take(flattened, edge_peer.reshape(-1), axis=0)
    turned = jnp.where(edge_flip.reshape(-1)[:, None, None] == 1, picked[:, :, ::-1], picked)
    return turned.reshape(face_count, 4, half_width, edge_cells)

def fold_edges(base, arrived):
    half_width, edge_cells = (arrived.shape[2], arrived.shape[3])
    base = base.at[:, :half_width, :].add(arrived[:, 0])
    base = base.at[:, edge_cells - half_width:, :].add(arrived[:, 1][:, ::-1, :])
    base = base.at[:, :, :half_width].add(jnp.swapaxes(arrived[:, 2], 1, 2))
    base = base.at[:, :, edge_cells - half_width:].add(jnp.swapaxes(arrived[:, 3][:, ::-1, :], 1, 2))
    return base

def forward_rows(field, taps_rows, edge_peer, edge_flip):
    half_width = taps_rows.shape[1] // 2
    edge_cells = field.shape[-1]
    arrived = arriving(edge_strips(field, half_width), edge_peer, edge_flip)
    padded = jnp.concatenate([arrived[:, 0][:, ::-1, :], field, arrived[:, 1]], axis=1).astype(jnp.float32)
    taps_wide = taps_rows.astype(jnp.float32)
    result = jnp.zeros(field.shape, jnp.float32)
    for offset in range(2 * half_width + 1):
        result = result + taps_wide[:, offset][None, :, None] * padded[:, offset:offset + edge_cells, :]
    return result.astype(jnp.bfloat16)

def forward_cols(field, taps_cols, edge_peer, edge_flip):
    half_width = taps_cols.shape[1] // 2
    edge_cells = field.shape[-1]
    arrived = arriving(edge_strips(field, half_width), edge_peer, edge_flip)
    left_side = jnp.swapaxes(arrived[:, 2][:, ::-1, :], 1, 2)
    right_side = jnp.swapaxes(arrived[:, 3], 1, 2)
    padded = jnp.concatenate([left_side, field, right_side], axis=2).astype(jnp.float32)
    taps_wide = taps_cols.astype(jnp.float32)
    result = jnp.zeros(field.shape, jnp.float32)
    for offset in range(2 * half_width + 1):
        result = result + taps_wide[:, offset][None, None, :] * padded[:, :, offset:offset + edge_cells]
    return result.astype(jnp.bfloat16)

def adjoint_cols(field, taps_cols, edge_peer, edge_flip):
    half_width = taps_cols.shape[1] // 2
    face_count, edge_cells = (field.shape[0], field.shape[-1])
    taps_wide = taps_cols.astype(jnp.float32)
    values = field.astype(jnp.float32)
    spread = jnp.zeros((face_count, edge_cells, edge_cells + 2 * half_width), jnp.float32)
    for offset in range(2 * half_width + 1):
        spread = spread.at[:, :, offset:offset + edge_cells].add(taps_wide[:, offset][None, None, :] * values)
    interior = spread[:, :, half_width:half_width + edge_cells]
    empty_rims = jnp.zeros((face_count, half_width, edge_cells), jnp.float32)
    third = jnp.swapaxes(spread[:, :, :half_width][:, :, ::-1], 1, 2)
    fourth = jnp.swapaxes(spread[:, :, edge_cells + half_width:], 1, 2)
    rims = jnp.stack([empty_rims, empty_rims, third, fourth], axis=1).astype(jnp.bfloat16)
    arrived = arriving(rims, edge_peer, edge_flip).astype(jnp.float32)
    return fold_edges(interior, arrived).astype(jnp.bfloat16)

def adjoint_rows(field, taps_rows, edge_peer, edge_flip):
    half_width = taps_rows.shape[1] // 2
    face_count, edge_cells = (field.shape[0], field.shape[-1])
    taps_wide = taps_rows.astype(jnp.float32)
    values = field.astype(jnp.float32)
    spread = jnp.zeros((face_count, edge_cells + 2 * half_width, edge_cells), jnp.float32)
    for offset in range(2 * half_width + 1):
        spread = spread.at[:, offset:offset + edge_cells, :].add(taps_wide[:, offset][None, :, None] * values)
    interior = spread[:, half_width:half_width + edge_cells, :]
    empty_rims = jnp.zeros((face_count, half_width, edge_cells), jnp.float32)
    first = spread[:, :half_width, :][:, ::-1, :]
    second = spread[:, edge_cells + half_width:, :]
    rims = jnp.stack([first, second, empty_rims, empty_rims], axis=1).astype(jnp.bfloat16)
    arrived = arriving(rims, edge_peer, edge_flip).astype(jnp.float32)
    return fold_edges(interior, arrived)

def reference(perturbations, control, band_rows, band_cols, edge_peer, edge_flip):
    taps_rows = filter_taps(band_rows, HALF)
    taps_cols = filter_taps(band_cols, HALF)

    def add_member(member_index, running):
        member = lax.dynamic_index_in_dim(perturbations, member_index, 0, keepdims=False)
        member_wide = member.astype(jnp.float32)
        weighted = (member_wide * control).astype(jnp.bfloat16)
        section = forward_rows(weighted, taps_rows, edge_peer, edge_flip)
        section = forward_cols(section, taps_cols, edge_peer, edge_flip)
        section = adjoint_cols(section, taps_cols, edge_peer, edge_flip)
        filtered = adjoint_rows(section, taps_rows, edge_peer, edge_flip)
        return running + member_wide * filtered
    running = lax.fori_loop(0, MEMBERS, add_member, jnp.zeros(control.shape, jnp.float32))
    return running / (MEMBERS - 1.0)
```

```python
import functools
import math

import jax
import jax.numpy as jnp
import numpy as np
from jax import lax
from jax.experimental import pallas as pl
from jax.experimental.pallas import tpu as pltpu
from jax.sharding import PartitionSpec as P

HALF = 12
ROWS = 16
FACES = 6
LANES = 128
FR = FACES * ROWS
COLW = 256
FLIPPED = 24 << 4
f32, bf16, i32 = jnp.float32, jnp.bfloat16, jnp.int32


def iota(shape, dim):
    return lax.broadcasted_iota(i32, shape, dim)


def dot(a, b):
    return lax.dot_general(a, b, (((1,), (0,)), ((), ())), preferred_element_type=f32)


def dot_nt(a, b):
    return lax.dot_general(a, b, (((1,), (1,)), ((), ())), preferred_element_type=f32)


def dot_tn(a, b):
    return lax.dot_general(a, b, (((0,), (0,)), ((), ())), preferred_element_type=f32)


def onehot(mask):
    return jnp.where(mask, 1.0, 0.0).astype(bf16)


def taper(band):
    rows, taps = band.shape
    steps = np.arange(2 * HALF + 1, dtype=np.float32) - HALF
    curve = np.exp(-((steps / HALF) ** 2))
    scale = 1.0 / math.sqrt(math.sqrt(float(np.sum(curve * curve))) * float(np.sum(curve)))
    lane = iota((1, taps), 1).astype(f32)
    g = jnp.exp(-(((lane - HALF) / HALF) ** 2)) * scale
    wide = jnp.concatenate([band * g, jnp.zeros((rows, LANES - taps), f32)], axis=1)
    return wide.astype(bf16).astype(f32)


def col_key(lane):
    face, rest = lane >> 5, lane & 31
    second = rest >= HALF
    layer = jnp.where(second, rest - HALF, rest)
    edge = jnp.where(second, 3, 2)
    good = (rest < 2 * HALF) & (face < FACES)
    return jnp.where(good, ((4 * face + edge) << 4) + layer, -1)


def row_key(index, edge, backwards):
    face, rest = index >> 4, index & 15
    layer = ROWS - 1 - rest if backwards else rest
    good = (layer < HALF) & (face < FACES)
    return jnp.where(good, ((4 * face + edge) << 4) + layer, -1)


def wanted_cols(lane, peer, flip):
    face, rest = lane >> 5, lane & 31
    second = rest >= HALF
    layer = jnp.where(second, rest - HALF, rest)
    good = (rest < 2 * HALF) & (face < FACES)
    base = jnp.zeros(lane.shape, i32)
    for f in range(FACES):
        for e in (2, 3):
            here = (face == f) & (second == (e == 3))
            base = jnp.where(here, (peer[f, e] << 4) + flip[f, e] * FLIPPED, base)
    return jnp.where(good, base + layer, -2)


def wanted_rows(index, peer, flip, hub, backwards):
    turned = index >= FR
    within = jnp.where(turned, index - FR, index)
    face, rest = within >> 4, within & 15
    layer = jnp.where(backwards, ROWS - 1 - rest, rest)
    base = jnp.zeros(index.shape, i32)
    here_turned = jnp.zeros(index.shape, i32)
    for f in range(FACES):
        base = jnp.where(face == f, peer[f, hub] << 4, base)
        here_turned = jnp.where(face == f, flip[f, hub], here_turned)
    good = (layer < HALF) & ((here_turned == 1) == turned)
    return jnp.where(good, base + layer, -2)


def tile_kernel(
    tiles, members,
    pert, control, band_rows, band_cols, peer, flip, out,
    wp, pa, pall_a, pb, pb_mir, qb, qr_b, pc, pc_mir, pall_c, ds, drs, qd, qr_d,
    dmat, xs, zacc, bd, bdt, jn, gmat,
    ring_s, ring_r, hub_s, hub_r, mir_s, mir_r, sc_s, sc_r,
):
    T, M = tiles, members
    N = ROWS * T
    NB = N // LANES
    t = lax.axis_index("tile")
    prev, nxt, mirror = lax.rem(t + T - 1, T), lax.rem(t + 1, T), T - 1 - t
    hub = jnp.where(t == T - 1, 1, 0)
    is_hub = (t == 0) | (t == T - 1)
    last = hub == 1

    def remote(src, dst, send, recv, where):
        return pltpu.make_async_remote_copy(
            src_ref=src, dst_ref=dst, send_sem=send, recv_sem=recv,
            device_id={"tile": where}, device_id_type=pl.DeviceIdType.MESH,
        )

    barrier = pltpu.get_barrier_semaphore()

    def greet(where):
        pl.semaphore_signal(
            barrier, inc=1, device_id={"tile": where}, device_id_type=pl.DeviceIdType.MESH
        )

    for where in (prev, nxt, mirror):
        greet(where)

    @pl.when(is_hub)
    def _():
        def body(i, carry):
            greet(lax.rem(t + i, T))
            return carry

        lax.fori_loop(1, T, body, 0)

    @pl.when(jnp.logical_not(is_hub))
    def _():
        greet(0)
        greet(T - 1)

    r256, c128 = iota((2 * LANES, LANES), 0), iota((2 * LANES, LANES), 1) & 31
    sel = onehot(
        ((r256 < HALF) & (c128 == r256))
        | ((r256 >= 2 * LANES - HALF) & (c128 == HALF + 2 * LANES - 1 - r256))
    )
    group = iota((ROWS, LANES), 1) >> 5

    def pack(quad):
        packs = []
        for m in range(M):
            blocks = []
            for g in range(2):
                block = jnp.zeros((ROWS, LANES), f32)
                for q in range(4):
                    f = 4 * g + q
                    if f < FACES:
                        at = (m * FACES + f) * ROWS
                        block = jnp.where(group == q, quad[at : at + ROWS], block)
                blocks.append(block)
            packs.append(jnp.concatenate(blocks, axis=1).astype(bf16))
        return packs

    def pack_ends(flat):
        ends = jnp.concatenate([flat[:, :LANES], flat[:, N - LANES :]], axis=1)
        return pack(dot(ends, sel))

    def spread(packs):
        parts = []
        for m in range(M):
            for f in range(FACES):
                g, q = f // 4, f % 4
                block = packs[m][:, g * LANES : (g + 1) * LANES]
                parts.append(jnp.where(group == q, block, 0.0))
        return jnp.concatenate(parts, axis=0).astype(bf16)

    for m in range(M):
        wp[1, m] = (pert[m].astype(f32) * control[...]).astype(bf16)
    own = wp[1].reshape(M * FR, N)
    for m, value in enumerate(pack_ends(own)):
        pa[m] = value

    @pl.when(is_hub)
    def _():
        pl.semaphore_wait(barrier, 3 + T - 1)

    @pl.when(jnp.logical_not(is_hub))
    def _():
        pl.semaphore_wait(barrier, 5)

    ring_a = [
        remote(wp.at[1], wp.at[2], ring_s.at[0], ring_r.at[0], prev),
        remote(wp.at[1], wp.at[0], ring_s.at[1], ring_r.at[1], nxt),
    ]
    for copy in ring_a:
        copy.start()

    def hub_copies(src, dst, base):
        return [
            remote(src, dst.at[:, t], hub_s.at[base + h], hub_r.at[base // 2], h * (T - 1))
            for h in range(2)
        ]

    def start_to_hubs(copies):
        for h in range(2):
            @pl.when(t != h * (T - 1))
            def _():
                copies[h].start()

    def finish_to_hubs(copies):
        for h in range(2):
            @pl.when(t != h * (T - 1))
            def _():
                copies[h].wait_send()

    def wait_at_hub(dst, base):
        others = dst.at[:, pl.ds(0, T - 1)]
        pltpu.make_async_copy(others, others, hub_r.at[base // 2]).wait()

    to_hubs_a = hub_copies(pa, pall_a, 0)
    start_to_hubs(to_hubs_a)

    lane = iota((LANES, LANES), 1)
    blocks = {}
    for b in range(NB):
        wide = taper(band_cols[b * LANES : (b + 1) * LANES, :])
        wide = jnp.concatenate([wide, jnp.zeros((LANES, LANES), f32)], axis=1)
        wide = pltpu.roll(wide, 0, 1, stride=1, stride_axis=0)
        wide = pltpu.roll(wide, 2 * LANES - HALF, 1)
        over = wide[:, LANES:]
        for c, value in (
            (b, wide[:, :LANES]),
            ((b + 1) % (NB + 1), jnp.where(lane < HALF, over, 0.0)),
            ((b + NB) % (NB + 1), jnp.where(lane >= LANES - HALF, over, 0.0)),
        ):
            blocks[b, c] = blocks[b, c] + value if (b, c) in blocks else value
    from_lane, to_lane = iota((LANES, LANES), 0), iota((LANES, LANES), 1) & 31
    rim_order = onehot(
        ((to_lane < HALF) & (from_lane == LANES - 1 - to_lane))
        | ((to_lane >= HALF) & (to_lane < 2 * HALF) & (from_lane == to_lane - HALF))
    )
    for b in range(NB):
        for c in range(NB + 1):
            value = blocks.get((b, c))
            value = jnp.zeros((LANES, LANES), bf16) if value is None else value.astype(bf16)
            if c == NB:
                value = dot(value, rim_order).astype(bf16)
            dmat[b * LANES : (b + 1) * LANES, c * LANES : (c + 1) * LANES] = value

    taps = taper(band_rows[...])
    base = jnp.concatenate([taps, jnp.zeros((ROWS, LANES), f32)], axis=1)
    skew = pltpu.roll(base, ROWS - HALF, 1, stride=1, stride_axis=0)
    skew = skew[:, :LANES].astype(bf16)
    six = jnp.concatenate([skew] * FACES, axis=0)
    e0, e1 = iota((LANES, 3 * LANES), 0), iota((LANES, 3 * LANES), 1)
    expand = onehot((e0 == ((e1 >> 7) << 4) + (e1 & 15)) & ((e1 & 127) < FR))
    k0, k1 = iota((FR, 3 * LANES), 0), iota((FR, 3 * LANES), 1)
    band = jnp.where((k0 >> 4) == ((k1 & 127) >> 4), dot(six, expand), 0.0)
    for p in range(3):
        part = band[:, p * LANES : (p + 1) * LANES]
        bd[p] = part[:, :FR].astype(bf16)
        square = jnp.concatenate([part, jnp.zeros((LANES - FR, LANES), f32)], axis=0)
        bdt[p] = jnp.transpose(square)[:FR, :FR].astype(bf16)

    want = wanted_cols(iota((COLW, COLW), 1), peer, flip)
    src = iota((COLW, COLW), 0)
    from_cols = col_key(src)
    upper = src < LANES
    from_rows = row_key(jnp.where(upper, src, src - LANES), jnp.where(upper, 0, 1), False)
    turn = jnp.where(want >= FLIPPED, want - FLIPPED, want)
    straight = want < FLIPPED
    is_cols, is_rows = from_cols == turn, from_rows == turn
    gmat[0] = onehot(is_cols & straight)
    gmat[1] = onehot(is_rows & straight)
    gmat[2] = onehot(is_cols & jnp.logical_not(straight))
    gmat[3] = onehot(is_rows & jnp.logical_not(straight))
    back = onehot(iota((ROWS, ROWS), 0) + iota((ROWS, ROWS), 1) == ROWS - 1)

    @pl.when(is_hub)
    def _():
        jn[...] = onehot(iota((N, N), 0) + iota((N, N), 1) == N - 1)

    def gather_rows(cols, rows, store, dst_back, src_back):
        want_r = wanted_rows(iota((2 * FR, COLW), 0), peer, flip, hub, dst_back)
        s_cols = onehot(want_r == col_key(iota((2 * FR, COLW), 1)))
        if rows is not None:
            want_e = wanted_rows(iota((2 * FR, FR), 0), peer, flip, hub, dst_back)
            s_rows = [
                onehot(want_e == row_key(iota((2 * FR, FR), 1), h, src_back[h]))
                for h in range(2)
            ]
        for m in range(M):
            total = jnp.zeros((2 * FR, N), f32)
            if cols is not None:
                total = total + dot_nt(s_cols, cols[m].reshape(N, COLW))
            if rows is not None:
                total = total + dot(s_rows[0], rows[1 + hub, m].reshape(FR, N))
                total = total + dot(s_rows[1], rows[hub, m].reshape(FR, N))
            store(m, total[:FR] + dot(total[FR:].astype(bf16), jn[...]))

    def scatter(flat, q, qr, base, back_of_first):
        s0, s1 = iota((FR, LANES), 0), iota((FR, LANES), 1)
        row = s0 & 15
        layer = jnp.where(last != back_of_first, ROWS - 1 - row, row)
        pick = onehot((layer < HALF) & (s1 == ((s0 >> 4) << 4) + layer))
        for m in range(M):
            q[m] = dot_tn(flat(m), pick).astype(bf16).reshape(T, ROWS, LANES)

        def body(i, carry):
            there = lax.rem(t + i, T)
            for turned, block in ((0, there), (1, T - 1 - there)):
                remote(
                    q.at[:, block], qr.at[hub, turned],
                    sc_s.at[base, turned], sc_r.at[base, hub, turned], there,
                ).start()
            return carry

        lax.fori_loop(1, T, body, 0)
        qr[hub, 0] = q[:, t]
        qr[hub, 1] = q[:, mirror]

    def finish_scatter(q, base):
        others = q.at[:, pl.ds(0, T - 1)]
        for turned in range(2):
            pltpu.make_async_copy(others, others, sc_s.at[base, turned]).wait()

    def wait_scatter(q, qr, base):
        for h in range(2):
            @pl.when(t != h * (T - 1))
            def _():
                for turned in range(2):
                    remote(
                        q.at[:, 0], qr.at[h, turned],
                        sc_s.at[base, turned], sc_r.at[base, h, turned], h * (T - 1),
                    ).wait_recv()

    def arrive_cols(direct, mirrored, qr):
        packs = []
        for m in range(M):
            straight, turned = jnp.zeros((ROWS, COLW), f32), jnp.zeros((ROWS, COLW), f32)
            if direct is not None:
                straight = straight + dot(direct[m], gmat[0])
                turned = turned + dot(mirrored[m], gmat[2])
            if qr is not None:
                near = jnp.concatenate([qr[0, 0, m], qr[1, 0, m]], axis=1)
                far = jnp.concatenate([qr[0, 1, m], qr[1, 1, m]], axis=1)
                straight = straight + dot(near, gmat[1])
                turned = turned + dot(far, gmat[3])
            packs.append(straight + dot(back, turned.astype(bf16)))
        return packs

    for copy in ring_a:
        copy.wait_recv()

    @pl.when(is_hub)
    def _():
        pall_a[:, t] = pa[...]
        wait_at_hub(pall_a, 0)
        got = [None] * M

        def keep(m, value):
            got[m] = value.astype(bf16).reshape(FACES, ROWS, N)

        gather_rows(pall_a, wp, keep, jnp.logical_not(last), (False, True))
        for m in range(M):
            wp[2 * hub, m] = got[m]

    for m in range(M):
        x = dot(bd[0], wp[0, m].reshape(FR, N))
        x = x + dot(bd[1], wp[1, m].reshape(FR, N))
        x = x + dot(bd[2], wp[2, m].reshape(FR, N))
        xs[m * FR : (m + 1) * FR, :N] = x.astype(bf16)

    @pl.when(is_hub)
    def _():
        scatter(lambda m: xs[m * FR : (m + 1) * FR, :N], qb, qr_b, 0, False)

    for m, value in enumerate(pack_ends(xs[:, :N])):
        pb[m] = value
    mirror_b = remote(pb, pb_mir, mir_s.at[0], mir_r.at[0], mirror)
    mirror_b.start()
    mirror_b.wait_recv()
    wait_scatter(qb, qr_b, 0)
    xs[:, N:] = spread(arrive_cols(pb, pb_mir, qr_b))
    y = dot_nt(xs[...], dmat[...]).astype(bf16)

    zrim = dot(y, dmat[:, N:])
    for m, value in enumerate(pack(zrim)):
        pc[m] = value
    mirror_c = remote(pc, pc_mir, mir_s.at[1], mir_r.at[1], mirror)
    mirror_c.start()
    to_hubs_c = hub_copies(pc, pall_c, 2)
    start_to_hubs(to_hubs_c)
    zacc[...] = dot(y, dmat[:, :N])
    mirror_c.wait_recv()

    @pl.when(is_hub)
    def _():
        pall_c[:, t] = pc[...]
        wait_at_hub(pall_c, 2)

        def add(m, value):
            zacc[m * FR : (m + 1) * FR, :] += value

        gather_rows(pall_c, None, add, last, None)

    ends = dot_nt(spread(arrive_cols(pc, pc_mir, None)), sel)
    zacc[:, :LANES] += ends[:, :LANES]
    zacc[:, N - LANES :] += ends[:, LANES:]

    ring_d = [
        remote(ds.at[0], drs.at[2], ring_s.at[2], ring_r.at[2], prev),
        remote(ds.at[1], drs.at[0], ring_s.at[3], ring_r.at[3], nxt),
    ]
    for m in range(M):
        z = zacc[m * FR : (m + 1) * FR, :].astype(bf16)
        ds[0, m] = dot(bdt[0], z).astype(bf16).reshape(FACES, ROWS, N)
        ds[1, m] = dot(bdt[2], z).astype(bf16).reshape(FACES, ROWS, N)
        zacc[m * FR : (m + 1) * FR, :] = dot(bdt[1], z)
    for copy in ring_d:
        copy.start()

    @pl.when(is_hub)
    def _():
        scatter(lambda m: ds[hub, m].reshape(FR, N), qd, qr_d, 1, True)
        drs[1] = ds[hub]

    for copy in ring_d:
        copy.wait_recv()

    @pl.when(is_hub)
    def _():
        got = [None] * M

        def keep(m, value):
            got[m] = value.astype(bf16).reshape(FACES, ROWS, N)

        gather_rows(None, drs, keep, last, (True, False))
        for m in range(M):
            drs[2 * hub, m] = got[m]

    wait_scatter(qd, qr_d, 1)
    ends = dot_nt(spread(arrive_cols(None, None, qr_d)), sel)
    zacc[:, :LANES] += ends[:, :LANES]
    zacc[:, N - LANES :] += ends[:, LANES:]

    total = jnp.zeros((FR, N), f32)
    for m in range(M):
        spill = drs[0, m].astype(f32) + drs[2, m].astype(f32)
        filtered = zacc[m * FR : (m + 1) * FR, :] + spill.reshape(FR, N)
        total = total + pert[m].astype(f32).reshape(FR, N) * filtered
    chunks, per_chunk = out.shape[:2]
    for u in range(chunks * per_chunk):
        r, c = u // NB, u % NB
        out[u // per_chunk, u % per_chunk] = total[r * 8 : r * 8 + 8, c * LANES : (c + 1) * LANES]

    for copy in ring_a + ring_d + [mirror_b, mirror_c]:
        copy.wait_send()
    finish_to_hubs(to_hubs_a)
    finish_to_hubs(to_hubs_c)

    @pl.when(is_hub)
    def _():
        finish_scatter(qb, 0)
        finish_scatter(qd, 1)


def member_kernel(count, ensemble, part, out, got, mine, done, s1, r1, s2, r2):
    me = lax.axis_index("member")

    def remote(src, dst, send, recv, where):
        return pltpu.make_async_remote_copy(
            src_ref=src, dst_ref=dst, send_sem=send, recv_sem=recv,
            device_id={"member": where}, device_id_type=pl.DeviceIdType.MESH,
        )

    barrier = pltpu.get_barrier_semaphore()
    for i in range(1, count):
        pl.semaphore_signal(
            barrier, inc=1, device_id={"member": lax.rem(me + i, count)},
            device_id_type=pl.DeviceIdType.MESH,
        )
    pl.semaphore_wait(barrier, count - 1)
    for i in range(1, count):
        there = lax.rem(me + i, count)
        remote(part.at[there], got.at[me], s1, r1, there).start()
    got[me] = part[me]
    others = got.at[pl.ds(0, count - 1)]
    pltpu.make_async_copy(others, others, r1).wait()
    total = got[0]
    for i in range(1, count):
        total = total + got[i]
    mine[...] = total
    for i in range(1, count):
        there = lax.rem(me + i, count)
        remote(mine, done.at[me], s2, r2, there).start()
    done[me] = total
    others = done.at[pl.ds(0, count - 1)]
    pltpu.make_async_copy(others, others, r2).wait()
    per_chunk = part.shape[1]
    blocks = out.shape[1] // LANES
    scale = 1.0 / (ensemble - 1.0)
    for u in range(count * per_chunk):
        r, c = u // blocks, u % blocks
        out[r * 8 : r * 8 + 8, c * LANES : (c + 1) * LANES] = (
            done[u // per_chunk, u % per_chunk] * scale
        )
    others = got.at[pl.ds(0, count - 1)]
    pltpu.make_async_copy(others, others, s1).wait()
    pltpu.make_async_copy(others, others, s2).wait()


def per_device(perturbations, control, band_rows, band_cols, edge_peer, edge_flip):
    T, count = lax.axis_size("tile"), lax.axis_size("member")
    M = perturbations.shape[0]
    N = control.shape[-1]
    units = FR * N // (8 * LANES)
    per_chunk = units // count
    vmem, smem = pl.BlockSpec(memory_space=pltpu.VMEM), pl.BlockSpec(memory_space=pltpu.SMEM)
    dma = pltpu.SemaphoreType.DMA
    part = pl.pallas_call(
        functools.partial(tile_kernel, T, M),
        out_shape=jax.ShapeDtypeStruct((count, per_chunk, 8, LANES), f32),
        in_specs=[vmem, vmem, vmem, vmem, smem, smem],
        out_specs=vmem,
        scratch_shapes=[
            pltpu.VMEM((3, M, FACES, ROWS, N), bf16),
            pltpu.VMEM((M, ROWS, COLW), bf16),
            pltpu.VMEM((M, T, ROWS, COLW), bf16),
            pltpu.VMEM((M, ROWS, COLW), bf16),
            pltpu.VMEM((M, ROWS, COLW), bf16),
            pltpu.VMEM((M, T, ROWS, LANES), bf16),
            pltpu.VMEM((2, 2, M, ROWS, LANES), bf16),
            pltpu.VMEM((M, ROWS, COLW), bf16),
            pltpu.VMEM((M, ROWS, COLW), bf16),
            pltpu.VMEM((M, T, ROWS, COLW), bf16),
            pltpu.VMEM((2, M, FACES, ROWS, N), bf16),
            pltpu.VMEM((3, M, FACES, ROWS, N), bf16),
            pltpu.VMEM((M, T, ROWS, LANES), bf16),
            pltpu.VMEM((2, 2, M, ROWS, LANES), bf16),
            pltpu.VMEM((N, N + LANES), bf16),
            pltpu.VMEM((M * FR, N + LANES), bf16),
            pltpu.VMEM((M * FR, N), f32),
            pltpu.VMEM((3, FR, FR), bf16),
            pltpu.VMEM((3, FR, FR), bf16),
            pltpu.VMEM((N, N), bf16),
            pltpu.VMEM((4, COLW, COLW), bf16),
            dma((4,)), dma((4,)),
            dma((4,)), dma((2,)),
            dma((2,)), dma((2,)),
            dma((2, 2)), dma((2, 2, 2)),
        ],
        compiler_params=pltpu.CompilerParams(
            collective_id=0, has_side_effects=True, vmem_limit_bytes=40 * 1024 * 1024
        ),
        name="filters",
    )(perturbations, control, band_rows, band_cols, edge_peer, edge_flip)
    whole = pl.pallas_call(
        functools.partial(member_kernel, count, count * M),
        out_shape=jax.ShapeDtypeStruct((FR, N), f32),
        in_specs=[vmem],
        out_specs=vmem,
        scratch_shapes=[
            pltpu.VMEM((count, per_chunk, 8, LANES), f32),
            pltpu.VMEM((per_chunk, 8, LANES), f32),
            pltpu.VMEM((count, per_chunk, 8, LANES), f32),
            dma, dma, dma, dma,
        ],
        compiler_params=pltpu.CompilerParams(
            collective_id=1, has_side_effects=True, vmem_limit_bytes=8 * 1024 * 1024
        ),
        name="member_sum",
    )(part)
    return whole.reshape(control.shape)


def solution(mesh):
    return jax.shard_map(
        per_device,
        mesh=mesh,
        in_specs=(
            P("member", None, "tile", None),
            P(None, "tile", None),
            P("tile", None),
            P(),
            P(),
            P(),
        ),
        out_specs=P(None, "tile", None),
        check_vma=False,
    )
```

```python
import functools
import math

import jax
import jax.numpy as jnp
import numpy as np
from jax import lax
from jax.experimental import pallas as pl
from jax.experimental.pallas import tpu as pltpu
from jax.sharding import PartitionSpec as P

HALF = 12
ROWS = 16
FACES = 6
LANES = 128
WIDE = 2 * LANES
f32, bf16, i32 = jnp.float32, jnp.bfloat16, jnp.int32


def iota(shape, dim):
    return lax.broadcasted_iota(i32, shape, dim)


def dot(a, b):
    return lax.dot_general(a, b, (((1,), (0,)), ((), ())), preferred_element_type=f32)


def dot_nt(a, b):
    return lax.dot_general(a, b, (((1,), (1,)), ((), ())), preferred_element_type=f32)


def dot_tn(a, b):
    return lax.dot_general(a, b, (((0,), (0,)), ((), ())), preferred_element_type=f32)


def onehot(mask):
    return jnp.where(mask, 1.0, 0.0).astype(bf16)


def taper(band):
    rows, taps = band.shape
    steps = np.arange(2 * HALF + 1, dtype=np.float32) - HALF
    curve = np.exp(-((steps / HALF) ** 2))
    scale = 1.0 / math.sqrt(math.sqrt(float(np.sum(curve * curve))) * float(np.sum(curve)))
    lane = iota((1, taps), 1).astype(f32)
    g = jnp.exp(-(((lane - HALF) / HALF) ** 2)) * scale
    wide = jnp.concatenate([band * g, jnp.zeros((rows, LANES - taps), f32)], axis=1)
    return wide.astype(bf16).astype(f32)


def make_key(member, code, layer, good, other):
    return jnp.where(good, ((member * 24 + code) << 4) + layer, other)


def col_parts(lane):
    face, rest = lane >> 5, lane & 31
    second = rest >= HALF
    layer = jnp.where(second, rest - HALF, rest)
    return face, jnp.where(second, 3, 2), layer, (rest < 2 * HALF) & (face < FACES)


def hub_parts(lane):
    face, layer = (lane & (LANES - 1)) >> 4, lane & 15
    return lane >> 7, face, layer, (face < FACES) & (layer < HALF)


def row_parts(index):
    both = index >> 4
    member = jnp.where(both >= FACES, 1, 0)
    return member, both - FACES * member, index & 15


def halo_parts(index):
    both = (index * 171) >> 11
    member = jnp.where(both >= FACES, 1, 0)
    return member, both - FACES * member, index - both * HALF


def pick_face(face, values):
    out = jnp.zeros(face.shape, i32)
    for f in range(FACES):
        out = jnp.where(face == f, values[f], out)
    return out


def whole_kernel(
    tiles, members, count,
    pert_in, control_in, rows_in, cols_in, peer_in, flip_in, out,
    pert, control, band_rows, band_cols, peer, flip,
    w, wh, halo_s, pa, pall_a, pb, pb_mir, qb, qr_b, pc, pc_mir, pa_c, pall_c, sp, drh, qd, qr_d,
    dmat, xs, zacc, bd, bdh, bdt, bdht, jn, gmat, part, got, mine, done,
    load, ring_s, ring_r, hub_s, hub_r, mir_s, mir_r, sc_s, sc_r, mem_s, mem_r,
):
    T, M = tiles, members
    N = ROWS * T
    NB = N // LANES
    MR, MH = M * FACES * ROWS, M * FACES * HALF
    t, me = lax.axis_index("tile"), lax.axis_index("member")
    prev, nxt, mirror = lax.rem(t + T - 1, T), lax.rem(t + 1, T), T - 1 - t
    hub = jnp.where(t == T - 1, 1, 0)
    is_hub = (t == 0) | (t == T - 1)
    last = hub == 1

    def remote(src, dst, send, recv, where, axis="tile"):
        return pltpu.make_async_remote_copy(
            src_ref=src, dst_ref=dst, send_sem=send, recv_sem=recv,
            device_id={axis: where}, device_id_type=pl.DeviceIdType.MESH,
        )

    def each_tile(act):
        act(lax.rem(t + T // 2, T))

        def body(d, carry):
            act(lax.rem(t + T // 2 + d, T))
            act(lax.rem(t + T // 2 - d, T))
            return carry

        lax.fori_loop(1, T // 2, body, 0)

    barrier = pltpu.get_barrier_semaphore()

    def greet(where, axis="tile"):
        pl.semaphore_signal(
            barrier, inc=1, device_id={axis: where}, device_id_type=pl.DeviceIdType.MESH
        )

    @pl.when(is_hub)
    def _():
        each_tile(greet)

    @pl.when(jnp.logical_not(is_hub))
    def _():
        greet(0)
        greet(T - 1)

    for where in (mirror, prev, nxt):
        greet(where)
    for i in range(1, count):
        greet(lax.rem(me + i, count), "member")

    loads = [
        pltpu.make_async_copy(src, dst, load.at[i])
        for i, (src, dst) in enumerate(
            (
                (pert_in, pert), (control_in, control), (peer_in, peer), (flip_in, flip),
                (rows_in, band_rows), (cols_in, band_cols),
            )
        )
    ]
    for copy in loads:
        copy.start()

    r256, c128 = iota((WIDE, LANES), 0), iota((WIDE, LANES), 1) & 31
    sel = onehot(
        ((r256 < HALF) & (c128 == r256))
        | ((r256 >= WIDE - HALF) & (c128 == HALF + WIDE - 1 - r256))
    )
    group = iota((ROWS, LANES), 1) >> 5
    s0, s1 = iota((MH, MR), 0), iota((MH, MR), 1)
    half_of_row = (s0 * 171) >> 11
    ahead = s1 - (half_of_row << 4) - (s0 - half_of_row * HALF)
    comp = [onehot(ahead == 0), onehot(ahead == ROWS - HALF)]

    def pack(quad):
        packs = []
        for m in range(M):
            blocks = []
            for g in range(2):
                block = jnp.zeros((ROWS, LANES), f32)
                for q in range(4):
                    f = 4 * g + q
                    if f < FACES:
                        at = (m * FACES + f) * ROWS
                        block = jnp.where(group == q, quad[at : at + ROWS], block)
                blocks.append(block)
            packs.append(jnp.concatenate(blocks, axis=1).astype(bf16))
        return packs

    def pack_ends(flat):
        ends = jnp.concatenate([flat[:, :LANES], flat[:, N - LANES :]], axis=1)
        return pack(dot(ends, sel))

    def spread(packs):
        parts = []
        for m in range(M):
            for f in range(FACES):
                g, q = f // 4, f % 4
                block = packs[m][:, g * LANES : (g + 1) * LANES]
                parts.append(jnp.where(group == q, block, 0.0))
        return jnp.concatenate(parts, axis=0).astype(bf16)

    for copy in loads[:4]:
        copy.wait()
    for m in range(M):
        weighted = (pert[m].astype(f32) * control[...]).astype(bf16)
        w[m * FACES * ROWS : (m + 1) * FACES * ROWS, :] = weighted.reshape(FACES * ROWS, N)

    peers = [[peer[e, f] for e in range(4)] for f in range(FACES)]
    flips = [[flip[e, f] for e in range(4)] for f in range(FACES)]
    src_face, src_edge, src_layer, src_good = col_parts(iota((WIDE, WIDE), 0))
    src_cols = make_key(0, 4 * src_face + src_edge, src_layer, src_good, -1)
    lane = iota((WIDE, WIDE), 1)
    _, hub_face, hub_layer, hub_good = hub_parts(lane)
    to_hub = jnp.where(
        lane < LANES,
        pick_face(hub_face, [peers[f][0] for f in range(FACES)]),
        pick_face(hub_face, [peers[f][1] for f in range(FACES)]),
    )
    hub_pick = onehot(src_cols == make_key(0, to_hub, hub_layer, hub_good, -2))

    def hub_messages(packs, dst):
        chosen = [dot(value, hub_pick).astype(bf16) for value in packs]
        for h in range(2):
            for m in range(M):
                dst[h, :, m * LANES : (m + 1) * LANES] = chosen[m][:, h * LANES : (h + 1) * LANES]

    hub_messages(pack_ends(w[...]), pa)
    halo_s[0] = dot(comp[0], w[...]).astype(bf16)
    halo_s[1] = dot(comp[1], w[...]).astype(bf16)

    @pl.when(is_hub)
    def _():
        pl.semaphore_wait(barrier, 3 + T - 1 + count - 1)

    @pl.when(jnp.logical_not(is_hub))
    def _():
        pl.semaphore_wait(barrier, 5 + count - 1)

    def hub_copies(src, dst, base):
        return [
            remote(src.at[h], dst.at[t], hub_s.at[base, h], hub_r.at[base], h * (T - 1))
            for h in range(2)
        ]

    def start_to_hubs(copies):
        for h in range(2):
            @pl.when(t != h * (T - 1))
            def _():
                copies[h].start()

    def finish_to_hubs(copies):
        for h in range(2):
            @pl.when(t != h * (T - 1))
            def _():
                copies[h].wait_send()

    def wait_at_hub(dst, base):
        others = dst.at[pl.ds(0, T - 1)]
        pltpu.make_async_copy(others, others, hub_r.at[base]).wait()

    to_hubs_a = hub_copies(pa, pall_a, 0)
    start_to_hubs(to_hubs_a)
    ring_a = [
        remote(halo_s.at[0], wh.at[1], ring_s.at[0], ring_r.at[0], prev),
        remote(halo_s.at[1], wh.at[0], ring_s.at[1], ring_r.at[1], nxt),
    ]
    for copy in ring_a:
        copy.start()

    for copy in loads[4:]:
        copy.wait()
    lane = iota((LANES, LANES), 1)
    blocks = {}
    for b in range(NB):
        wide = taper(jnp.transpose(band_cols[:, b * LANES : (b + 1) * LANES]))
        wide = jnp.concatenate([wide, jnp.zeros((LANES, LANES), f32)], axis=1)
        wide = pltpu.roll(wide, 0, 1, stride=1, stride_axis=0)
        wide = pltpu.roll(wide, WIDE - HALF, 1)
        over = wide[:, LANES:]
        for c, value in (
            (b, wide[:, :LANES]),
            ((b + 1) % (NB + 1), jnp.where(lane < HALF, over, 0.0)),
            ((b + NB) % (NB + 1), jnp.where(lane >= LANES - HALF, over, 0.0)),
        ):
            blocks[b, c] = blocks[b, c] + value if (b, c) in blocks else value
    from_lane, to_lane = iota((LANES, LANES), 0), iota((LANES, LANES), 1) & 31
    rim_order = onehot(
        ((to_lane < HALF) & (from_lane == LANES - 1 - to_lane))
        | ((to_lane >= HALF) & (to_lane < 2 * HALF) & (from_lane == to_lane - HALF))
    )
    for b in range(NB):
        for c in range(NB + 1):
            value = blocks.get((b, c))
            value = jnp.zeros((LANES, LANES), bf16) if value is None else value.astype(bf16)
            if c == NB:
                value = dot(value, rim_order).astype(bf16)
            dmat[b * LANES : (b + 1) * LANES, c * LANES : (c + 1) * LANES] = value

    base = jnp.concatenate([taper(band_rows[...]), jnp.zeros((ROWS, LANES), f32)], axis=1)
    skew = pltpu.roll(base, ROWS - HALF, 1, stride=1, stride_axis=0)
    skew = skew[:, :LANES].astype(bf16)
    every = jnp.concatenate([skew] * (M * FACES), axis=0)
    tap_at, dst_at = iota((LANES, WIDE), 0), iota((LANES, WIDE), 1)
    row_at, col_at = iota((MR, WIDE), 0) >> 4, iota((MR, WIDE), 1)
    half_at = (dst_at * 171) >> 11
    step_at = dst_at - half_at * HALF

    def banded(expand, same):
        full = jnp.where(same, dot(every, onehot(expand)), 0.0)
        square = jnp.concatenate([full, jnp.zeros((WIDE - MR, WIDE), f32)], axis=0)
        return full, jnp.transpose(square)

    full, turned = banded(tap_at == ROWS + (dst_at & 15), row_at == col_at >> 4)
    bd[...] = full[:, :MR].astype(bf16)
    bdt[...] = turned[:MR, :MR].astype(bf16)
    for side, first in ((0, ROWS - HALF), (1, 2 * ROWS)):
        full, turned = banded(
            (tap_at == first + step_at) & (dst_at < MH), row_at == (col_at * 171) >> 11
        )
        bdh[side] = full[:, :MH].astype(bf16)
        bdht[side] = turned[:MH, :MR].astype(bf16)

    want_face, want_edge, want_layer, want_good = col_parts(iota((WIDE, WIDE), 1))
    want_code = jnp.where(
        want_edge == 2,
        pick_face(want_face, [peers[f][2] for f in range(FACES)]),
        pick_face(want_face, [peers[f][3] for f in range(FACES)]),
    )
    want_turn = jnp.where(
        want_edge == 2,
        pick_face(want_face, [flips[f][2] for f in range(FACES)]),
        pick_face(want_face, [flips[f][3] for f in range(FACES)]),
    )
    want = make_key(0, want_code, want_layer, want_good, -2)
    src_hub, row_face, row_layer, row_good = hub_parts(iota((WIDE, WIDE), 0))
    src_rows = make_key(0, 4 * row_face + src_hub, row_layer, row_good, -1)
    gmat[0] = onehot((src_cols == want) & (want_turn == 0))
    gmat[1] = onehot(src_rows == want)
    gmat[2] = onehot((src_cols == want) & (want_turn == 1))
    back = onehot(iota((ROWS, ROWS), 0) + iota((ROWS, ROWS), 1) == ROWS - 1)

    hub_peers = [jnp.where(last, peers[f][1], peers[f][0]) for f in range(FACES)]
    hub_flips = [jnp.where(last, flips[f][1], flips[f][0]) for f in range(FACES)]

    @pl.when(is_hub)
    def _():
        jn[...] = onehot(iota((N, N), 0) + iota((N, N), 1) == N - 1)

    def flipped(value):
        return dot(value.astype(bf16), jn[...])

    def gather_rows(shape, parts, layer_of, cols, rows):
        def wanted(width):
            index = iota((2 * shape, width), 0)
            turned = index >= shape
            member, face, at = parts(jnp.where(turned, index - shape, index))
            layer = layer_of(at)
            good = (layer < HALF) & ((pick_face(face, hub_flips) == 1) == turned)
            return member, face, layer, good

        total = None
        if cols is not None:
            member, face, layer, good = wanted(WIDE)
            src_m, src_f, src_k, src_ok = hub_parts(iota((2 * shape, WIDE), 1))
            pick = onehot(
                make_key(member, face, layer, good, -2) == make_key(src_m, src_f, src_k, src_ok, -1)
            )
            total = dot_nt(pick, cols[...].reshape(N, WIDE))
        for source, source_parts, source_layer, source_edge in rows:
            member, face, layer, good = wanted(source.shape[0])
            code = pick_face(face, hub_peers)
            src_m, src_f, src_at = source_parts(iota((2 * shape, source.shape[0]), 1))
            src_k = source_layer(src_at)
            pick = onehot(
                make_key(member, code, layer, good, -2)
                == make_key(src_m, 4 * src_f + source_edge, src_k, src_k < HALF, -1)
            )
            value = dot(pick, source)
            total = value if total is None else total + value
        return total[:shape] + flipped(total[shape:])

    def scatter(flat, parts, layer_of, q, qr, base):
        shape = (flat.shape[0], WIDE)
        member, face, at = parts(iota(shape, 0))
        layer = layer_of(at)
        lane = iota(shape, 1)
        here = (layer < HALF) & (lane == member * LANES + (face << 4) + layer)
        turned = pick_face(face, hub_flips) == 1
        value = dot_tn(flat, onehot(here & jnp.logical_not(turned)))
        value = value + dot_tn(flipped(flat).astype(bf16), onehot(here & turned))
        q[...] = value.astype(bf16).reshape(T, ROWS, WIDE)

        def send(there):
            remote(q.at[there], qr.at[hub], sc_s.at[base], sc_r.at[base, hub], there).start()

        each_tile(send)
        qr[hub] = q[t]

    def finish_scatter(q, base):
        others = q.at[pl.ds(0, T - 1)]
        pltpu.make_async_copy(others, others, sc_s.at[base]).wait()

    def wait_scatter(q, qr, base):
        for h in range(2):
            @pl.when(t != h * (T - 1))
            def _():
                remote(
                    q.at[0], qr.at[h], sc_s.at[base], sc_r.at[base, h], h * (T - 1)
                ).wait_recv()

    def arrive_cols(direct, mirrored, qr):
        packs = []
        for m in range(M):
            value = jnp.zeros((ROWS, WIDE), f32)
            if direct is not None:
                value = value + dot(direct[m], gmat[0])
                value = value + dot(back, dot(mirrored[m], gmat[2]).astype(bf16))
            if qr is not None:
                near = [qr[h, :, m * LANES : (m + 1) * LANES] for h in range(2)]
                value = value + dot(jnp.concatenate(near, axis=1), gmat[1])
            packs.append(value)
        return packs

    def forward(at):
        return at

    def by_hub(first, second):
        return lambda at: jnp.where(last, second(at), first(at))

    def back_row(at):
        return ROWS - 1 - at

    def back_halo(at):
        return HALF - 1 - at

    x = dot(bd[...], w[...])
    for copy in ring_a:
        copy.wait_recv()

    @pl.when(is_hub)
    def _():
        pall_a[t] = pa[hub]
        wait_at_hub(pall_a, 0)
        halo = by_hub(back_halo, forward)
        wh[hub] = gather_rows(
            MH, halo_parts, halo, pall_a,
            (
                (w[...], row_parts, by_hub(forward, back_row), hub),
                (wh[hub], halo_parts, halo, 1 - hub),
            ),
        ).astype(bf16)

    x = x + dot(bdh[0], wh[0]) + dot(bdh[1], wh[1])
    xs[:, :N] = x.astype(bf16)

    @pl.when(is_hub)
    def _():
        scatter(xs[:, :N], row_parts, by_hub(forward, back_row), qb, qr_b, 0)

    for m, value in enumerate(pack_ends(xs[:, :N])):
        pb[m] = value
    mirror_b = remote(pb, pb_mir, mir_s.at[0], mir_r.at[0], mirror)
    mirror_b.start()
    mirror_b.wait_recv()
    wait_scatter(qb, qr_b, 0)
    xs[:, N:] = spread(arrive_cols(pb, pb_mir, qr_b))
    y = dot_nt(xs[...], dmat[...]).astype(bf16)

    rims = pack(dot(y, dmat[:, N:]))
    for m, value in enumerate(rims):
        pc[m] = value
    mirror_c = remote(pc, pc_mir, mir_s.at[1], mir_r.at[1], mirror)
    hub_messages(rims, pa_c)
    to_hubs_c = hub_copies(pa_c, pall_c, 1)
    start_to_hubs(to_hubs_c)
    mirror_c.start()
    zacc[...] = dot(y, dmat[:, :N])
    mirror_c.wait_recv()

    @pl.when(is_hub)
    def _():
        pall_c[t] = pa_c[hub]
        wait_at_hub(pall_c, 1)
        zacc[...] += gather_rows(MR, row_parts, by_hub(forward, back_row), pall_c, ())

    ends = dot_nt(spread(arrive_cols(pc, pc_mir, None)), sel)
    zacc[:, :LANES] += ends[:, :LANES]
    zacc[:, N - LANES :] += ends[:, LANES:]

    z = zacc[...].astype(bf16)
    sp[0] = dot(bdht[0], z).astype(bf16)
    sp[1] = dot(bdht[1], z).astype(bf16)
    ring_d = [
        remote(sp.at[0], drh.at[1], ring_s.at[2], ring_r.at[2], prev),
        remote(sp.at[1], drh.at[0], ring_s.at[3], ring_r.at[3], nxt),
    ]

    @pl.when(is_hub)
    def _():
        scatter(sp[hub], halo_parts, by_hub(back_halo, forward), qd, qr_d, 1)

    for copy in ring_d:
        copy.start()
    zacc[...] = dot(bdt[...], z)
    for copy in ring_d:
        copy.wait_recv()

    @pl.when(is_hub)
    def _():
        drh[hub] = gather_rows(
            MH, halo_parts, by_hub(forward, back_halo), None,
            (
                (sp[hub], halo_parts, by_hub(back_halo, forward), hub),
                (drh[hub], halo_parts, by_hub(forward, back_halo), 1 - hub),
            ),
        ).astype(bf16)

    zacc[...] += dot_tn(comp[0], drh[0]) + dot_tn(comp[1], drh[1])
    wait_scatter(qd, qr_d, 1)
    ends = dot_nt(spread(arrive_cols(None, None, qr_d)), sel)
    zacc[:, :LANES] += ends[:, :LANES]
    zacc[:, N - LANES :] += ends[:, LANES:]

    FR = FACES * ROWS
    total = jnp.zeros((FR, N), f32)
    for m in range(M):
        total = total + pert[m].astype(f32).reshape(FR, N) * zacc[m * FR : (m + 1) * FR, :]
    per_chunk = part.shape[1]
    for u in range(count * per_chunk):
        r, c = u // NB, u % NB
        part[u // per_chunk, u % per_chunk] = total[r * 8 : r * 8 + 8, c * LANES : (c + 1) * LANES]

    peers_of_me = [lax.rem(me + i, count) for i in range(1, count)]
    for there in peers_of_me:
        remote(part.at[there], got.at[me], mem_s.at[0], mem_r.at[0], there, "member").start()
    got[me] = part[me]
    others = got.at[pl.ds(0, count - 1)]
    pltpu.make_async_copy(others, others, mem_r.at[0]).wait()
    chunk = got[0]
    for i in range(1, count):
        chunk = chunk + got[i]
    mine[...] = chunk * (1.0 / (M * count - 1.0))
    for there in peers_of_me:
        remote(mine, done.at[me], mem_s.at[1], mem_r.at[1], there, "member").start()
    done[me] = mine[...]
    finished = done.at[pl.ds(0, count - 1)]
    pltpu.make_async_copy(finished, finished, mem_r.at[1]).wait()
    for u in range(count * per_chunk):
        r, c = u // NB, u % NB
        out[r * 8 : r * 8 + 8, c * LANES : (c + 1) * LANES] = done[u // per_chunk, u % per_chunk]

    for copy in ring_a + ring_d + [mirror_b, mirror_c]:
        copy.wait_send()
    finish_to_hubs(to_hubs_a)
    finish_to_hubs(to_hubs_c)

    @pl.when(is_hub)
    def _():
        finish_scatter(qb, 0)
        finish_scatter(qd, 1)

    for i in range(2):
        pltpu.make_async_copy(others, others, mem_s.at[i]).wait()


def per_device(perturbations, control, band_rows, band_cols, edge_peer, edge_flip):
    T, count = lax.axis_size("tile"), lax.axis_size("member")
    M = perturbations.shape[0]
    N = control.shape[-1]
    MR, MH = M * FACES * ROWS, M * FACES * HALF
    per_chunk = FACES * ROWS * N // (8 * LANES) // count
    vmem, hbm = pl.BlockSpec(memory_space=pltpu.VMEM), pl.BlockSpec(memory_space=pltpu.HBM)
    dma = pltpu.SemaphoreType.DMA
    args = (perturbations, control, band_rows, band_cols.T, edge_peer.T, edge_flip.T)
    result = pl.pallas_call(
        functools.partial(whole_kernel, T, M, count),
        out_shape=jax.ShapeDtypeStruct((FACES * ROWS, N), f32),
        in_specs=[hbm] * 6,
        out_specs=vmem,
        scratch_shapes=[
            pltpu.VMEM(args[0].shape, bf16),
            pltpu.VMEM(args[1].shape, f32),
            pltpu.VMEM(args[2].shape, f32),
            pltpu.VMEM(args[3].shape, f32),
            pltpu.SMEM(args[4].shape, i32),
            pltpu.SMEM(args[5].shape, i32),
            pltpu.VMEM((MR, N), bf16),
            pltpu.VMEM((2, MH, N), bf16),
            pltpu.VMEM((2, MH, N), bf16),
            pltpu.VMEM((2, ROWS, WIDE), bf16),
            pltpu.VMEM((T, ROWS, WIDE), bf16),
            pltpu.VMEM((M, ROWS, WIDE), bf16),
            pltpu.VMEM((M, ROWS, WIDE), bf16),
            pltpu.VMEM((T, ROWS, WIDE), bf16),
            pltpu.VMEM((2, ROWS, WIDE), bf16),
            pltpu.VMEM((M, ROWS, WIDE), bf16),
            pltpu.VMEM((M, ROWS, WIDE), bf16),
            pltpu.VMEM((2, ROWS, WIDE), bf16),
            pltpu.VMEM((T, ROWS, WIDE), bf16),
            pltpu.VMEM((2, MH, N), bf16),
            pltpu.VMEM((2, MH, N), bf16),
            pltpu.VMEM((T, ROWS, WIDE), bf16),
            pltpu.VMEM((2, ROWS, WIDE), bf16),
            pltpu.VMEM((N, N + LANES), bf16),
            pltpu.VMEM((MR, N + LANES), bf16),
            pltpu.VMEM((MR, N), f32),
            pltpu.VMEM((MR, MR), bf16),
            pltpu.VMEM((2, MR, MH), bf16),
            pltpu.VMEM((MR, MR), bf16),
            pltpu.VMEM((2, MH, MR), bf16),
            pltpu.VMEM((N, N), bf16),
            pltpu.VMEM((3, WIDE, WIDE), bf16),
            pltpu.VMEM((count, per_chunk, 8, LANES), f32),
            pltpu.VMEM((count, per_chunk, 8, LANES), f32),
            pltpu.VMEM((per_chunk, 8, LANES), f32),
            pltpu.VMEM((count, per_chunk, 8, LANES), f32),
            dma((6,)),
            dma((4,)), dma((4,)),
            dma((2, 2)), dma((2,)),
            dma((2,)), dma((2,)),
            dma((2,)), dma((2, 2)),
            dma((2,)), dma((2,)),
        ],
        compiler_params=pltpu.CompilerParams(
            collective_id=0, has_side_effects=True, vmem_limit_bytes=48 * 1024 * 1024
        ),
        name="covariance",
    )(*args)
    return result.reshape(control.shape)


def solution(mesh):
    return jax.shard_map(
        per_device,
        mesh=mesh,
        in_specs=(
            P("member", None, "tile", None),
            P(None, "tile", None),
            P("tile", None),
            P(),
            P(),
            P(),
        ),
        out_specs=P(None, "tile", None),
        check_vma=False,
    )
```

```python
import functools
import math

import jax
import jax.numpy as jnp
import numpy as np
from jax import lax
from jax.experimental import pallas as pl
from jax.experimental.pallas import tpu as pltpu
from jax.sharding import PartitionSpec as P

HALF = 12
ROWS = 16
FACES = 6
LANES = 128
WIDE = 2 * LANES
f32, bf16, i32 = jnp.float32, jnp.bfloat16, jnp.int32


def iota(shape, dim):
    return lax.broadcasted_iota(i32, shape, dim)


def dot(a, b):
    return lax.dot_general(a, b, (((1,), (0,)), ((), ())), preferred_element_type=f32)


def dot_nt(a, b):
    return lax.dot_general(a, b, (((1,), (1,)), ((), ())), preferred_element_type=f32)


def dot_tn(a, b):
    return lax.dot_general(a, b, (((0,), (0,)), ((), ())), preferred_element_type=f32)


def onehot(mask):
    return jnp.where(mask, 1.0, 0.0).astype(bf16)


def taper(band):
    rows, taps = band.shape
    steps = np.arange(2 * HALF + 1, dtype=np.float32) - HALF
    curve = np.exp(-((steps / HALF) ** 2))
    scale = 1.0 / math.sqrt(math.sqrt(float(np.sum(curve * curve))) * float(np.sum(curve)))
    lane = iota((1, taps), 1).astype(f32)
    g = jnp.exp(-(((lane - HALF) / HALF) ** 2)) * scale
    wide = jnp.concatenate([band * g, jnp.zeros((rows, LANES - taps), f32)], axis=1)
    return wide.astype(bf16).astype(f32)


def make_key(member, code, layer, good, other):
    return jnp.where(good, ((member * 24 + code) << 4) + layer, other)


def col_parts(lane):
    face, rest = lane >> 5, lane & 31
    second = rest >= HALF
    layer = jnp.where(second, rest - HALF, rest)
    return face, jnp.where(second, 3, 2), layer, (rest < 2 * HALF) & (face < FACES)


def hub_parts(lane):
    face, layer = (lane & (LANES - 1)) >> 4, lane & 15
    return lane >> 7, face, layer, (face < FACES) & (layer < HALF)


def row_parts(index):
    both = index >> 4
    member = jnp.where(both >= FACES, 1, 0)
    return member, both - FACES * member, index & 15


def halo_parts(index):
    both = (index * 171) >> 11
    member = jnp.where(both >= FACES, 1, 0)
    return member, both - FACES * member, index - both * HALF


def pick_face(face, values):
    out = jnp.zeros(face.shape, i32)
    for f in range(FACES):
        out = jnp.where(face == f, values[f], out)
    return out


def whole_kernel(
    tiles, members, count,
    pert_in, control_in, rows_in, cols_in, peer_in, flip_in, out,
    pert, control, band_rows, band_cols, peer, flip,
    w, wh, halo_s, pa, pall_a, pw, pw_mir, qw, qr_w, qs, qr_s, pb, pb_mir, qr_b,
    pc, pc_mir, pa_c, pall_c, qc, qr_c, sp, drh, qd, qr_d,
    dmat, xs, zacc, bd, bdh, bdt, bdht, jn, gmat, seam, part, got, mine, done,
    load, ring_s, ring_r, hub_s, hub_r, mir_s, mir_r, strip_s, strip_r, sc_s, sc_r, mem_s, mem_r,
):
    T, M = tiles, members
    N = ROWS * T
    NB = N // LANES
    MR, MH = M * FACES * ROWS, M * FACES * HALF
    t, me = lax.axis_index("tile"), lax.axis_index("member")
    prev, nxt, mirror = lax.rem(t + T - 1, T), lax.rem(t + 1, T), T - 1 - t
    hub = jnp.where(t >= T // 2, 1, 0)
    is_hub = (t == 0) | (t == T - 1)
    is_second = (t == 1) | (t == T - 2)
    inner = jnp.logical_not(is_hub)
    last = hub == 1

    def remote(src, dst, send, recv, where, axis="tile"):
        return pltpu.make_async_remote_copy(
            src_ref=src, dst_ref=dst, send_sem=send, recv_sem=recv,
            device_id={axis: where}, device_id_type=pl.DeviceIdType.MESH,
        )

    def each_tile(act):
        act(lax.rem(t + T // 2, T))

        def body(d, carry):
            act(lax.rem(t + T // 2 + d, T))
            act(lax.rem(t + T // 2 - d, T))
            return carry

        lax.fori_loop(1, T // 2, body, 0)

    barrier = pltpu.get_barrier_semaphore()

    def greet(where, axis="tile"):
        pl.semaphore_signal(
            barrier, inc=1, device_id={axis: where}, device_id_type=pl.DeviceIdType.MESH
        )

    @pl.when(is_hub)
    def _():
        each_tile(greet)

    @pl.when(jnp.logical_not(is_hub))
    def _():
        greet(0)
        greet(T - 1)

    for where in (mirror, prev, nxt):
        greet(where)
    for second in (1, T - 2):
        @pl.when(t != second)
        def _():
            greet(second)

    beside = []
    for step in (-1, 1):
        there = mirror + step
        beside.append((jnp.clip(there, 0, T - 1), there != t, (there >= 1) & (there <= T - 2)))

        @pl.when(inner & (there != t))
        def _():
            greet(there)
    for i in range(1, count):
        greet(lax.rem(me + i, count), "member")

    loads = [
        pltpu.make_async_copy(src, dst, load.at[i])
        for i, (src, dst) in enumerate(
            (
                (pert_in, pert), (control_in, control), (peer_in, peer), (flip_in, flip),
                (rows_in, band_rows), (cols_in, band_cols),
            )
        )
    ]
    for copy in loads:
        copy.start()

    r256, c128 = iota((WIDE, LANES), 0), iota((WIDE, LANES), 1) & 31
    sel = onehot(
        ((r256 < HALF) & (c128 == r256))
        | ((r256 >= WIDE - HALF) & (c128 == HALF + WIDE - 1 - r256))
    )
    group = iota((ROWS, LANES), 1) >> 5
    s0, s1 = iota((MH, MR), 0), iota((MH, MR), 1)
    half_of_row = (s0 * 171) >> 11
    ahead = s1 - (half_of_row << 4) - (s0 - half_of_row * HALF)
    comp = [onehot(ahead == 0), onehot(ahead == ROWS - HALF)]

    def pack(quad):
        packs = []
        for m in range(M):
            blocks = []
            for g in range(2):
                block = jnp.zeros((ROWS, LANES), f32)
                for q in range(4):
                    f = 4 * g + q
                    if f < FACES:
                        at = (m * FACES + f) * ROWS
                        block = jnp.where(group == q, quad[at : at + ROWS], block)
                blocks.append(block)
            packs.append(jnp.concatenate(blocks, axis=1).astype(bf16))
        return packs

    def pack_ends(flat):
        ends = jnp.concatenate([flat[:, :LANES], flat[:, N - LANES :]], axis=1)
        return pack(dot(ends, sel))

    def spread(packs):
        parts = []
        for m in range(M):
            for f in range(FACES):
                g, q = f // 4, f % 4
                block = packs[m][:, g * LANES : (g + 1) * LANES]
                parts.append(jnp.where(group == q, block, 0.0))
        return jnp.concatenate(parts, axis=0).astype(bf16)

    for copy in loads[:5]:
        copy.wait()
    for m in range(M):
        weighted = (pert[m].astype(f32) * control[...]).astype(bf16)
        w[m * FACES * ROWS : (m + 1) * FACES * ROWS, :] = weighted.reshape(FACES * ROWS, N)

    peers = [[peer[e, f] for e in range(4)] for f in range(FACES)]
    flips = [[flip[e, f] for e in range(4)] for f in range(FACES)]
    src_face, src_edge, src_layer, src_good = col_parts(iota((WIDE, WIDE), 0))
    src_cols = make_key(0, 4 * src_face + src_edge, src_layer, src_good, -1)
    lane = iota((WIDE, WIDE), 1)
    _, hub_face, hub_layer, hub_good = hub_parts(lane)
    to_hub = jnp.where(
        lane < LANES,
        pick_face(hub_face, [peers[f][0] for f in range(FACES)]),
        pick_face(hub_face, [peers[f][1] for f in range(FACES)]),
    )
    hub_pick = onehot(src_cols == make_key(0, to_hub, hub_layer, hub_good, -2))

    def hub_messages(packs, dst):
        chosen = [dot(value, hub_pick).astype(bf16) for value in packs]
        for h in range(2):
            for m in range(M):
                dst[h, :, m * LANES : (m + 1) * LANES] = chosen[m][:, h * LANES : (h + 1) * LANES]

    own_taps = taper(band_rows[...])
    strips = pack_ends(w[...])
    hub_messages(strips, pa)
    for m, value in enumerate(strips):
        pw[m] = value
    pw[0, :, LANES:] += pltpu.roll(own_taps, LANES // 2, 1).astype(bf16)
    halo_s[0] = dot(comp[0], w[...]).astype(bf16)
    halo_s[1] = dot(comp[1], w[...]).astype(bf16)

    hub_peers = [jnp.where(last, peers[f][1], peers[f][0]) for f in range(FACES)]
    hub_flips = [jnp.where(last, flips[f][1], flips[f][0]) for f in range(FACES)]

    def flipped(value):
        return dot(value.astype(bf16), jn[...])

    def by_hub(first, second):
        return lambda at: jnp.where(last, second(at), first(at))

    def forward(at):
        return at

    def back_row(at):
        return ROWS - 1 - at

    def back_halo(at):
        return HALF - 1 - at

    def turn_rows(flat, lanes_of):
        shape = (flat.shape[0], WIDE)
        member, face, at = row_parts(iota(shape, 0))
        here = lanes_of(member, face, by_hub(forward, back_row)(at)) == iota(shape, 1)
        turned = pick_face(face, hub_flips) == 1
        value = dot_tn(flat, onehot(here & jnp.logical_not(turned)))
        return value + dot_tn(flipped(flat).astype(bf16), onehot(here & turned))

    @pl.when(is_hub | is_second)
    def _():
        jn[...] = onehot(iota((N, N), 0) + iota((N, N), 1) == N - 1)

    @pl.when(is_hub)
    def _():
        value = turn_rows(w[...], lambda member, face, at: 96 * member + 16 * face + at)
        low, high = value[:, :LANES].astype(bf16), value[:, LANES:].astype(bf16)
        extra = pltpu.roll(own_taps, LANES // 2, 1).astype(bf16)
        qw[:, :, :LANES] = low.reshape(T, ROWS, LANES)
        qw[:, :, LANES:] = high.reshape(T, ROWS, LANES) + extra[None]

    @pl.when(is_second)
    def _():
        value = turn_rows(
            w[...],
            lambda member, face, at: jnp.where(at < 8, 48 * member + 8 * face + at, -1),
        )
        qs[...] = value[:, :LANES].astype(bf16).reshape(T, ROWS, LANES)

    greeted = 3 + count - 1 + jnp.where(is_hub, T - 1, 2) + jnp.where(is_second, T - 1, 0)
    for _, other, inside in beside:
        greeted = greeted + jnp.where(other & inside, 1, 0)
    pl.semaphore_wait(barrier, greeted)

    def hub_copies(src, dst, base):
        return [
            remote(src.at[h], dst.at[t], hub_s.at[base, h], hub_r.at[base], h * (T - 1))
            for h in range(2)
        ]

    def start_to_hubs(copies):
        for h in range(2):
            @pl.when(t != h * (T - 1))
            def _():
                copies[h].start()

    def finish_to_hubs(copies):
        for h in range(2):
            @pl.when(t != h * (T - 1))
            def _():
                copies[h].wait_send()

    def wait_at_hub(dst, base):
        others = dst.at[pl.ds(0, T - 1)]
        pltpu.make_async_copy(others, others, hub_r.at[base]).wait()

    def send_all(q, qr, base):
        def send(there):
            remote(q.at[there], qr.at[hub], sc_s.at[base], sc_r.at[base, hub], there).start()

        each_tile(send)
        qr[hub] = q[t]

    def wait_all(q, qr, base, places):
        for h, place in enumerate(places):
            @pl.when(t != place)
            def _():
                remote(q.at[0], qr.at[h], sc_s.at[base], sc_r.at[base, h], place).wait_recv()

    to_hubs_a = hub_copies(pa, pall_a, 0)
    start_to_hubs(to_hubs_a)

    @pl.when(is_hub)
    def _():
        send_all(qw, qr_w, 0)

    @pl.when(is_second)
    def _():
        send_all(qs, qr_s, 1)

    strip_copies = []
    middle = (mirror, t >= 0, inner)
    for i, (there, other, inside) in enumerate((beside[0], middle, beside[1])):
        strip_copies.append(remote(pw, pw_mir.at[i], strip_s.at[i], strip_r.at[i], there))

        @pl.when(other & inside)
        def _():
            strip_copies[i].start()

    ring_a = [
        remote(halo_s.at[0], wh.at[1], ring_s.at[0], ring_r.at[0], prev),
        remote(halo_s.at[1], wh.at[0], ring_s.at[1], ring_r.at[1], nxt),
    ]
    for copy in ring_a:
        copy.start()

    for copy in loads[5:]:
        copy.wait()
    lane = iota((LANES, LANES), 1)
    blocks = {}
    for b in range(NB):
        wide = taper(jnp.transpose(band_cols[:, b * LANES : (b + 1) * LANES]))
        wide = jnp.concatenate([wide, jnp.zeros((LANES, LANES), f32)], axis=1)
        wide = pltpu.roll(wide, 0, 1, stride=1, stride_axis=0)
        wide = pltpu.roll(wide, WIDE - HALF, 1)
        over = wide[:, LANES:]
        for c, value in (
            (b, wide[:, :LANES]),
            ((b + 1) % (NB + 1), jnp.where(lane < HALF, over, 0.0)),
            ((b + NB) % (NB + 1), jnp.where(lane >= LANES - HALF, over, 0.0)),
        ):
            blocks[b, c] = blocks[b, c] + value if (b, c) in blocks else value
    from_lane, to_lane = iota((LANES, LANES), 0), iota((LANES, LANES), 1) & 31
    rim_order = onehot(
        ((to_lane < HALF) & (from_lane == LANES - 1 - to_lane))
        | ((to_lane >= HALF) & (to_lane < 2 * HALF) & (from_lane == to_lane - HALF))
    )
    for b in range(NB):
        for c in range(NB + 1):
            value = blocks.get((b, c))
            value = jnp.zeros((LANES, LANES), bf16) if value is None else value.astype(bf16)
            if c == NB:
                value = dot(value, rim_order).astype(bf16)
            dmat[b * LANES : (b + 1) * LANES, c * LANES : (c + 1) * LANES] = value

    def skewed(taps, first):
        wide = jnp.concatenate([taps, jnp.zeros((ROWS, LANES), f32)], axis=1)
        wide = pltpu.roll(wide, first, 1, stride=1, stride_axis=0)
        return wide[:, :LANES].astype(bf16)

    skew = skewed(own_taps, ROWS - HALF)
    every = jnp.concatenate([skew] * (M * FACES), axis=0)
    tap_at, dst_at = iota((LANES, WIDE), 0), iota((LANES, WIDE), 1)
    row_at, col_at = iota((MR, WIDE), 0) >> 4, iota((MR, WIDE), 1)
    half_at = (dst_at * 171) >> 11
    step_at = dst_at - half_at * HALF

    def banded(expand, same):
        full = jnp.where(same, dot(every, onehot(expand)), 0.0)
        square = jnp.concatenate([full, jnp.zeros((WIDE - MR, WIDE), f32)], axis=0)
        return full, jnp.transpose(square)

    full, turned = banded(tap_at == ROWS + (dst_at & 15), row_at == col_at >> 4)
    bd[...] = full[:, :MR].astype(bf16)
    bdt[...] = turned[:MR, :MR].astype(bf16)
    for side, first in ((0, ROWS - HALF), (1, 2 * ROWS)):
        full, turned = banded(
            (tap_at == first + step_at) & (dst_at < MH), row_at == (col_at * 171) >> 11
        )
        bdh[side] = full[:, :MH].astype(bf16)
        bdht[side] = turned[:MH, :MR].astype(bf16)

    want_face, want_edge, want_layer, want_good = col_parts(iota((WIDE, WIDE), 1))
    want_code = jnp.where(
        want_edge == 2,
        pick_face(want_face, [peers[f][2] for f in range(FACES)]),
        pick_face(want_face, [peers[f][3] for f in range(FACES)]),
    )
    want_turn = jnp.where(
        want_edge == 2,
        pick_face(want_face, [flips[f][2] for f in range(FACES)]),
        pick_face(want_face, [flips[f][3] for f in range(FACES)]),
    )
    want = make_key(0, want_code, want_layer, want_good, -2)
    src_hub, row_face, row_layer, row_good = hub_parts(iota((WIDE, WIDE), 0))
    src_rows = make_key(0, 4 * row_face + src_hub, row_layer, row_good, -1)
    gmat[0] = onehot((src_cols == want) & (want_turn == 0))
    gmat[1] = onehot(src_rows == want)
    gmat[2] = onehot((src_cols == want) & (want_turn == 1))
    back = onehot(iota((ROWS, ROWS), 0) + iota((ROWS, ROWS), 1) == ROWS - 1)

    def gather_rows(shape, parts, layer_of, cols, rows):
        def wanted(width):
            index = iota((2 * shape, width), 0)
            turned = index >= shape
            member, face, at = parts(jnp.where(turned, index - shape, index))
            layer = layer_of(at)
            good = (layer < HALF) & ((pick_face(face, hub_flips) == 1) == turned)
            return member, face, layer, good

        total = None
        if cols is not None:
            member, face, layer, good = wanted(WIDE)
            src_m, src_f, src_k, src_ok = hub_parts(iota((2 * shape, WIDE), 1))
            pick = onehot(
                make_key(member, face, layer, good, -2) == make_key(src_m, src_f, src_k, src_ok, -1)
            )
            total = dot_nt(pick, cols[...].reshape(N, WIDE))
        for source, source_parts, source_layer, source_edge in rows:
            member, face, layer, good = wanted(source.shape[0])
            code = pick_face(face, hub_peers)
            src_m, src_f, src_at = source_parts(iota((2 * shape, source.shape[0]), 1))
            src_k = source_layer(src_at)
            pick = onehot(
                make_key(member, code, layer, good, -2)
                == make_key(src_m, 4 * src_f + source_edge, src_k, src_k < HALF, -1)
            )
            value = dot(pick, source)
            total = value if total is None else total + value
        return total[:shape] + flipped(total[shape:])

    def finish_scatter(q, base):
        others = q.at[pl.ds(0, T - 1)]
        pltpu.make_async_copy(others, others, sc_s.at[base]).wait()

    def arrive_cols(direct, mirrored, qr):
        packs = []
        for m in range(M):
            value = jnp.zeros((ROWS, WIDE), f32)
            if direct is not None:
                value = value + dot(direct[m], gmat[0])
                value = value + dot(back, dot(mirrored[m], gmat[2]).astype(bf16))
            if qr is not None:
                near = [qr[h, :, m * LANES : (m + 1) * LANES] for h in range(2)]
                value = value + dot(jnp.concatenate(near, axis=1), gmat[1])
            packs.append(value)
        return packs

    x = dot(bd[...], w[...])
    for copy in ring_a:
        copy.wait_recv()

    @pl.when(is_hub)
    def _():
        pall_a[t] = pa[hub]
        wait_at_hub(pall_a, 0)
        halo = by_hub(back_halo, forward)
        wh[hub] = gather_rows(
            MH, halo_parts, halo, pall_a,
            (
                (w[...], row_parts, by_hub(forward, back_row), hub),
                (wh[hub], halo_parts, halo, 1 - hub),
            ),
        ).astype(bf16)

    x = x + dot(bdh[0], wh[0]) + dot(bdh[1], wh[1])
    xs[:, :N] = x.astype(bf16)

    for m, value in enumerate(pack_ends(xs[:, :N])):
        pb[m] = value
    mirror_b = remote(pb, pb_mir, mir_s.at[0], mir_r.at[0], mirror)

    @pl.when(is_hub)
    def _():
        mirror_b.start()

    wait_all(qw, qr_w, 0, (0, T - 1))
    wait_all(qs, qr_s, 1, (1, T - 2))

    def sent_taps(block):
        taps = pltpu.roll(block.astype(f32), LANES // 2, 1)
        return jnp.where(iota((ROWS, LANES), 1) <= 2 * HALF, taps, 0.0)

    edge_shape = (WIDE + LANES + WIDE, WIDE)
    index = iota(edge_shape, 0)
    part_w, part_s = index < WIDE, index < WIDE + LANES
    low = jnp.where(part_w, index, index - WIDE)
    arr_m, arr_f, arr_k, arr_ok = hub_parts(index - WIDE - LANES)
    half_w, half_s = jnp.where(low >= 96, 1, 0), jnp.where(low >= 48, 1, 0)
    rest_w, rest_s = low - 96 * half_w, low - 48 * half_s
    src_mf = jnp.where(
        part_w,
        jnp.where(low < 192, FACES * half_w + (rest_w >> 4), -1),
        jnp.where(
            part_s,
            jnp.where(low < 96, FACES * half_s + (rest_s >> 3), -1),
            jnp.where(arr_ok, FACES * arr_m + arr_f, -1),
        ),
    )
    place = jnp.where(
        part_w,
        HALF + (rest_w & 15),
        jnp.where(part_s, HALF + ROWS + (rest_s & 7), HALF - 1 - arr_k),
    )
    dst_m, dst_f, dst_k, dst_ok = hub_parts(iota(edge_shape, 1))
    same = src_mf == jnp.where(dst_ok, FACES * dst_m + dst_f, -2)
    from_place = onehot(place[:, :LANES] == iota((edge_shape[0], LANES), 1))
    layer_lane = iota((ROWS, WIDE), 1) & 15
    to_layer = onehot((iota((ROWS, WIDE), 0) == layer_lane) & (layer_lane < HALF))
    turn_taps = onehot(
        (iota((LANES, LANES), 0) + iota((LANES, LANES), 1) == 2 * HALF)
    )
    for h in range(2):
        taps = sent_taps(qr_w[h, :, LANES:])
        if h == 1:
            taps = dot(dot(back, taps.astype(bf16)).astype(bf16), turn_taps)
        by_layer = dot_nt(from_place, skewed(taps, 0)).astype(bf16)
        seam[h] = jnp.where(same, dot(by_layer, to_layer), 0.0).astype(bf16)
        line = jnp.concatenate([qr_w[h], qr_s[h], pa[h]], axis=1)
        qr_b[h] = dot(line, seam[h]).astype(bf16)

    @pl.when(inner)
    def _():
        for i, (there, other, inside) in enumerate((beside[0], middle, beside[1])):
            @pl.when(other)
            def _():
                strip_copies[i].wait_recv()

            if i != 1:
                @pl.when(jnp.logical_not(other))
                def _():
                    pw_mir[i] = pw[...]

        mirror_skew = skewed(sent_taps(pw_mir[1, 0, :, LANES:]), ROWS - HALF)
        for m in range(M):
            rows = jnp.concatenate([pw_mir[0, m], pw_mir[1, m], pw_mir[2, m]], axis=0)
            pb_mir[m] = dot(mirror_skew[:, : 3 * ROWS], rows).astype(bf16)

    @pl.when(is_hub)
    def _():
        mirror_b.wait_recv()

    xs[:, N:] = spread(arrive_cols(pb, pb_mir, qr_b))
    y = dot_nt(xs[...], dmat[...]).astype(bf16)

    rims = pack(dot(y, dmat[:, N:]))
    for m, value in enumerate(rims):
        pc[m] = value
    mirror_c = remote(pc, pc_mir, mir_s.at[1], mir_r.at[1], mirror)
    hub_messages(rims, pa_c)
    to_hubs_c = hub_copies(pa_c, pall_c, 1)
    start_to_hubs(to_hubs_c)
    mirror_c.start()
    zacc[...] = dot(y, dmat[:, :N])

    @pl.when(is_hub)
    def _():
        value = turn_rows(
            zacc[...].astype(bf16),
            lambda member, face, at: jnp.where(
                at < HALF, LANES * member + 16 * face + at, -1
            ),
        )
        qc[...] = value.astype(bf16).reshape(T, ROWS, WIDE)
        send_all(qc, qr_c, 2)

    mirror_c.wait_recv()

    @pl.when(is_hub)
    def _():
        pall_c[t] = pa_c[hub]
        wait_at_hub(pall_c, 1)
        zacc[...] += gather_rows(MR, row_parts, by_hub(forward, back_row), pall_c, ())

    ends = dot_nt(spread(arrive_cols(pc, pc_mir, None)), sel)
    zacc[:, :LANES] += ends[:, :LANES]
    zacc[:, N - LANES :] += ends[:, LANES:]

    z = zacc[...].astype(bf16)
    sp[0] = dot(bdht[0], z).astype(bf16)
    sp[1] = dot(bdht[1], z).astype(bf16)
    ring_d = [
        remote(sp.at[0], drh.at[1], ring_s.at[2], ring_r.at[2], prev),
        remote(sp.at[1], drh.at[0], ring_s.at[3], ring_r.at[3], nxt),
    ]

    for copy in ring_d:
        copy.start()

    wait_all(qc, qr_c, 2, (0, T - 1))
    hub_d = remote(qd.at[1 - hub], qr_d.at[hub], sc_s.at[3], sc_r.at[3, hub], mirror)

    @pl.when(is_hub)
    def _():
        at, end = iota((WIDE, 2 * ROWS), 0), iota((WIDE, 2 * ROWS), 1)
        ends = onehot(at == jnp.where(end < ROWS, end, end + WIDE - 2 * ROWS))
        rim = sp[hub]
        near = dot(jnp.concatenate([rim[:, :LANES], rim[:, N - LANES :]], axis=1), ends)
        near = near.astype(bf16)
        mirrored = onehot(iota((2 * ROWS, 2 * ROWS), 0) + iota((2 * ROWS, 2 * ROWS), 1) == 2 * ROWS - 1)
        shape = (MH, WIDE)
        member, face, step = halo_parts(iota(shape, 0))
        layer = by_hub(back_halo, forward)(step)
        here = iota(shape, 1) == member * LANES + (face << 4) + layer
        turned = pick_face(face, hub_flips) == 1
        value = dot_tn(near, onehot(here & jnp.logical_not(turned)))
        value = value + dot_tn(dot(near, mirrored).astype(bf16), onehot(here & turned))
        qd[...] = value.astype(bf16).reshape(2, ROWS, WIDE)
        qr_d[hub] = qd[hub]
        hub_d.start()

    @pl.when(inner)
    def _():
        for h in range(2):
            strip = (qr_c[h].astype(f32) + pa_c[h].astype(f32)).astype(bf16)
            qr_d[h] = dot_nt(strip, seam[h, WIDE + LANES :, :]).astype(bf16)

    zacc[...] = dot(bdt[...], z)
    for copy in ring_d:
        copy.wait_recv()

    @pl.when(is_hub)
    def _():
        drh[hub] = gather_rows(
            MH, halo_parts, by_hub(forward, back_halo), None,
            (
                (sp[hub], halo_parts, by_hub(back_halo, forward), hub),
                (drh[hub], halo_parts, by_hub(forward, back_halo), 1 - hub),
            ),
        ).astype(bf16)

    zacc[...] += dot_tn(comp[0], drh[0]) + dot_tn(comp[1], drh[1])
    @pl.when(is_hub)
    def _():
        remote(qd.at[0], qr_d.at[1 - hub], sc_s.at[3], sc_r.at[3, 1 - hub], mirror).wait_recv()

    ends = dot_nt(spread(arrive_cols(None, None, qr_d)), sel)
    zacc[:, :LANES] += ends[:, :LANES]
    zacc[:, N - LANES :] += ends[:, LANES:]

    FR = FACES * ROWS
    total = jnp.zeros((FR, N), f32)
    for m in range(M):
        total = total + pert[m].astype(f32).reshape(FR, N) * zacc[m * FR : (m + 1) * FR, :]
    per_chunk = part.shape[1]
    for u in range(count * per_chunk):
        r, c = u // NB, u % NB
        part[u // per_chunk, u % per_chunk] = total[r * 8 : r * 8 + 8, c * LANES : (c + 1) * LANES]

    peers_of_me = [lax.rem(me + i, count) for i in range(1, count)]
    for there in peers_of_me:
        remote(part.at[there], got.at[me], mem_s.at[0], mem_r.at[0], there, "member").start()
    got[me] = part[me]
    others = got.at[pl.ds(0, count - 1)]
    pltpu.make_async_copy(others, others, mem_r.at[0]).wait()
    chunk = got[0]
    for i in range(1, count):
        chunk = chunk + got[i]
    mine[...] = chunk * (1.0 / (M * count - 1.0))
    for there in peers_of_me:
        remote(mine, done.at[me], mem_s.at[1], mem_r.at[1], there, "member").start()
    done[me] = mine[...]
    finished = done.at[pl.ds(0, count - 1)]
    pltpu.make_async_copy(finished, finished, mem_r.at[1]).wait()
    for u in range(count * per_chunk):
        r, c = u // NB, u % NB
        out[r * 8 : r * 8 + 8, c * LANES : (c + 1) * LANES] = done[u // per_chunk, u % per_chunk]

    for copy in ring_a + ring_d + [mirror_c]:
        copy.wait_send()
    for i, (there, other, inside) in enumerate((beside[0], middle, beside[1])):
        @pl.when(other & inside)
        def _():
            strip_copies[i].wait_send()

    finish_to_hubs(to_hubs_a)
    finish_to_hubs(to_hubs_c)

    @pl.when(is_hub)
    def _():
        finish_scatter(qw, 0)
        finish_scatter(qc, 2)
        mirror_b.wait_send()
        hub_d.wait_send()

    @pl.when(is_second)
    def _():
        finish_scatter(qs, 1)

    for i in range(2):
        pltpu.make_async_copy(others, others, mem_s.at[i]).wait()


def per_device(perturbations, control, band_rows, band_cols, edge_peer, edge_flip):
    T, count = lax.axis_size("tile"), lax.axis_size("member")
    M = perturbations.shape[0]
    N = control.shape[-1]
    MR, MH = M * FACES * ROWS, M * FACES * HALF
    per_chunk = FACES * ROWS * N // (8 * LANES) // count
    vmem, hbm = pl.BlockSpec(memory_space=pltpu.VMEM), pl.BlockSpec(memory_space=pltpu.HBM)
    dma = pltpu.SemaphoreType.DMA
    args = (perturbations, control, band_rows, band_cols.T, edge_peer.T, edge_flip.T)
    result = pl.pallas_call(
        functools.partial(whole_kernel, T, M, count),
        out_shape=jax.ShapeDtypeStruct((FACES * ROWS, N), f32),
        in_specs=[hbm] * 6,
        out_specs=vmem,
        scratch_shapes=[
            pltpu.VMEM(args[0].shape, bf16),
            pltpu.VMEM(args[1].shape, f32),
            pltpu.VMEM(args[2].shape, f32),
            pltpu.VMEM(args[3].shape, f32),
            pltpu.SMEM(args[4].shape, i32),
            pltpu.SMEM(args[5].shape, i32),
            pltpu.VMEM((MR, N), bf16),
            pltpu.VMEM((2, MH, N), bf16),
            pltpu.VMEM((2, MH, N), bf16),
            pltpu.VMEM((2, ROWS, WIDE), bf16),
            pltpu.VMEM((T, ROWS, WIDE), bf16),
            pltpu.VMEM((M, ROWS, WIDE), bf16),
            pltpu.VMEM((3, M, ROWS, WIDE), bf16),
            pltpu.VMEM((T, ROWS, WIDE), bf16),
            pltpu.VMEM((2, ROWS, WIDE), bf16),
            pltpu.VMEM((T, ROWS, LANES), bf16),
            pltpu.VMEM((2, ROWS, LANES), bf16),
            pltpu.VMEM((M, ROWS, WIDE), bf16),
            pltpu.VMEM((M, ROWS, WIDE), bf16),
            pltpu.VMEM((2, ROWS, WIDE), bf16),
            pltpu.VMEM((M, ROWS, WIDE), bf16),
            pltpu.VMEM((M, ROWS, WIDE), bf16),
            pltpu.VMEM((2, ROWS, WIDE), bf16),
            pltpu.VMEM((T, ROWS, WIDE), bf16),
            pltpu.VMEM((T, ROWS, WIDE), bf16),
            pltpu.VMEM((2, ROWS, WIDE), bf16),
            pltpu.VMEM((2, MH, N), bf16),
            pltpu.VMEM((2, MH, N), bf16),
            pltpu.VMEM((2, ROWS, WIDE), bf16),
            pltpu.VMEM((2, ROWS, WIDE), bf16),
            pltpu.VMEM((N, N + LANES), bf16),
            pltpu.VMEM((MR, N + LANES), bf16),
            pltpu.VMEM((MR, N), f32),
            pltpu.VMEM((MR, MR), bf16),
            pltpu.VMEM((2, MR, MH), bf16),
            pltpu.VMEM((MR, MR), bf16),
            pltpu.VMEM((2, MH, MR), bf16),
            pltpu.VMEM((N, N), bf16),
            pltpu.VMEM((3, WIDE, WIDE), bf16),
            pltpu.VMEM((2, 2 * WIDE + LANES, WIDE), bf16),
            pltpu.VMEM((count, per_chunk, 8, LANES), f32),
            pltpu.VMEM((count, per_chunk, 8, LANES), f32),
            pltpu.VMEM((per_chunk, 8, LANES), f32),
            pltpu.VMEM((count, per_chunk, 8, LANES), f32),
            dma((6,)),
            dma((4,)), dma((4,)),
            dma((2, 2)), dma((2,)),
            dma((2,)), dma((2,)),
            dma((3,)), dma((3,)),
            dma((4,)), dma((4, 2)),
            dma((2,)), dma((2,)),
        ],
        compiler_params=pltpu.CompilerParams(
            collective_id=0, has_side_effects=True, vmem_limit_bytes=60 * 1024 * 1024
        ),
        name="covariance",
    )(*args)
    return result.reshape(control.shape)


def solution(mesh):
    return jax.shard_map(
        per_device,
        mesh=mesh,
        in_specs=(
            P("member", None, "tile", None),
            P(None, "tile", None),
            P("tile", None),
            P(),
            P(),
            P(),
        ),
        out_specs=P(None, "tile", None),
        check_vma=False,
    )
```

```python
import functools
import math

import jax
import jax.numpy as jnp
import numpy as np
from jax import lax
from jax.experimental import pallas as pl
from jax.experimental.pallas import tpu as pltpu
from jax.sharding import PartitionSpec as P

HALF = 12
ROWS = 16
FACES = 6
LANES = 128
WIDE = 2 * LANES
f32, bf16, i32 = jnp.float32, jnp.bfloat16, jnp.int32


def iota(shape, dim):
    return lax.broadcasted_iota(i32, shape, dim)


def dot(a, b):
    return lax.dot_general(a, b, (((1,), (0,)), ((), ())), preferred_element_type=f32)


def dot_nt(a, b):
    return lax.dot_general(a, b, (((1,), (1,)), ((), ())), preferred_element_type=f32)


def dot_tn(a, b):
    return lax.dot_general(a, b, (((0,), (0,)), ((), ())), preferred_element_type=f32)


def onehot(mask):
    return jnp.where(mask, 1.0, 0.0).astype(bf16)


def taper(band):
    rows, taps = band.shape
    steps = np.arange(2 * HALF + 1, dtype=np.float32) - HALF
    curve = np.exp(-((steps / HALF) ** 2))
    scale = 1.0 / math.sqrt(math.sqrt(float(np.sum(curve * curve))) * float(np.sum(curve)))
    lane = iota((1, taps), 1).astype(f32)
    g = jnp.exp(-(((lane - HALF) / HALF) ** 2)) * scale
    wide = jnp.concatenate([band * g, jnp.zeros((rows, LANES - taps), f32)], axis=1)
    return wide.astype(bf16).astype(f32)


def make_key(member, code, layer, good, other):
    return jnp.where(good, ((member * 24 + code) << 4) + layer, other)


def col_parts(lane):
    face, rest = lane >> 5, lane & 31
    second = rest >= HALF
    layer = jnp.where(second, rest - HALF, rest)
    return face, jnp.where(second, 3, 2), layer, (rest < 2 * HALF) & (face < FACES)


def hub_parts(lane):
    face, layer = (lane & (LANES - 1)) >> 4, lane & 15
    return lane >> 7, face, layer, (face < FACES) & (layer < HALF)


def row_parts(index):
    both = index >> 4
    member = jnp.where(both >= FACES, 1, 0)
    return member, both - FACES * member, index & 15


def halo_parts(index):
    both = (index * 171) >> 11
    member = jnp.where(both >= FACES, 1, 0)
    return member, both - FACES * member, index - both * HALF


def pick_face(face, values):
    out = jnp.zeros(face.shape, i32)
    for f in range(FACES):
        out = jnp.where(face == f, values[f], out)
    return out


def whole_kernel(
    tiles, members, count,
    pert_in, control_in, rows_in, cols_in, peer_in, flip_in, out,
    pert, control, band_rows, band_cols, peer, flip,
    w, wh, halo_s, pa, pall_a, pw, pw_mir, qw, qr_w, qs, qr_s, pb, pb_mir, qr_b,
    pc, pc_mir, pa_c, pall_c, qc, qc_near, qr_c, sp, drh, late, late_r, qd, qr_d,
    dmat, xs, zacc, bd, bdh, bdt, bdht, jn, gmat, seam, part, got, mine, done,
    load, ring_s, ring_r, hub_s, hub_r, mir_s, mir_r, strip_s, strip_r, sc_s, sc_r, mem_s, mem_r,
):
    T, M = tiles, members
    N = ROWS * T
    NB = N // LANES
    MR, MH = M * FACES * ROWS, M * FACES * HALF
    t, me = lax.axis_index("tile"), lax.axis_index("member")
    prev, nxt, mirror = lax.rem(t + T - 1, T), lax.rem(t + 1, T), T - 1 - t
    hub = jnp.where(t >= T // 2, 1, 0)
    is_hub = (t == 0) | (t == T - 1)
    is_second = (t == 1) | (t == T - 2)
    inner = jnp.logical_not(is_hub)
    last = hub == 1

    def remote(src, dst, send, recv, where, axis="tile"):
        return pltpu.make_async_remote_copy(
            src_ref=src, dst_ref=dst, send_sem=send, recv_sem=recv,
            device_id={axis: where}, device_id_type=pl.DeviceIdType.MESH,
        )

    def each_tile(act):
        act(lax.rem(t + T // 2, T))

        def body(d, carry):
            act(lax.rem(t + T // 2 + d, T))
            act(lax.rem(t + T // 2 - d, T))
            return carry

        lax.fori_loop(1, T // 2, body, 0)

    barrier = pltpu.get_barrier_semaphore()

    def greet(where, axis="tile"):
        pl.semaphore_signal(
            barrier, inc=1, device_id={axis: where}, device_id_type=pl.DeviceIdType.MESH
        )

    @pl.when(is_hub)
    def _():
        each_tile(greet)

    @pl.when(jnp.logical_not(is_hub))
    def _():
        greet(0)
        greet(T - 1)

    for where in (mirror, prev, nxt):
        greet(where)
    for second in (1, T - 2):
        @pl.when(t != second)
        def _():
            greet(second)

    beside = []
    for step in (-1, 1):
        there = mirror + step
        beside.append((jnp.clip(there, 0, T - 1), there != t, (there >= 1) & (there <= T - 2)))

        @pl.when(inner & (there != t))
        def _():
            greet(there)
    for i in range(1, count):
        greet(lax.rem(me + i, count), "member")

    loads = [
        pltpu.make_async_copy(src, dst, load.at[i])
        for i, (src, dst) in enumerate(
            (
                (pert_in, pert), (control_in, control), (peer_in, peer), (flip_in, flip),
                (rows_in, band_rows), (cols_in, band_cols),
            )
        )
    ]
    for copy in loads:
        copy.start()

    r256, c128 = iota((WIDE, LANES), 0), iota((WIDE, LANES), 1) & 31
    sel = onehot(
        ((r256 < HALF) & (c128 == r256))
        | ((r256 >= WIDE - HALF) & (c128 == HALF + WIDE - 1 - r256))
    )
    group = iota((ROWS, LANES), 1) >> 5
    s0, s1 = iota((MH, MR), 0), iota((MH, MR), 1)
    half_of_row = (s0 * 171) >> 11
    ahead = s1 - (half_of_row << 4) - (s0 - half_of_row * HALF)
    comp = [onehot(ahead == 0), onehot(ahead == ROWS - HALF)]

    def pack(quad):
        packs = []
        for m in range(M):
            blocks = []
            for g in range(2):
                block = jnp.zeros((ROWS, LANES), f32)
                for q in range(4):
                    f = 4 * g + q
                    if f < FACES:
                        at = (m * FACES + f) * ROWS
                        block = jnp.where(group == q, quad[at : at + ROWS], block)
                blocks.append(block)
            packs.append(jnp.concatenate(blocks, axis=1).astype(bf16))
        return packs

    def pack_ends(flat):
        ends = jnp.concatenate([flat[:, :LANES], flat[:, N - LANES :]], axis=1)
        return pack(dot(ends, sel))

    def spread(packs):
        parts = []
        for m in range(M):
            for f in range(FACES):
                g, q = f // 4, f % 4
                block = packs[m][:, g * LANES : (g + 1) * LANES]
                parts.append(jnp.where(group == q, block, 0.0))
        return jnp.concatenate(parts, axis=0).astype(bf16)

    for copy in loads[:5]:
        copy.wait()
    for m in range(M):
        weighted = (pert[m].astype(f32) * control[...]).astype(bf16)
        w[m * FACES * ROWS : (m + 1) * FACES * ROWS, :] = weighted.reshape(FACES * ROWS, N)

    peers = [[peer[e, f] for e in range(4)] for f in range(FACES)]
    flips = [[flip[e, f] for e in range(4)] for f in range(FACES)]
    src_face, src_edge, src_layer, src_good = col_parts(iota((WIDE, WIDE), 0))
    src_cols = make_key(0, 4 * src_face + src_edge, src_layer, src_good, -1)
    lane = iota((WIDE, WIDE), 1)
    _, hub_face, hub_layer, hub_good = hub_parts(lane)
    to_hub = jnp.where(
        lane < LANES,
        pick_face(hub_face, [peers[f][0] for f in range(FACES)]),
        pick_face(hub_face, [peers[f][1] for f in range(FACES)]),
    )
    hub_pick = onehot(src_cols == make_key(0, to_hub, hub_layer, hub_good, -2))

    def hub_messages(packs, dst):
        chosen = [dot(value, hub_pick).astype(bf16) for value in packs]
        for h in range(2):
            for m in range(M):
                dst[h, :, m * LANES : (m + 1) * LANES] = chosen[m][:, h * LANES : (h + 1) * LANES]

    own_taps = taper(band_rows[...])
    strips = pack_ends(w[...])
    hub_messages(strips, pa)
    for m, value in enumerate(strips):
        pw[m] = value
    pw[0, :, LANES:] += pltpu.roll(own_taps, LANES // 2, 1).astype(bf16)
    halo_s[0] = dot(comp[0], w[...]).astype(bf16)
    halo_s[1] = dot(comp[1], w[...]).astype(bf16)

    hub_peers = [jnp.where(last, peers[f][1], peers[f][0]) for f in range(FACES)]
    hub_flips = [jnp.where(last, flips[f][1], flips[f][0]) for f in range(FACES)]

    def flipped(value):
        return dot(value.astype(bf16), jn[...])

    def by_hub(first, second):
        return lambda at: jnp.where(last, second(at), first(at))

    def forward(at):
        return at

    def back_row(at):
        return ROWS - 1 - at

    def back_halo(at):
        return HALF - 1 - at

    def turn_rows(flat, lanes_of):
        shape = (flat.shape[0], WIDE)
        member, face, at = row_parts(iota(shape, 0))
        here = lanes_of(member, face, by_hub(forward, back_row)(at)) == iota(shape, 1)
        turned = pick_face(face, hub_flips) == 1
        value = dot_tn(flat, onehot(here & jnp.logical_not(turned)))
        return value + dot_tn(flipped(flat).astype(bf16), onehot(here & turned))

    @pl.when(is_hub | is_second)
    def _():
        jn[...] = onehot(iota((N, N), 0) + iota((N, N), 1) == N - 1)

    @pl.when(is_hub)
    def _():
        value = turn_rows(w[...], lambda member, face, at: 96 * member + 16 * face + at)
        low, high = value[:, :LANES].astype(bf16), value[:, LANES:].astype(bf16)
        extra = pltpu.roll(own_taps, LANES // 2, 1).astype(bf16)
        qw[:, :, :LANES] = low.reshape(T, ROWS, LANES)
        qw[:, :, LANES:] = high.reshape(T, ROWS, LANES) + extra[None]

    @pl.when(is_second)
    def _():
        value = turn_rows(
            w[...],
            lambda member, face, at: jnp.where(at < 8, 48 * member + 8 * face + at, -1),
        )
        qs[...] = value[:, :LANES].astype(bf16).reshape(T, ROWS, LANES)

    greeted = 3 + count - 1 + jnp.where(is_hub, T - 1, 2) + jnp.where(is_second, T - 1, 0)
    for _, other, inside in beside:
        greeted = greeted + jnp.where(other & inside, 1, 0)
    pl.semaphore_wait(barrier, greeted)

    def hub_copies(src, dst, base):
        return [
            remote(src.at[h], dst.at[t], hub_s.at[base, h], hub_r.at[base], h * (T - 1))
            for h in range(2)
        ]

    def start_to_hubs(copies):
        for h in range(2):
            @pl.when(t != h * (T - 1))
            def _():
                copies[h].start()

    def finish_to_hubs(copies):
        for h in range(2):
            @pl.when(t != h * (T - 1))
            def _():
                copies[h].wait_send()

    def wait_at_hub(dst, base):
        others = dst.at[pl.ds(0, T - 1)]
        pltpu.make_async_copy(others, others, hub_r.at[base]).wait()

    def send_all(q, qr, base):
        def send(there):
            remote(q.at[there], qr.at[hub], sc_s.at[base], sc_r.at[base, hub], there).start()

        each_tile(send)
        qr[hub] = q[t]

    def wait_all(q, qr, base, places):
        for h, place in enumerate(places):
            @pl.when(t != place)
            def _():
                remote(q.at[0], qr.at[h], sc_s.at[base], sc_r.at[base, h], place).wait_recv()

    to_hubs_a = hub_copies(pa, pall_a, 0)
    start_to_hubs(to_hubs_a)

    @pl.when(is_hub)
    def _():
        send_all(qw, qr_w, 0)

    @pl.when(is_second)
    def _():
        send_all(qs, qr_s, 1)

    strip_copies = []
    middle = (mirror, t >= 0, inner)
    for i, (there, other, inside) in enumerate((beside[0], middle, beside[1])):
        strip_copies.append(remote(pw, pw_mir.at[i], strip_s.at[i], strip_r.at[i], there))

        @pl.when(other & inside)
        def _():
            strip_copies[i].start()

    ring_a = [
        remote(halo_s.at[0], wh.at[1], ring_s.at[0], ring_r.at[0], prev),
        remote(halo_s.at[1], wh.at[0], ring_s.at[1], ring_r.at[1], nxt),
    ]
    for copy in ring_a:
        copy.start()

    for copy in loads[5:]:
        copy.wait()
    lane = iota((LANES, LANES), 1)
    blocks = {}
    for b in range(NB):
        wide = taper(jnp.transpose(band_cols[:, b * LANES : (b + 1) * LANES]))
        wide = jnp.concatenate([wide, jnp.zeros((LANES, LANES), f32)], axis=1)
        wide = pltpu.roll(wide, 0, 1, stride=1, stride_axis=0)
        wide = pltpu.roll(wide, WIDE - HALF, 1)
        over = wide[:, LANES:]
        for c, value in (
            (b, wide[:, :LANES]),
            ((b + 1) % (NB + 1), jnp.where(lane < HALF, over, 0.0)),
            ((b + NB) % (NB + 1), jnp.where(lane >= LANES - HALF, over, 0.0)),
        ):
            blocks[b, c] = blocks[b, c] + value if (b, c) in blocks else value
    from_lane, to_lane = iota((LANES, LANES), 0), iota((LANES, LANES), 1) & 31
    rim_order = onehot(
        ((to_lane < HALF) & (from_lane == LANES - 1 - to_lane))
        | ((to_lane >= HALF) & (to_lane < 2 * HALF) & (from_lane == to_lane - HALF))
    )
    for b in range(NB):
        for c in range(NB + 1):
            value = blocks.get((b, c))
            value = jnp.zeros((LANES, LANES), bf16) if value is None else value.astype(bf16)
            if c == NB:
                value = dot(value, rim_order).astype(bf16)
            dmat[b * LANES : (b + 1) * LANES, c * LANES : (c + 1) * LANES] = value

    def skewed(taps, first):
        wide = jnp.concatenate([taps, jnp.zeros((ROWS, LANES), f32)], axis=1)
        wide = pltpu.roll(wide, first, 1, stride=1, stride_axis=0)
        return wide[:, :LANES].astype(bf16)

    skew = skewed(own_taps, ROWS - HALF)
    every = jnp.concatenate([skew] * (M * FACES), axis=0)
    tap_at, dst_at = iota((LANES, WIDE), 0), iota((LANES, WIDE), 1)
    row_at, col_at = iota((MR, WIDE), 0) >> 4, iota((MR, WIDE), 1)
    half_at = (dst_at * 171) >> 11
    step_at = dst_at - half_at * HALF

    def banded(expand, same):
        full = jnp.where(same, dot(every, onehot(expand)), 0.0)
        square = jnp.concatenate([full, jnp.zeros((WIDE - MR, WIDE), f32)], axis=0)
        return full, jnp.transpose(square)

    full, turned = banded(tap_at == ROWS + (dst_at & 15), row_at == col_at >> 4)
    bd[...] = full[:, :MR].astype(bf16)
    bdt[...] = turned[:MR, :MR].astype(bf16)
    for side, first in ((0, ROWS - HALF), (1, 2 * ROWS)):
        full, turned = banded(
            (tap_at == first + step_at) & (dst_at < MH), row_at == (col_at * 171) >> 11
        )
        bdh[side] = full[:, :MH].astype(bf16)
        bdht[side] = turned[:MH, :MR].astype(bf16)

    want_face, want_edge, want_layer, want_good = col_parts(iota((WIDE, WIDE), 1))
    want_code = jnp.where(
        want_edge == 2,
        pick_face(want_face, [peers[f][2] for f in range(FACES)]),
        pick_face(want_face, [peers[f][3] for f in range(FACES)]),
    )
    want_turn = jnp.where(
        want_edge == 2,
        pick_face(want_face, [flips[f][2] for f in range(FACES)]),
        pick_face(want_face, [flips[f][3] for f in range(FACES)]),
    )
    want = make_key(0, want_code, want_layer, want_good, -2)
    src_hub, row_face, row_layer, row_good = hub_parts(iota((WIDE, WIDE), 0))
    src_rows = make_key(0, 4 * row_face + src_hub, row_layer, row_good, -1)
    gmat[0] = onehot((src_cols == want) & (want_turn == 0))
    gmat[1] = onehot(src_rows == want)
    gmat[2] = onehot((src_cols == want) & (want_turn == 1))
    back = onehot(iota((ROWS, ROWS), 0) + iota((ROWS, ROWS), 1) == ROWS - 1)

    def gather_rows(shape, parts, layer_of, cols, rows):
        def wanted(width):
            index = iota((2 * shape, width), 0)
            turned = index >= shape
            member, face, at = parts(jnp.where(turned, index - shape, index))
            layer = layer_of(at)
            good = (layer < HALF) & ((pick_face(face, hub_flips) == 1) == turned)
            return member, face, layer, good

        total = None
        if cols is not None:
            member, face, layer, good = wanted(WIDE)
            src_m, src_f, src_k, src_ok = hub_parts(iota((2 * shape, WIDE), 1))
            pick = onehot(
                make_key(member, face, layer, good, -2) == make_key(src_m, src_f, src_k, src_ok, -1)
            )
            total = dot_nt(pick, cols[...].reshape(N, WIDE))
        for source, source_parts, source_layer, source_edge in rows:
            member, face, layer, good = wanted(source.shape[0])
            code = pick_face(face, hub_peers)
            src_m, src_f, src_at = source_parts(iota((2 * shape, source.shape[0]), 1))
            src_k = source_layer(src_at)
            pick = onehot(
                make_key(member, code, layer, good, -2)
                == make_key(src_m, 4 * src_f + source_edge, src_k, src_k < HALF, -1)
            )
            value = dot(pick, source)
            total = value if total is None else total + value
        return total[:shape] + flipped(total[shape:])

    def finish_scatter(q, base):
        others = q.at[pl.ds(0, T - 1)]
        pltpu.make_async_copy(others, others, sc_s.at[base]).wait()

    def arrive_cols(direct, mirrored, qr):
        packs = []
        for m in range(M):
            value = jnp.zeros((ROWS, WIDE), f32)
            if direct is not None:
                value = value + dot(direct[m], gmat[0])
                value = value + dot(back, dot(mirrored[m], gmat[2]).astype(bf16))
            if qr is not None:
                near = [qr[h, :, m * LANES : (m + 1) * LANES] for h in range(2)]
                value = value + dot(jnp.concatenate(near, axis=1), gmat[1])
            packs.append(value)
        return packs

    x = dot(bd[...], w[...])
    for copy in ring_a:
        copy.wait_recv()

    @pl.when(is_hub)
    def _():
        pall_a[t] = pa[hub]
        wait_at_hub(pall_a, 0)
        halo = by_hub(back_halo, forward)
        wh[hub] = gather_rows(
            MH, halo_parts, halo, pall_a,
            (
                (w[...], row_parts, by_hub(forward, back_row), hub),
                (wh[hub], halo_parts, halo, 1 - hub),
            ),
        ).astype(bf16)

    x = x + dot(bdh[0], wh[0]) + dot(bdh[1], wh[1])
    xs[:, :N] = x.astype(bf16)

    for m, value in enumerate(pack_ends(xs[:, :N])):
        pb[m] = value
    mirror_b = remote(pb, pb_mir, mir_s.at[0], mir_r.at[0], mirror)

    def to_strips(member, face, at):
        return jnp.where(at < HALF, LANES * member + 16 * face + at, -1)

    @pl.when(is_hub)
    def _():
        mirror_b.start()
        rough = dot_nt(xs[:, :N], dmat[:, :N]).astype(bf16)
        value = turn_rows(dot(rough, dmat[:, :N]).astype(bf16), to_strips)
        qc[...] = value.astype(bf16).reshape(T, ROWS, WIDE)

        def send(there):
            @pl.when((there > 1) & (there < T - 2))
            def _():
                remote(qc.at[there], qr_c.at[hub], sc_s.at[2], sc_r.at[2, hub], there).start()

        each_tile(send)

    wait_all(qw, qr_w, 0, (0, T - 1))
    wait_all(qs, qr_s, 1, (1, T - 2))

    def sent_taps(block):
        taps = pltpu.roll(block.astype(f32), LANES // 2, 1)
        return jnp.where(iota((ROWS, LANES), 1) <= 2 * HALF, taps, 0.0)

    edge_shape = (WIDE + LANES + WIDE, WIDE)
    index = iota(edge_shape, 0)
    part_w, part_s = index < WIDE, index < WIDE + LANES
    low = jnp.where(part_w, index, index - WIDE)
    arr_m, arr_f, arr_k, arr_ok = hub_parts(index - WIDE - LANES)
    half_w, half_s = jnp.where(low >= 96, 1, 0), jnp.where(low >= 48, 1, 0)
    rest_w, rest_s = low - 96 * half_w, low - 48 * half_s
    src_mf = jnp.where(
        part_w,
        jnp.where(low < 192, FACES * half_w + (rest_w >> 4), -1),
        jnp.where(
            part_s,
            jnp.where(low < 96, FACES * half_s + (rest_s >> 3), -1),
            jnp.where(arr_ok, FACES * arr_m + arr_f, -1),
        ),
    )
    place = jnp.where(
        part_w,
        HALF + (rest_w & 15),
        jnp.where(part_s, HALF + ROWS + (rest_s & 7), HALF - 1 - arr_k),
    )
    dst_m, dst_f, dst_k, dst_ok = hub_parts(iota(edge_shape, 1))
    same = src_mf == jnp.where(dst_ok, FACES * dst_m + dst_f, -2)
    from_place = onehot(place[:, :LANES] == iota((edge_shape[0], LANES), 1))
    layer_lane = iota((ROWS, WIDE), 1) & 15
    to_layer = onehot((iota((ROWS, WIDE), 0) == layer_lane) & (layer_lane < HALF))
    turn_taps = onehot(
        (iota((LANES, LANES), 0) + iota((LANES, LANES), 1) == 2 * HALF)
    )
    for h in range(2):
        taps = sent_taps(qr_w[h, :, LANES:])
        if h == 1:
            taps = dot(dot(back, taps.astype(bf16)).astype(bf16), turn_taps)
        by_layer = dot_nt(from_place, skewed(taps, 0)).astype(bf16)
        seam[h] = jnp.where(same, dot(by_layer, to_layer), 0.0).astype(bf16)
        line = jnp.concatenate([qr_w[h], qr_s[h], pa[h]], axis=1)
        qr_b[h] = dot(line, seam[h]).astype(bf16)

    @pl.when(inner)
    def _():
        for i, (there, other, inside) in enumerate((beside[0], middle, beside[1])):
            @pl.when(other)
            def _():
                strip_copies[i].wait_recv()

            if i != 1:
                @pl.when(jnp.logical_not(other))
                def _():
                    pw_mir[i] = pw[...]

        mirror_skew = skewed(sent_taps(pw_mir[1, 0, :, LANES:]), ROWS - HALF)
        for m in range(M):
            rows = jnp.concatenate([pw_mir[0, m], pw_mir[1, m], pw_mir[2, m]], axis=0)
            pb_mir[m] = dot(mirror_skew[:, : 3 * ROWS], rows).astype(bf16)

    @pl.when(is_hub)
    def _():
        mirror_b.wait_recv()

    xs[:, N:] = spread(arrive_cols(pb, pb_mir, qr_b))
    y = dot_nt(xs[...], dmat[...]).astype(bf16)

    rims = pack(dot(y, dmat[:, N:]))
    for m, value in enumerate(rims):
        pc[m] = value
    mirror_c = remote(pc, pc_mir, mir_s.at[1], mir_r.at[1], mirror)
    hub_messages(rims, pa_c)
    to_hubs_c = hub_copies(pa_c, pall_c, 1)
    start_to_hubs(to_hubs_c)
    mirror_c.start()
    zacc[...] = dot(y, dmat[:, :N])

    def end_columns(flat, width):
        at, end = iota((WIDE, 2 * width), 0), iota((WIDE, 2 * width), 1)
        pick = onehot(at == jnp.where(end < width, end, end + WIDE - 2 * width))
        both = iota((2 * width, 2 * width), 0) + iota((2 * width, 2 * width), 1)
        near = jnp.concatenate([flat[:, :LANES], flat[:, N - LANES :]], axis=1)
        near = dot(near, pick).astype(bf16)
        return near, dot(near, onehot(both == 2 * width - 1)).astype(bf16)

    def near_strips(flat, width, parts, layer_of, lanes_of):
        near, far = end_columns(flat, width)
        shape = (flat.shape[0], WIDE)
        member, face, at = parts(iota(shape, 0))
        here = lanes_of(member, face, layer_of(at)) == iota(shape, 1)
        turned = pick_face(face, hub_flips) == 1
        value = dot_tn(near, onehot(here & jnp.logical_not(turned)))
        value = value + dot_tn(far, onehot(here & turned))
        return value.astype(bf16).reshape(2 * width // ROWS, ROWS, WIDE)

    @pl.when(is_hub)
    def _():
        qc_near[...] = near_strips(
            zacc[...].astype(bf16), 2 * ROWS, row_parts, by_hub(forward, back_row), to_strips
        )
        for i, there in ((1, 1), (2, T - 2)):
            remote(
                qc_near.at[i], qr_c.at[hub], sc_s.at[3 + i], sc_r.at[2, hub], there
            ).start()

    ring_d = [
        remote(sp.at[0], drh.at[1], ring_s.at[2], ring_r.at[2], prev),
        remote(sp.at[1], drh.at[0], ring_s.at[3], ring_r.at[3], nxt),
    ]
    ring_late = [
        remote(late.at[0], late_r.at[1], ring_s.at[4], ring_r.at[4], prev),
        remote(late.at[1], late_r.at[0], ring_s.at[5], ring_r.at[5], nxt),
    ]

    def start_spills(value):
        for side in range(2):
            sp[side] = dot(bdht[side], value).astype(bf16)
            ring_d[side].start()

    @pl.when(inner)
    def _():
        start_spills(zacc[...].astype(bf16))

    mirror_c.wait_recv()

    @pl.when(is_hub)
    def _():
        pall_c[t] = pa_c[hub]
        wait_at_hub(pall_c, 1)
        zacc[...] += gather_rows(MR, row_parts, by_hub(forward, back_row), pall_c, ())

    ends = dot_nt(spread(arrive_cols(pc, pc_mir, None)), sel)
    zacc[:, :LANES] += ends[:, :LANES]
    zacc[:, N - LANES :] += ends[:, LANES:]

    z = zacc[...].astype(bf16)
    quarter = iota((MH, LANES), 1) >> 5

    def both_ends(value):
        return dot(jnp.concatenate([value[:, :LANES], value[:, N - LANES :]], axis=1), sel)

    z_ends = both_ends(z).astype(bf16)
    for side in range(2):
        value = dot(bdht[side], z_ends)
        late[side] = jnp.where(quarter == 1 - side, value, 0.0).astype(bf16)
        ring_late[side].start()

    @pl.when(is_hub)
    def _():
        start_spills(z)

    hub_d = remote(qd.at[1 - hub], qr_d.at[hub], sc_s.at[3], sc_r.at[3, hub], mirror)

    @pl.when(is_hub)
    def _():
        qd[...] = near_strips(
            sp[hub], ROWS, halo_parts, by_hub(back_halo, forward),
            lambda member, face, at: LANES * member + 16 * face + at,
        )
        qr_d[hub] = qd[hub]
        hub_d.start()

    zacc[...] = dot(bdt[...], z)

    @pl.when(inner)
    def _():
        wait_all(qc, qr_c, 2, (0, T - 1))
        for h in range(2):
            strip = (qr_c[h].astype(f32) + pa_c[h].astype(f32)).astype(bf16)
            qr_d[h] = dot_nt(strip, seam[h, WIDE + LANES :, :]).astype(bf16)

    for copy in ring_d + ring_late:
        copy.wait_recv()

    @pl.when(is_hub)
    def _():
        arrived = gather_rows(
            MH, halo_parts, by_hub(forward, back_halo), None,
            (
                (sp[hub], halo_parts, by_hub(back_halo, forward), hub),
                (drh[hub], halo_parts, by_hub(forward, back_halo), 1 - hub),
            ),
        ).astype(bf16)
        drh[hub] = arrived
        late_r[hub] = jnp.where(quarter == hub, both_ends(arrived), 0.0).astype(bf16)

    spill = dot_tn(comp[0], drh[0]) + dot_tn(comp[1], drh[1])
    column = iota((MR, N), 1)
    zacc[...] += jnp.where((column >= HALF) & (column < N - HALF), spill, 0.0)
    spill_ends = dot_tn(comp[0], late_r[0]) + dot_tn(comp[1], late_r[1])
    ends = dot_nt(spill_ends.astype(bf16), sel)
    zacc[:, :LANES] += ends[:, :LANES]
    zacc[:, N - LANES :] += ends[:, LANES:]
    @pl.when(is_hub)
    def _():
        remote(qd.at[0], qr_d.at[1 - hub], sc_s.at[3], sc_r.at[3, 1 - hub], mirror).wait_recv()

    ends = dot_nt(spread(arrive_cols(None, None, qr_d)), sel)
    zacc[:, :LANES] += ends[:, :LANES]
    zacc[:, N - LANES :] += ends[:, LANES:]

    FR = FACES * ROWS
    total = jnp.zeros((FR, N), f32)
    for m in range(M):
        total = total + pert[m].astype(f32).reshape(FR, N) * zacc[m * FR : (m + 1) * FR, :]
    per_chunk = part.shape[1]
    for u in range(count * per_chunk):
        r, c = u // NB, u % NB
        part[u // per_chunk, u % per_chunk] = total[r * 8 : r * 8 + 8, c * LANES : (c + 1) * LANES]

    peers_of_me = [lax.rem(me + i, count) for i in range(1, count)]
    for there in peers_of_me:
        remote(part.at[there], got.at[me], mem_s.at[0], mem_r.at[0], there, "member").start()
    got[me] = part[me]
    others = got.at[pl.ds(0, count - 1)]
    pltpu.make_async_copy(others, others, mem_r.at[0]).wait()
    chunk = got[0]
    for i in range(1, count):
        chunk = chunk + got[i]
    mine[...] = chunk * (1.0 / (M * count - 1.0))
    for there in peers_of_me:
        remote(mine, done.at[me], mem_s.at[1], mem_r.at[1], there, "member").start()
    done[me] = mine[...]
    finished = done.at[pl.ds(0, count - 1)]
    pltpu.make_async_copy(finished, finished, mem_r.at[1]).wait()
    for u in range(count * per_chunk):
        r, c = u // NB, u % NB
        out[r * 8 : r * 8 + 8, c * LANES : (c + 1) * LANES] = done[u // per_chunk, u % per_chunk]

    for copy in ring_a + ring_d + ring_late + [mirror_c]:
        copy.wait_send()
    for i, (there, other, inside) in enumerate((beside[0], middle, beside[1])):
        @pl.when(other & inside)
        def _():
            strip_copies[i].wait_send()

    finish_to_hubs(to_hubs_a)
    finish_to_hubs(to_hubs_c)

    @pl.when(is_hub)
    def _():
        finish_scatter(qw, 0)
        far = qc.at[pl.ds(0, T - 4)]
        pltpu.make_async_copy(far, far, sc_s.at[2]).wait()
        for i in (1, 2):
            remote(qc_near.at[i], qr_c.at[hub], sc_s.at[3 + i], sc_r.at[2, hub], 1).wait_send()
        mirror_b.wait_send()
        hub_d.wait_send()

    @pl.when(is_second)
    def _():
        finish_scatter(qs, 1)

    for i in range(2):
        pltpu.make_async_copy(others, others, mem_s.at[i]).wait()


def per_device(perturbations, control, band_rows, band_cols, edge_peer, edge_flip):
    T, count = lax.axis_size("tile"), lax.axis_size("member")
    M = perturbations.shape[0]
    N = control.shape[-1]
    MR, MH = M * FACES * ROWS, M * FACES * HALF
    per_chunk = FACES * ROWS * N // (8 * LANES) // count
    vmem, hbm = pl.BlockSpec(memory_space=pltpu.VMEM), pl.BlockSpec(memory_space=pltpu.HBM)
    dma = pltpu.SemaphoreType.DMA
    args = (perturbations, control, band_rows, band_cols.T, edge_peer.T, edge_flip.T)
    result = pl.pallas_call(
        functools.partial(whole_kernel, T, M, count),
        out_shape=jax.ShapeDtypeStruct((FACES * ROWS, N), f32),
        in_specs=[hbm] * 6,
        out_specs=vmem,
        scratch_shapes=[
            pltpu.VMEM(args[0].shape, bf16),
            pltpu.VMEM(args[1].shape, f32),
            pltpu.VMEM(args[2].shape, f32),
            pltpu.VMEM(args[3].shape, f32),
            pltpu.SMEM(args[4].shape, i32),
            pltpu.SMEM(args[5].shape, i32),
            pltpu.VMEM((MR, N), bf16),
            pltpu.VMEM((2, MH, N), bf16),
            pltpu.VMEM((2, MH, N), bf16),
            pltpu.VMEM((2, ROWS, WIDE), bf16),
            pltpu.VMEM((T, ROWS, WIDE), bf16),
            pltpu.VMEM((M, ROWS, WIDE), bf16),
            pltpu.VMEM((3, M, ROWS, WIDE), bf16),
            pltpu.VMEM((T, ROWS, WIDE), bf16),
            pltpu.VMEM((2, ROWS, WIDE), bf16),
            pltpu.VMEM((T, ROWS, LANES), bf16),
            pltpu.VMEM((2, ROWS, LANES), bf16),
            pltpu.VMEM((M, ROWS, WIDE), bf16),
            pltpu.VMEM((M, ROWS, WIDE), bf16),
            pltpu.VMEM((2, ROWS, WIDE), bf16),
            pltpu.VMEM((M, ROWS, WIDE), bf16),
            pltpu.VMEM((M, ROWS, WIDE), bf16),
            pltpu.VMEM((2, ROWS, WIDE), bf16),
            pltpu.VMEM((T, ROWS, WIDE), bf16),
            pltpu.VMEM((T, ROWS, WIDE), bf16),
            pltpu.VMEM((4, ROWS, WIDE), bf16),
            pltpu.VMEM((2, ROWS, WIDE), bf16),
            pltpu.VMEM((2, MH, N), bf16),
            pltpu.VMEM((2, MH, N), bf16),
            pltpu.VMEM((2, MH, LANES), bf16),
            pltpu.VMEM((2, MH, LANES), bf16),
            pltpu.VMEM((2, ROWS, WIDE), bf16),
            pltpu.VMEM((2, ROWS, WIDE), bf16),
            pltpu.VMEM((N, N + LANES), bf16),
            pltpu.VMEM((MR, N + LANES), bf16),
            pltpu.VMEM((MR, N), f32),
            pltpu.VMEM((MR, MR), bf16),
            pltpu.VMEM((2, MR, MH), bf16),
            pltpu.VMEM((MR, MR), bf16),
            pltpu.VMEM((2, MH, MR), bf16),
            pltpu.VMEM((N, N), bf16),
            pltpu.VMEM((3, WIDE, WIDE), bf16),
            pltpu.VMEM((2, 2 * WIDE + LANES, WIDE), bf16),
            pltpu.VMEM((count, per_chunk, 8, LANES), f32),
            pltpu.VMEM((count, per_chunk, 8, LANES), f32),
            pltpu.VMEM((per_chunk, 8, LANES), f32),
            pltpu.VMEM((count, per_chunk, 8, LANES), f32),
            dma((6,)),
            dma((6,)), dma((6,)),
            dma((2, 2)), dma((2,)),
            dma((2,)), dma((2,)),
            dma((3,)), dma((3,)),
            dma((6,)), dma((4, 2)),
            dma((2,)), dma((2,)),
        ],
        compiler_params=pltpu.CompilerParams(
            collective_id=0, has_side_effects=True, vmem_limit_bytes=60 * 1024 * 1024
        ),
        name="covariance",
    )(*args)
    return result.reshape(control.shape)


def solution(mesh):
    return jax.shard_map(
        per_device,
        mesh=mesh,
        in_specs=(
            P("member", None, "tile", None),
            P(None, "tile", None),
            P("tile", None),
            P(),
            P(),
            P(),
        ),
        out_specs=P(None, "tile", None),
        check_vma=False,
    )
```

```python
import functools
import math

import jax
import jax.numpy as jnp
import numpy as np
from jax import lax
from jax.experimental import pallas as pl
from jax.experimental.pallas import tpu as pltpu
from jax.sharding import PartitionSpec as P

HALF = 12
ROWS = 16
FACES = 6
LANES = 128
WIDE = 2 * LANES
f32, bf16, i32 = jnp.float32, jnp.bfloat16, jnp.int32


def iota(shape, dim):
    return lax.broadcasted_iota(i32, shape, dim)


def dot(a, b):
    return lax.dot_general(a, b, (((1,), (0,)), ((), ())), preferred_element_type=f32)


def dot_nt(a, b):
    return lax.dot_general(a, b, (((1,), (1,)), ((), ())), preferred_element_type=f32)


def dot_tn(a, b):
    return lax.dot_general(a, b, (((0,), (0,)), ((), ())), preferred_element_type=f32)


def onehot(mask):
    return jnp.where(mask, 1.0, 0.0).astype(bf16)


def taper(band):
    rows, taps = band.shape
    steps = np.arange(2 * HALF + 1, dtype=np.float32) - HALF
    curve = np.exp(-((steps / HALF) ** 2))
    scale = 1.0 / math.sqrt(math.sqrt(float(np.sum(curve * curve))) * float(np.sum(curve)))
    lane = iota((1, taps), 1).astype(f32)
    g = jnp.exp(-(((lane - HALF) / HALF) ** 2)) * scale
    wide = jnp.concatenate([band * g, jnp.zeros((rows, LANES - taps), f32)], axis=1)
    return wide.astype(bf16).astype(f32)


def make_key(member, code, layer, good, other):
    return jnp.where(good, ((member * 24 + code) << 4) + layer, other)


def col_parts(lane):
    face, rest = lane >> 5, lane & 31
    second = rest >= HALF
    layer = jnp.where(second, rest - HALF, rest)
    return face, jnp.where(second, 3, 2), layer, (rest < 2 * HALF) & (face < FACES)


def hub_parts(lane):
    face, layer = (lane & (LANES - 1)) >> 4, lane & 15
    return lane >> 7, face, layer, (face < FACES) & (layer < HALF)


def row_parts(index):
    both = index >> 4
    member = jnp.where(both >= FACES, 1, 0)
    return member, both - FACES * member, index & 15


def halo_parts(index):
    both = (index * 171) >> 11
    member = jnp.where(both >= FACES, 1, 0)
    return member, both - FACES * member, index - both * HALF


def pick_face(face, values):
    out = jnp.zeros(face.shape, i32)
    for f in range(FACES):
        out = jnp.where(face == f, values[f], out)
    return out


def whole_kernel(
    tiles, members, count,
    pert_in, control_in, rows_in, cols_in, peer_in, flip_in, out,
    pert, control, band_rows, band_cols, peer, flip,
    w, wh, halo_s, pa, pall_a, pw, pw_mir, qw, qr_w, qs, qr_s, pb, pb_mir, qr_b,
    pc, pc_mir, pa_c, pall_c, qc, qr_c, sp, drh, late, late_r, qd, qr_d,
    dmat, xs, zacc, bd, bdh, bdt, bdht, jn, gmat, seam, seam_mask, from_place, picks, part, got, mine, done,
    load, ring_s, ring_r, hub_s, hub_r, mir_s, mir_r, strip_s, strip_r, sc_s, sc_r, mem_s, mem_r,
):
    T, M = tiles, members
    N = ROWS * T
    NB = N // LANES
    MR, MH = M * FACES * ROWS, M * FACES * HALF
    t, me = lax.axis_index("tile"), lax.axis_index("member")
    prev, nxt, mirror = lax.rem(t + T - 1, T), lax.rem(t + 1, T), T - 1 - t
    hub = jnp.where(t >= T // 2, 1, 0)
    is_hub = (t == 0) | (t == T - 1)
    is_second = (t == 1) | (t == T - 2)
    inner = jnp.logical_not(is_hub)
    last = hub == 1

    def remote(src, dst, send, recv, where, axis="tile"):
        return pltpu.make_async_remote_copy(
            src_ref=src, dst_ref=dst, send_sem=send, recv_sem=recv,
            device_id={axis: where}, device_id_type=pl.DeviceIdType.MESH,
        )

    def each_tile(act):
        act(lax.rem(t + T // 2, T))

        def body(d, carry):
            act(lax.rem(t + T // 2 + d, T))
            act(lax.rem(t + T // 2 - d, T))
            return carry

        lax.fori_loop(1, T // 2, body, 0)

    barrier = pltpu.get_barrier_semaphore()

    def greet(where, axis="tile"):
        pl.semaphore_signal(
            barrier, inc=1, device_id={axis: where}, device_id_type=pl.DeviceIdType.MESH
        )

    @pl.when(is_hub)
    def _():
        each_tile(greet)

    @pl.when(jnp.logical_not(is_hub))
    def _():
        greet(0)
        greet(T - 1)

    for where in (mirror, prev, nxt):
        greet(where)
    for second in (1, T - 2):
        @pl.when(t != second)
        def _():
            greet(second)

    beside = []
    for step in (-1, 1):
        there = mirror + step
        beside.append((jnp.clip(there, 0, T - 1), there != t, (there >= 1) & (there <= T - 2)))

        @pl.when(inner & (there != t))
        def _():
            greet(there)
    for i in range(1, count):
        greet(lax.rem(me + i, count), "member")

    loads = [
        pltpu.make_async_copy(src, dst, load.at[i])
        for i, (src, dst) in enumerate(
            (
                (pert_in, pert), (control_in, control), (peer_in, peer), (flip_in, flip),
                (rows_in, band_rows), (cols_in, band_cols),
            )
        )
    ]
    for copy in loads:
        copy.start()

    r256, c128 = iota((WIDE, LANES), 0), iota((WIDE, LANES), 1) & 31
    sel = onehot(
        ((r256 < HALF) & (c128 == r256))
        | ((r256 >= WIDE - HALF) & (c128 == HALF + WIDE - 1 - r256))
    )
    group = iota((ROWS, LANES), 1) >> 5
    s0, s1 = iota((MH, MR), 0), iota((MH, MR), 1)
    half_of_row = (s0 * 171) >> 11
    ahead = s1 - (half_of_row << 4) - (s0 - half_of_row * HALF)
    comp = [onehot(ahead == 0), onehot(ahead == ROWS - HALF)]

    def pack(quad):
        packs = []
        for m in range(M):
            blocks = []
            for g in range(2):
                block = jnp.zeros((ROWS, LANES), f32)
                for q in range(4):
                    f = 4 * g + q
                    if f < FACES:
                        at = (m * FACES + f) * ROWS
                        block = jnp.where(group == q, quad[at : at + ROWS], block)
                blocks.append(block)
            packs.append(jnp.concatenate(blocks, axis=1).astype(bf16))
        return packs

    def pack_ends(flat):
        ends = jnp.concatenate([flat[:, :LANES], flat[:, N - LANES :]], axis=1)
        return pack(dot(ends, sel))

    def spread(packs):
        parts = []
        for m in range(M):
            for f in range(FACES):
                g, q = f // 4, f % 4
                block = packs[m][:, g * LANES : (g + 1) * LANES]
                parts.append(jnp.where(group == q, block, 0.0))
        return jnp.concatenate(parts, axis=0).astype(bf16)

    for copy in loads[:5]:
        copy.wait()
    for m in range(M):
        weighted = (pert[m].astype(f32) * control[...]).astype(bf16)
        w[m * FACES * ROWS : (m + 1) * FACES * ROWS, :] = weighted.reshape(FACES * ROWS, N)

    peers = [[peer[e, f] for e in range(4)] for f in range(FACES)]
    flips = [[flip[e, f] for e in range(4)] for f in range(FACES)]
    src_face, src_edge, src_layer, src_good = col_parts(iota((WIDE, WIDE), 0))
    src_cols = make_key(0, 4 * src_face + src_edge, src_layer, src_good, -1)
    lane = iota((WIDE, WIDE), 1)
    _, hub_face, hub_layer, hub_good = hub_parts(lane)
    to_hub = jnp.where(
        lane < LANES,
        pick_face(hub_face, [peers[f][0] for f in range(FACES)]),
        pick_face(hub_face, [peers[f][1] for f in range(FACES)]),
    )
    hub_pick = onehot(src_cols == make_key(0, to_hub, hub_layer, hub_good, -2))

    def hub_messages(packs, dst):
        chosen = [dot(value, hub_pick).astype(bf16) for value in packs]
        for h in range(2):
            for m in range(M):
                dst[h, :, m * LANES : (m + 1) * LANES] = chosen[m][:, h * LANES : (h + 1) * LANES]

    own_taps = taper(band_rows[...])
    strips = pack_ends(w[...])
    hub_messages(strips, pa)
    for m, value in enumerate(strips):
        pw[m] = value
    pw[0, :, LANES:] += pltpu.roll(own_taps, LANES // 2, 1).astype(bf16)

    def end_blocks(flat):
        return jnp.concatenate([flat[:, :LANES], flat[:, N - LANES :]], axis=1)

    for side in range(2):
        rows = dot(comp[side], w[...]).astype(bf16)
        halo_s[side, 0] = end_blocks(rows)
        halo_s[side, 1] = rows[:, LANES : N - LANES]

    hub_peers = [jnp.where(last, peers[f][1], peers[f][0]) for f in range(FACES)]
    hub_flips = [jnp.where(last, flips[f][1], flips[f][0]) for f in range(FACES)]

    def flipped(value):
        width = value.shape[1]
        return dot(value.astype(bf16), jn[:width, N - width :])

    def by_hub(first, second):
        return lambda at: jnp.where(last, second(at), first(at))

    def forward(at):
        return at

    def back_row(at):
        return ROWS - 1 - at

    def back_halo(at):
        return HALF - 1 - at

    def turn_rows(flat, lanes_of):
        shape = (flat.shape[0], WIDE)
        member, face, at = row_parts(iota(shape, 0))
        here = lanes_of(member, face, by_hub(forward, back_row)(at)) == iota(shape, 1)
        turned = pick_face(face, hub_flips) == 1
        value = dot_tn(flat, onehot(here & jnp.logical_not(turned)))
        return value + dot_tn(flipped(flat).astype(bf16), onehot(here & turned))

    @pl.when(is_hub | is_second)
    def _():
        jn[...] = onehot(iota((N, N), 0) + iota((N, N), 1) == N - 1)

    @pl.when(is_hub)
    def _():
        value = turn_rows(w[...], lambda member, face, at: 96 * member + 16 * face + at)
        low, high = value[:, :LANES].astype(bf16), value[:, LANES:].astype(bf16)
        extra = pltpu.roll(own_taps, LANES // 2, 1).astype(bf16)
        qw[:, :, :LANES] = low.reshape(T, ROWS, LANES)
        qw[:, :, LANES:] = high.reshape(T, ROWS, LANES) + extra[None]

    @pl.when(is_second)
    def _():
        value = turn_rows(
            w[...],
            lambda member, face, at: jnp.where(at < 8, 48 * member + 8 * face + at, -1),
        )
        qs[...] = value[:, :LANES].astype(bf16).reshape(T, ROWS, LANES)

    greeted = 3 + count - 1 + jnp.where(is_hub, T - 1, 2) + jnp.where(is_second, T - 1, 0)
    for _, other, inside in beside:
        greeted = greeted + jnp.where(other & inside, 1, 0)
    pl.semaphore_wait(barrier, greeted)

    def hub_copies(src, dst, base):
        return [
            remote(src.at[h], dst.at[t], hub_s.at[base, h], hub_r.at[base], h * (T - 1))
            for h in range(2)
        ]

    def start_to_hubs(copies):
        for h in range(2):
            @pl.when(t != h * (T - 1))
            def _():
                copies[h].start()

    def finish_to_hubs(copies):
        for h in range(2):
            @pl.when(t != h * (T - 1))
            def _():
                copies[h].wait_send()

    def wait_at_hub(dst, base):
        others = dst.at[pl.ds(0, T - 1)]
        pltpu.make_async_copy(others, others, hub_r.at[base]).wait()

    def send_all(q, qr, base):
        def send(there):
            remote(q.at[there], qr.at[hub], sc_s.at[base], sc_r.at[base, hub], there).start()

        each_tile(send)
        qr[hub] = q[t]

    def wait_all(q, qr, base, places):
        for h, place in enumerate(places):
            @pl.when(t != place)
            def _():
                remote(q.at[0], qr.at[h], sc_s.at[base], sc_r.at[base, h], place).wait_recv()

    to_hubs_a = hub_copies(pa, pall_a, 0)
    start_to_hubs(to_hubs_a)

    @pl.when(is_hub)
    def _():
        send_all(qw, qr_w, 0)

    @pl.when(is_second)
    def _():
        send_all(qs, qr_s, 1)

    strip_copies = []
    middle = (mirror, t >= 0, inner)
    for i, (there, other, inside) in enumerate((beside[0], middle, beside[1])):
        strip_copies.append(remote(pw, pw_mir.at[i], strip_s.at[i], strip_r.at[i], there))

        @pl.when(other & inside)
        def _():
            strip_copies[i].start()

    ring_a, ring_mid = [
        [
            remote(
                halo_s.at[side, part], wh.at[1 - side, part],
                ring_s.at[2 * part + side], ring_r.at[2 * part + side], (prev, nxt)[side],
            )
            for side in range(2)
        ]
        for part in range(2)
    ]
    for copy in ring_a:
        copy.start()

    for copy in loads[5:]:
        copy.wait()
    lane = iota((LANES, LANES), 1)
    blocks = {}
    for b in range(NB):
        wide = taper(jnp.transpose(band_cols[:, b * LANES : (b + 1) * LANES]))
        wide = jnp.concatenate([wide, jnp.zeros((LANES, LANES), f32)], axis=1)
        wide = pltpu.roll(wide, 0, 1, stride=1, stride_axis=0)
        wide = pltpu.roll(wide, WIDE - HALF, 1)
        over = wide[:, LANES:]
        for c, value in (
            (b, wide[:, :LANES]),
            ((b + 1) % (NB + 1), jnp.where(lane < HALF, over, 0.0)),
            ((b + NB) % (NB + 1), jnp.where(lane >= LANES - HALF, over, 0.0)),
        ):
            blocks[b, c] = blocks[b, c] + value if (b, c) in blocks else value
    from_lane, to_lane = iota((LANES, LANES), 0), iota((LANES, LANES), 1) & 31
    rim_order = onehot(
        ((to_lane < HALF) & (from_lane == LANES - 1 - to_lane))
        | ((to_lane >= HALF) & (to_lane < 2 * HALF) & (from_lane == to_lane - HALF))
    )
    for b in range(NB):
        for c in range(NB + 1):
            value = blocks.get((b, c))
            value = jnp.zeros((LANES, LANES), bf16) if value is None else value.astype(bf16)
            if c == NB:
                value = dot(value, rim_order).astype(bf16)
            dmat[b * LANES : (b + 1) * LANES, c * LANES : (c + 1) * LANES] = value

    def skewed(taps, first):
        wide = jnp.concatenate([taps, jnp.zeros((ROWS, LANES), f32)], axis=1)
        wide = pltpu.roll(wide, first, 1, stride=1, stride_axis=0)
        return wide[:, :LANES].astype(bf16)

    skew = skewed(own_taps, ROWS - HALF)
    every = jnp.concatenate([skew] * (M * FACES), axis=0)
    tap_at, dst_at = iota((LANES, WIDE), 0), iota((LANES, WIDE), 1)
    row_at, col_at = iota((MR, WIDE), 0) >> 4, iota((MR, WIDE), 1)
    half_at = (dst_at * 171) >> 11
    step_at = dst_at - half_at * HALF

    def banded(expand, same):
        full = jnp.where(same, dot(every, onehot(expand)), 0.0)
        square = jnp.concatenate([full, jnp.zeros((WIDE - MR, WIDE), f32)], axis=0)
        return full, jnp.transpose(square)

    full, turned = banded(tap_at == ROWS + (dst_at & 15), row_at == col_at >> 4)
    bd[...] = full[:, :MR].astype(bf16)
    bdt[...] = turned[:MR, :MR].astype(bf16)
    for side, first in ((0, ROWS - HALF), (1, 2 * ROWS)):
        full, turned = banded(
            (tap_at == first + step_at) & (dst_at < MH), row_at == (col_at * 171) >> 11
        )
        bdh[side] = full[:, :MH].astype(bf16)
        bdht[side] = turned[:MH, :MR].astype(bf16)

    want_face, want_edge, want_layer, want_good = col_parts(iota((WIDE, WIDE), 1))
    want_code = jnp.where(
        want_edge == 2,
        pick_face(want_face, [peers[f][2] for f in range(FACES)]),
        pick_face(want_face, [peers[f][3] for f in range(FACES)]),
    )
    want_turn = jnp.where(
        want_edge == 2,
        pick_face(want_face, [flips[f][2] for f in range(FACES)]),
        pick_face(want_face, [flips[f][3] for f in range(FACES)]),
    )
    want = make_key(0, want_code, want_layer, want_good, -2)
    src_hub, row_face, row_layer, row_good = hub_parts(iota((WIDE, WIDE), 0))
    src_rows = make_key(0, 4 * row_face + src_hub, row_layer, row_good, -1)
    gmat[0] = onehot((src_cols == want) & (want_turn == 0))
    gmat[1] = onehot(src_rows == want)
    gmat[2] = onehot((src_cols == want) & (want_turn == 1))
    back = onehot(iota((ROWS, ROWS), 0) + iota((ROWS, ROWS), 1) == ROWS - 1)

    def hub_picks(slot, shape, parts, layer_of, cols, rows):
        def wanted(width):
            index = iota((2 * shape, width), 0)
            turned = index >= shape
            member, face, at = parts(jnp.where(turned, index - shape, index))
            layer = layer_of(at)
            good = (layer < HALF) & ((pick_face(face, hub_flips) == 1) == turned)
            return member, face, layer, good

        if cols:
            member, face, layer, good = wanted(WIDE)
            src_m, src_f, src_k, src_ok = hub_parts(iota((2 * shape, WIDE), 1))
            picks[slot, : 2 * shape] = onehot(
                make_key(member, face, layer, good, -2) == make_key(src_m, src_f, src_k, src_ok, -1)
            )
            slot += 1
        for width, source_parts, source_layer, source_edge in rows:
            member, face, layer, good = wanted(width)
            code = pick_face(face, hub_peers)
            src_m, src_f, src_at = source_parts(iota((2 * shape, width), 1))
            src_k = source_layer(src_at)
            picks[slot, : 2 * shape, :width] = onehot(
                make_key(member, code, layer, good, -2)
                == make_key(src_m, 4 * src_f + source_edge, src_k, src_k < HALF, -1)
            )
            slot += 1

    def gather_rows(slot, shape, cols, rows):
        total = None
        if cols is not None:
            total = dot_nt(picks[slot, : 2 * shape], cols)
            slot += 1
        for source in rows:
            value = dot(picks[slot, : 2 * shape, : source.shape[0]], source)
            total = value if total is None else total + value
            slot += 1
        return total[:shape] + flipped(total[shape:])

    def finish_scatter(q, base):
        others = q.at[pl.ds(0, T - 1)]
        pltpu.make_async_copy(others, others, sc_s.at[base]).wait()

    def arrive_cols(direct, mirrored, qr):
        packs = []
        for m in range(M):
            value = jnp.zeros((ROWS, WIDE), f32)
            if direct is not None:
                value = value + dot(direct[m], gmat[0])
                value = value + dot(back, dot(mirrored[m], gmat[2]).astype(bf16))
            if qr is not None:
                near = [qr[h, :, m * LANES : (m + 1) * LANES] for h in range(2)]
                value = value + dot(jnp.concatenate(near, axis=1), gmat[1])
            packs.append(value)
        return packs

    halo_near, halo_far = by_hub(forward, back_halo), by_hub(back_halo, forward)
    edge_rows = by_hub(forward, back_row)

    @pl.when(is_hub)
    def _():
        rows = ((MR, row_parts, edge_rows, hub), (MH, halo_parts, halo_far, 1 - hub))
        hub_picks(0, MH, halo_parts, halo_far, True, rows)
        hub_picks(3, MR, row_parts, edge_rows, True, ())
        rows = ((MH, halo_parts, halo_far, hub), (MH, halo_parts, halo_near, 1 - hub))
        hub_picks(4, MH, halo_parts, halo_near, False, rows)

    edge_shape = (WIDE + LANES + WIDE, WIDE)
    index = iota(edge_shape, 0)
    part_w, part_s = index < WIDE, index < WIDE + LANES
    low = jnp.where(part_w, index, index - WIDE)
    arr_m, arr_f, arr_k, arr_ok = hub_parts(index - WIDE - LANES)
    half_w, half_s = jnp.where(low >= 96, 1, 0), jnp.where(low >= 48, 1, 0)
    rest_w, rest_s = low - 96 * half_w, low - 48 * half_s
    src_mf = jnp.where(
        part_w,
        jnp.where(low < 192, FACES * half_w + (rest_w >> 4), -1),
        jnp.where(
            part_s,
            jnp.where(low < 96, FACES * half_s + (rest_s >> 3), -1),
            jnp.where(arr_ok, FACES * arr_m + arr_f, -1),
        ),
    )
    place = jnp.where(
        part_w,
        HALF + (rest_w & 15),
        jnp.where(part_s, HALF + ROWS + (rest_s & 7), HALF - 1 - arr_k),
    )
    dst_m, dst_f, dst_k, dst_ok = hub_parts(iota(edge_shape, 1))
    same = src_mf == jnp.where(dst_ok, FACES * dst_m + dst_f, -2)
    seam_mask[...] = jnp.where(same, 1.0, 0.0)
    from_place[...] = onehot(place[:, :LANES] == iota((edge_shape[0], LANES), 1))
    layer_lane = iota((ROWS, WIDE), 1) & 15
    to_layer = onehot((iota((ROWS, WIDE), 0) == layer_lane) & (layer_lane < HALF))
    turn_taps = onehot(
        (iota((LANES, LANES), 0) + iota((LANES, LANES), 1) == 2 * HALF)
    )

    wait_all(qw, qr_w, 0, (0, T - 1))
    wait_all(qs, qr_s, 1, (1, T - 2))

    def sent_taps(block):
        taps = pltpu.roll(block.astype(f32), LANES // 2, 1)
        return jnp.where(iota((ROWS, LANES), 1) <= 2 * HALF, taps, 0.0)

    for h in range(2):
        taps = sent_taps(qr_w[h, :, LANES:])
        if h == 1:
            taps = dot(dot(back, taps.astype(bf16)).astype(bf16), turn_taps)
        by_layer = dot_nt(from_place[...], skewed(taps, 0)).astype(bf16)
        seam[h] = (dot(by_layer, to_layer) * seam_mask[...]).astype(bf16)
        line = jnp.concatenate([qr_w[h], qr_s[h], pa[h]], axis=1)
        qr_b[h] = dot(line, seam[h]).astype(bf16)

    @pl.when(inner)
    def _():
        for i, (there, other, inside) in enumerate((beside[0], middle, beside[1])):
            @pl.when(other)
            def _():
                strip_copies[i].wait_recv()

            if i != 1:
                @pl.when(jnp.logical_not(other))
                def _():
                    pw_mir[i] = pw[...]

        mirror_skew = skewed(sent_taps(pw_mir[1, 0, :, LANES:]), ROWS - HALF)
        for m in range(M):
            rows = jnp.concatenate([pw_mir[0, m], pw_mir[1, m], pw_mir[2, m]], axis=0)
            pb_mir[m] = dot(mirror_skew[:, : 3 * ROWS], rows).astype(bf16)

    x = dot(bd[...], w[...])
    for copy in ring_a:
        copy.wait_recv()
    for copy in ring_mid:
        copy.start()
    side_tiles = LANES // ROWS

    @pl.when(is_hub)
    def _():
        pall_a[t] = pa[hub]
        wait_at_hub(pall_a, 0)
        near = jnp.concatenate([pall_a[:side_tiles], pall_a[T - side_tiles :]], axis=0)
        wh[hub, 0] = gather_rows(
            0, MH, near.reshape(WIDE, WIDE), (end_blocks(w[...]), wh[hub, 0])
        ).astype(bf16)

    x_ends = (end_blocks(x) + dot(bdh[0], wh[0, 0]) + dot(bdh[1], wh[1, 0])).astype(bf16)
    xs[:, :LANES] = x_ends[:, :LANES]
    xs[:, N - LANES : N] = x_ends[:, LANES:]

    for m, value in enumerate(pack_ends(xs[:, :N])):
        pb[m] = value
    mirror_b = remote(pb, pb_mir, mir_s.at[0], mir_r.at[0], mirror)

    def to_strips(member, face, at):
        return jnp.where(at < HALF, LANES * member + 16 * face + at, -1)

    @pl.when(is_hub)
    def _():
        mirror_b.start()
        mirror_b.wait_recv()

    xs[:, N:] = spread(arrive_cols(pb, pb_mir, qr_b))

    zrim = jnp.zeros((MR, LANES), f32)
    for at in (0, N - LANES):
        here = slice(at, at + LANES)
        value = jnp.concatenate([xs[:, here], xs[:, N:]], axis=1)
        weights = jnp.concatenate([dmat[here, here], dmat[here, N:]], axis=1)
        zrim = zrim + dot(dot_nt(value, weights).astype(bf16), dmat[here, N:])
    rims = pack(zrim)
    for m, value in enumerate(rims):
        pc[m] = value
    mirror_c = remote(pc, pc_mir, mir_s.at[1], mir_r.at[1], mirror)
    hub_messages(rims, pa_c)
    to_hubs_c = hub_copies(pa_c, pall_c, 1)
    start_to_hubs(to_hubs_c)
    mirror_c.start()

    for copy in ring_mid:
        copy.wait_recv()

    @pl.when(is_hub)
    def _():
        middle_cols = pall_a[side_tiles : T - side_tiles].reshape(N - WIDE, WIDE)
        wh[hub, 1] = gather_rows(
            0, MH, middle_cols, (w[:, LANES : N - LANES], wh[hub, 1])
        ).astype(bf16)

    x_mid = x[:, LANES : N - LANES] + dot(bdh[0], wh[0, 1]) + dot(bdh[1], wh[1, 1])
    xs[:, LANES : N - LANES] = x_mid.astype(bf16)
    y = dot_nt(xs[...], dmat[...]).astype(bf16)
    zacc[...] = dot(y, dmat[:, :N])

    def end_columns(flat, width):
        at, end = iota((WIDE, 2 * width), 0), iota((WIDE, 2 * width), 1)
        pick = onehot(at == jnp.where(end < width, end, end + WIDE - 2 * width))
        both = iota((2 * width, 2 * width), 0) + iota((2 * width, 2 * width), 1)
        near = jnp.concatenate([flat[:, :LANES], flat[:, N - LANES :]], axis=1)
        near = dot(near, pick).astype(bf16)
        return near, dot(near, onehot(both == 2 * width - 1)).astype(bf16)

    def near_strips(flat, width, parts, layer_of, lanes_of):
        near, far = end_columns(flat, width)
        shape = (flat.shape[0], WIDE)
        member, face, at = parts(iota(shape, 0))
        here = lanes_of(member, face, layer_of(at)) == iota(shape, 1)
        turned = pick_face(face, hub_flips) == 1
        value = dot_tn(near, onehot(here & jnp.logical_not(turned)))
        value = value + dot_tn(far, onehot(here & turned))
        return value.astype(bf16).reshape(2 * width // ROWS, ROWS, WIDE)

    @pl.when(is_hub)
    def _():
        value = turn_rows(zacc[...].astype(bf16), to_strips)
        qc[...] = value.astype(bf16).reshape(T, ROWS, WIDE)

        def send(there):
            @pl.when((there > 0) & (there < T - 1))
            def _():
                remote(qc.at[there], qr_c.at[hub], sc_s.at[2], sc_r.at[2, hub], there).start()

        each_tile(send)

    ring_d = [
        remote(sp.at[0], drh.at[1], ring_s.at[4], ring_r.at[4], prev),
        remote(sp.at[1], drh.at[0], ring_s.at[5], ring_r.at[5], nxt),
    ]
    ring_late = [
        remote(late.at[0], late_r.at[1], ring_s.at[6], ring_r.at[6], prev),
        remote(late.at[1], late_r.at[0], ring_s.at[7], ring_r.at[7], nxt),
    ]

    def start_spills(value):
        for side in range(2):
            sp[side] = dot(bdht[side], value).astype(bf16)
            ring_d[side].start()

    @pl.when(inner)
    def _():
        start_spills(zacc[...].astype(bf16))

    mirror_c.wait_recv()

    @pl.when(is_hub)
    def _():
        pall_c[t] = pa_c[hub]
        wait_at_hub(pall_c, 1)
        zacc[...] += gather_rows(3, MR, pall_c[...].reshape(N, WIDE), ())

    ends = dot_nt(spread(arrive_cols(pc, pc_mir, None)), sel)
    zacc[:, :LANES] += ends[:, :LANES]
    zacc[:, N - LANES :] += ends[:, LANES:]

    z = zacc[...].astype(bf16)
    quarter = iota((MH, LANES), 1) >> 5

    def both_ends(value):
        return dot(jnp.concatenate([value[:, :LANES], value[:, N - LANES :]], axis=1), sel)

    @pl.when(is_hub)
    def _():
        start_spills(z)

    z_ends = both_ends(z).astype(bf16)
    for side in range(2):
        value = dot(bdht[side], z_ends)
        late[side] = jnp.where(quarter == 1 - side, value, 0.0).astype(bf16)
        ring_late[side].start()

    hub_d = remote(qd.at[1 - hub], qr_d.at[hub], sc_s.at[3], sc_r.at[3, hub], mirror)

    @pl.when(is_hub)
    def _():
        qd[...] = near_strips(
            sp[hub], ROWS, halo_parts, by_hub(back_halo, forward),
            lambda member, face, at: LANES * member + 16 * face + at,
        )
        qr_d[hub] = qd[hub]
        hub_d.start()

    zacc[...] = dot(bdt[...], z)

    @pl.when(inner)
    def _():
        wait_all(qc, qr_c, 2, (0, T - 1))
        for h in range(2):
            strip = (qr_c[h].astype(f32) + pa_c[h].astype(f32)).astype(bf16)
            qr_d[h] = dot_nt(strip, seam[h, WIDE + LANES :, :]).astype(bf16)

    for copy in ring_d + ring_late:
        copy.wait_recv()

    @pl.when(is_hub)
    def _():
        arrived = gather_rows(4, MH, None, (sp[hub], drh[hub])).astype(bf16)
        drh[hub] = arrived
        late_r[hub] = jnp.where(quarter == hub, both_ends(arrived), 0.0).astype(bf16)

    spill = dot_tn(comp[0], drh[0]) + dot_tn(comp[1], drh[1])
    column = iota((MR, N), 1)
    zacc[...] += jnp.where((column >= HALF) & (column < N - HALF), spill, 0.0)
    spill_ends = dot_tn(comp[0], late_r[0]) + dot_tn(comp[1], late_r[1])
    ends = dot_nt(spill_ends.astype(bf16), sel)
    zacc[:, :LANES] += ends[:, :LANES]
    zacc[:, N - LANES :] += ends[:, LANES:]
    @pl.when(is_hub)
    def _():
        remote(qd.at[0], qr_d.at[1 - hub], sc_s.at[3], sc_r.at[3, 1 - hub], mirror).wait_recv()

    ends = dot_nt(spread(arrive_cols(None, None, qr_d)), sel)
    zacc[:, :LANES] += ends[:, :LANES]
    zacc[:, N - LANES :] += ends[:, LANES:]

    FR = FACES * ROWS
    total = jnp.zeros((FR, N), f32)
    for m in range(M):
        total = total + pert[m].astype(f32).reshape(FR, N) * zacc[m * FR : (m + 1) * FR, :]
    per_chunk = part.shape[1]
    for u in range(count * per_chunk):
        r, c = u // NB, u % NB
        part[u // per_chunk, u % per_chunk] = total[r * 8 : r * 8 + 8, c * LANES : (c + 1) * LANES]

    order = [12, 13, 14, 15, 10, 11, 8, 9, 4, 5, 6, 7, 2, 3, 1] if count == 16 else range(1, count)
    peers_of_me = [me ^ i for i in order]
    for there in peers_of_me:
        remote(part.at[there], got.at[me], mem_s.at[0], mem_r.at[0], there, "member").start()
    got[me] = part[me]
    others = got.at[pl.ds(0, count - 1)]
    pltpu.make_async_copy(others, others, mem_r.at[0]).wait()
    chunk = got[0]
    for i in range(1, count):
        chunk = chunk + got[i]
    mine[...] = chunk * (1.0 / (M * count - 1.0))
    for there in peers_of_me:
        remote(mine, done.at[me], mem_s.at[1], mem_r.at[1], there, "member").start()
    done[me] = mine[...]
    finished = done.at[pl.ds(0, count - 1)]
    pltpu.make_async_copy(finished, finished, mem_r.at[1]).wait()
    for u in range(count * per_chunk):
        r, c = u // NB, u % NB
        out[r * 8 : r * 8 + 8, c * LANES : (c + 1) * LANES] = done[u // per_chunk, u % per_chunk]

    for copy in ring_a + ring_mid + ring_d + ring_late + [mirror_c]:
        copy.wait_send()
    for i, (there, other, inside) in enumerate((beside[0], middle, beside[1])):
        @pl.when(other & inside)
        def _():
            strip_copies[i].wait_send()

    finish_to_hubs(to_hubs_a)
    finish_to_hubs(to_hubs_c)

    @pl.when(is_hub)
    def _():
        finish_scatter(qw, 0)
        far = qc.at[pl.ds(0, T - 2)]
        pltpu.make_async_copy(far, far, sc_s.at[2]).wait()
        mirror_b.wait_send()
        hub_d.wait_send()

    @pl.when(is_second)
    def _():
        finish_scatter(qs, 1)

    for i in range(2):
        pltpu.make_async_copy(others, others, mem_s.at[i]).wait()


def per_device(perturbations, control, band_rows, band_cols, edge_peer, edge_flip):
    T, count = lax.axis_size("tile"), lax.axis_size("member")
    M = perturbations.shape[0]
    N = control.shape[-1]
    MR, MH = M * FACES * ROWS, M * FACES * HALF
    per_chunk = FACES * ROWS * N // (8 * LANES) // count
    vmem, hbm = pl.BlockSpec(memory_space=pltpu.VMEM), pl.BlockSpec(memory_space=pltpu.HBM)
    dma = pltpu.SemaphoreType.DMA
    args = (perturbations, control, band_rows, band_cols.T, edge_peer.T, edge_flip.T)
    result = pl.pallas_call(
        functools.partial(whole_kernel, T, M, count),
        out_shape=jax.ShapeDtypeStruct((FACES * ROWS, N), f32),
        in_specs=[hbm] * 6,
        out_specs=vmem,
        scratch_shapes=[
            pltpu.VMEM(args[0].shape, bf16),
            pltpu.VMEM(args[1].shape, f32),
            pltpu.VMEM(args[2].shape, f32),
            pltpu.VMEM(args[3].shape, f32),
            pltpu.SMEM(args[4].shape, i32),
            pltpu.SMEM(args[5].shape, i32),
            pltpu.VMEM((MR, N), bf16),
            pltpu.VMEM((2, 2, MH, WIDE), bf16),
            pltpu.VMEM((2, 2, MH, WIDE), bf16),
            pltpu.VMEM((2, ROWS, WIDE), bf16),
            pltpu.VMEM((T, ROWS, WIDE), bf16),
            pltpu.VMEM((M, ROWS, WIDE), bf16),
            pltpu.VMEM((3, M, ROWS, WIDE), bf16),
            pltpu.VMEM((T, ROWS, WIDE), bf16),
            pltpu.VMEM((2, ROWS, WIDE), bf16),
            pltpu.VMEM((T, ROWS, LANES), bf16),
            pltpu.VMEM((2, ROWS, LANES), bf16),
            pltpu.VMEM((M, ROWS, WIDE), bf16),
            pltpu.VMEM((M, ROWS, WIDE), bf16),
            pltpu.VMEM((2, ROWS, WIDE), bf16),
            pltpu.VMEM((M, ROWS, WIDE), bf16),
            pltpu.VMEM((M, ROWS, WIDE), bf16),
            pltpu.VMEM((2, ROWS, WIDE), bf16),
            pltpu.VMEM((T, ROWS, WIDE), bf16),
            pltpu.VMEM((T, ROWS, WIDE), bf16),
            pltpu.VMEM((2, ROWS, WIDE), bf16),
            pltpu.VMEM((2, MH, N), bf16),
            pltpu.VMEM((2, MH, N), bf16),
            pltpu.VMEM((2, MH, LANES), bf16),
            pltpu.VMEM((2, MH, LANES), bf16),
            pltpu.VMEM((2, ROWS, WIDE), bf16),
            pltpu.VMEM((2, ROWS, WIDE), bf16),
            pltpu.VMEM((N, N + LANES), bf16),
            pltpu.VMEM((MR, N + LANES), bf16),
            pltpu.VMEM((MR, N), f32),
            pltpu.VMEM((MR, MR), bf16),
            pltpu.VMEM((2, MR, MH), bf16),
            pltpu.VMEM((MR, MR), bf16),
            pltpu.VMEM((2, MH, MR), bf16),
            pltpu.VMEM((N, N), bf16),
            pltpu.VMEM((3, WIDE, WIDE), bf16),
            pltpu.VMEM((2, 2 * WIDE + LANES, WIDE), bf16),
            pltpu.VMEM((2 * WIDE + LANES, WIDE), f32),
            pltpu.VMEM((2 * WIDE + LANES, LANES), bf16),
            pltpu.VMEM((6, 2 * MR, WIDE), bf16),
            pltpu.VMEM((count, per_chunk, 8, LANES), f32),
            pltpu.VMEM((count, per_chunk, 8, LANES), f32),
            pltpu.VMEM((per_chunk, 8, LANES), f32),
            pltpu.VMEM((count, per_chunk, 8, LANES), f32),
            dma((6,)),
            dma((8,)), dma((8,)),
            dma((2, 2)), dma((2,)),
            dma((2,)), dma((2,)),
            dma((3,)), dma((3,)),
            dma((6,)), dma((4, 2)),
            dma((2,)), dma((2,)),
        ],
        compiler_params=pltpu.CompilerParams(
            collective_id=0, has_side_effects=True, vmem_limit_bytes=60 * 1024 * 1024
        ),
        name="covariance",
    )(*args)
    return result.reshape(control.shape)


def solution(mesh):
    return jax.shard_map(
        per_device,
        mesh=mesh,
        in_specs=(
            P("member", None, "tile", None),
            P(None, "tile", None),
            P("tile", None),
            P(),
            P(),
            P(),
        ),
        out_specs=P(None, "tile", None),
        check_vma=False,
    )
```

```python
import functools
import math

import jax
import jax.numpy as jnp
import numpy as np
from jax import lax
from jax.experimental import pallas as pl
from jax.experimental.pallas import tpu as pltpu
from jax.sharding import PartitionSpec as P

HALF = 12
ROWS = 16
FACES = 6
LANES = 128
WIDE = 2 * LANES
f32, bf16, i32 = jnp.float32, jnp.bfloat16, jnp.int32


def iota(shape, dim):
    return lax.broadcasted_iota(i32, shape, dim)


def dot(a, b):
    return lax.dot_general(a, b, (((1,), (0,)), ((), ())), preferred_element_type=f32)


def dot_nt(a, b):
    return lax.dot_general(a, b, (((1,), (1,)), ((), ())), preferred_element_type=f32)


def dot_tn(a, b):
    return lax.dot_general(a, b, (((0,), (0,)), ((), ())), preferred_element_type=f32)


def onehot(mask):
    return jnp.where(mask, 1.0, 0.0).astype(bf16)


def taper(band):
    rows, taps = band.shape
    steps = np.arange(2 * HALF + 1, dtype=np.float32) - HALF
    curve = np.exp(-((steps / HALF) ** 2))
    scale = 1.0 / math.sqrt(math.sqrt(float(np.sum(curve * curve))) * float(np.sum(curve)))
    lane = iota((1, taps), 1).astype(f32)
    g = jnp.exp(-(((lane - HALF) / HALF) ** 2)) * scale
    wide = jnp.concatenate([band * g, jnp.zeros((rows, LANES - taps), f32)], axis=1)
    return wide.astype(bf16).astype(f32)


def make_key(member, code, layer, good, other):
    return jnp.where(good, ((member * 24 + code) << 4) + layer, other)


def col_parts(lane):
    face, rest = lane >> 5, lane & 31
    second = rest >= HALF
    layer = jnp.where(second, rest - HALF, rest)
    return face, jnp.where(second, 3, 2), layer, (rest < 2 * HALF) & (face < FACES)


def hub_parts(lane):
    face, layer = (lane & (LANES - 1)) >> 4, lane & 15
    return lane >> 7, face, layer, (face < FACES) & (layer < HALF)


def row_parts(index):
    both = index >> 4
    member = jnp.where(both >= FACES, 1, 0)
    return member, both - FACES * member, index & 15


def halo_parts(index):
    both = (index * 171) >> 11
    member = jnp.where(both >= FACES, 1, 0)
    return member, both - FACES * member, index - both * HALF


def pick_face(face, values):
    out = jnp.zeros(face.shape, i32)
    for f in range(FACES):
        out = jnp.where(face == f, values[f], out)
    return out


def whole_kernel(
    tiles, members, count,
    pert_in, control_in, rows_in, cols_in, peer_in, flip_in, out,
    pert, control, band_rows, band_cols, peer, flip,
    w, wh, halo_s, pa, pall_a, pw, pw_mir, qw, qr_w, qs, qr_s, pb, pb_mir, qr_b,
    pc, pc_mir, pa_c, pall_c, qc, qr_c, sp, drh, late, late_r, qd, qr_d,
    dmat, xs, zacc, bd, bdh, bdt, bdht, jn, gmat, seam, seam_mask, from_place, picks, part, got, mine, done,
    load, ring_s, ring_r, hub_s, hub_r, mir_s, mir_r, strip_s, strip_r, sc_s, sc_r, mem_s, mem_r,
):
    T, M = tiles, members
    N = ROWS * T
    NB = N // LANES
    MR, MH = M * FACES * ROWS, M * FACES * HALF
    t, me = lax.axis_index("tile"), lax.axis_index("member")
    prev, nxt, mirror = lax.rem(t + T - 1, T), lax.rem(t + 1, T), T - 1 - t
    hub = jnp.where(t >= T // 2, 1, 0)
    is_hub = (t == 0) | (t == T - 1)
    is_second = (t == 1) | (t == T - 2)
    inner = jnp.logical_not(is_hub)
    last = hub == 1

    def remote(src, dst, send, recv, where, axis="tile"):
        return pltpu.make_async_remote_copy(
            src_ref=src, dst_ref=dst, send_sem=send, recv_sem=recv,
            device_id={axis: where}, device_id_type=pl.DeviceIdType.MESH,
        )

    def each_tile(act):
        act(lax.rem(t + T // 2, T))

        def body(d, carry):
            act(lax.rem(t + T // 2 + d, T))
            act(lax.rem(t + T // 2 - d, T))
            return carry

        lax.fori_loop(1, T // 2, body, 0)

    barrier = pltpu.get_barrier_semaphore()

    def greet(where, axis="tile"):
        pl.semaphore_signal(
            barrier, inc=1, device_id={axis: where}, device_id_type=pl.DeviceIdType.MESH
        )

    @pl.when(is_hub)
    def _():
        each_tile(greet)

    @pl.when(jnp.logical_not(is_hub))
    def _():
        greet(0)
        greet(T - 1)

    for where in (mirror, prev, nxt):
        greet(where)
    for second in (1, T - 2):
        @pl.when(t != second)
        def _():
            greet(second)

    beside = []
    for step in (-1, 1):
        there = mirror + step
        beside.append((jnp.clip(there, 0, T - 1), there != t, (there >= 1) & (there <= T - 2)))

        @pl.when(inner & (there != t))
        def _():
            greet(there)
    for i in range(1, count):
        greet(lax.rem(me + i, count), "member")

    loads = [
        pltpu.make_async_copy(src, dst, load.at[i])
        for i, (src, dst) in enumerate(
            (
                (pert_in, pert), (control_in, control), (peer_in, peer), (flip_in, flip),
                (rows_in, band_rows), (cols_in, band_cols),
            )
        )
    ]
    for copy in loads:
        copy.start()

    r256, c128 = iota((WIDE, LANES), 0), iota((WIDE, LANES), 1) & 31
    sel = onehot(
        ((r256 < HALF) & (c128 == r256))
        | ((r256 >= WIDE - HALF) & (c128 == HALF + WIDE - 1 - r256))
    )
    group = iota((ROWS, LANES), 1) >> 5
    s0, s1 = iota((MH, MR), 0), iota((MH, MR), 1)
    half_of_row = (s0 * 171) >> 11
    ahead = s1 - (half_of_row << 4) - (s0 - half_of_row * HALF)
    comp = [onehot(ahead == 0), onehot(ahead == ROWS - HALF)]

    def pack(quad):
        packs = []
        for m in range(M):
            blocks = []
            for g in range(2):
                block = jnp.zeros((ROWS, LANES), f32)
                for q in range(4):
                    f = 4 * g + q
                    if f < FACES:
                        at = (m * FACES + f) * ROWS
                        block = jnp.where(group == q, quad[at : at + ROWS], block)
                blocks.append(block)
            packs.append(jnp.concatenate(blocks, axis=1).astype(bf16))
        return packs

    def pack_ends(flat):
        ends = jnp.concatenate([flat[:, :LANES], flat[:, N - LANES :]], axis=1)
        return pack(dot(ends, sel))

    def spread(packs):
        parts = []
        for m in range(M):
            for f in range(FACES):
                g, q = f // 4, f % 4
                block = packs[m][:, g * LANES : (g + 1) * LANES]
                parts.append(jnp.where(group == q, block, 0.0))
        return jnp.concatenate(parts, axis=0).astype(bf16)

    for copy in loads[:5]:
        copy.wait()
    for m in range(M):
        weighted = (pert[m].astype(f32) * control[...]).astype(bf16)
        w[m * FACES * ROWS : (m + 1) * FACES * ROWS, :] = weighted.reshape(FACES * ROWS, N)

    peers = [[peer[e, f] for e in range(4)] for f in range(FACES)]
    flips = [[flip[e, f] for e in range(4)] for f in range(FACES)]
    src_face, src_edge, src_layer, src_good = col_parts(iota((WIDE, WIDE), 0))
    src_cols = make_key(0, 4 * src_face + src_edge, src_layer, src_good, -1)
    lane = iota((WIDE, WIDE), 1)
    _, hub_face, hub_layer, hub_good = hub_parts(lane)
    to_hub = jnp.where(
        lane < LANES,
        pick_face(hub_face, [peers[f][0] for f in range(FACES)]),
        pick_face(hub_face, [peers[f][1] for f in range(FACES)]),
    )
    hub_pick = onehot(src_cols == make_key(0, to_hub, hub_layer, hub_good, -2))

    def hub_messages(packs, dst):
        chosen = [dot(value, hub_pick).astype(bf16) for value in packs]
        for h in range(2):
            for m in range(M):
                dst[h, :, m * LANES : (m + 1) * LANES] = chosen[m][:, h * LANES : (h + 1) * LANES]

    own_taps = taper(band_rows[...])
    strips = pack_ends(w[...])
    hub_messages(strips, pa)
    for m, value in enumerate(strips):
        pw[m] = value
    pw[0, :, LANES:] += pltpu.roll(own_taps, LANES // 2, 1).astype(bf16)

    def end_blocks(flat):
        return jnp.concatenate([flat[:, :LANES], flat[:, N - LANES :]], axis=1)

    for side in range(2):
        rows = dot(comp[side], w[...]).astype(bf16)
        halo_s[side, 0] = end_blocks(rows)
        halo_s[side, 1] = rows[:, LANES : N - LANES]

    hub_peers = [jnp.where(last, peers[f][1], peers[f][0]) for f in range(FACES)]
    hub_flips = [jnp.where(last, flips[f][1], flips[f][0]) for f in range(FACES)]

    def flipped(value):
        width = value.shape[1]
        return dot(value.astype(bf16), jn[:width, N - width :])

    def by_hub(first, second):
        return lambda at: jnp.where(last, second(at), first(at))

    def forward(at):
        return at

    def back_row(at):
        return ROWS - 1 - at

    def back_halo(at):
        return HALF - 1 - at

    def turn_rows(flat, lanes_of):
        shape = (flat.shape[0], WIDE)
        member, face, at = row_parts(iota(shape, 0))
        here = lanes_of(member, face, by_hub(forward, back_row)(at)) == iota(shape, 1)
        turned = pick_face(face, hub_flips) == 1
        value = dot_tn(flat, onehot(here & jnp.logical_not(turned)))
        return value + dot_tn(flipped(flat).astype(bf16), onehot(here & turned))

    @pl.when(is_hub | is_second)
    def _():
        jn[...] = onehot(iota((N, N), 0) + iota((N, N), 1) == N - 1)

    @pl.when(is_hub)
    def _():
        value = turn_rows(w[...], lambda member, face, at: 96 * member + 16 * face + at)
        low, high = value[:, :LANES].astype(bf16), value[:, LANES:].astype(bf16)
        extra = pltpu.roll(own_taps, LANES // 2, 1).astype(bf16)
        qw[:, :, :LANES] = low.reshape(T, ROWS, LANES)
        qw[:, :, LANES:] = high.reshape(T, ROWS, LANES) + extra[None]

    @pl.when(is_second)
    def _():
        value = turn_rows(
            w[...],
            lambda member, face, at: jnp.where(at < 8, 48 * member + 8 * face + at, -1),
        )
        qs[...] = value[:, :LANES].astype(bf16).reshape(T, ROWS, LANES)

    greeted = 3 + count - 1 + jnp.where(is_hub, T - 1, 2) + jnp.where(is_second, T - 1, 0)
    for _, other, inside in beside:
        greeted = greeted + jnp.where(other & inside, 1, 0)
    pl.semaphore_wait(barrier, greeted)

    def hub_copies(src, dst, base):
        return [
            remote(src.at[h], dst.at[t], hub_s.at[base, h], hub_r.at[base], h * (T - 1))
            for h in range(2)
        ]

    def start_to_hubs(copies):
        for h in range(2):
            @pl.when(t != h * (T - 1))
            def _():
                copies[h].start()

    def finish_to_hubs(copies):
        for h in range(2):
            @pl.when(t != h * (T - 1))
            def _():
                copies[h].wait_send()

    def wait_at_hub(dst, base):
        others = dst.at[pl.ds(0, T - 1)]
        pltpu.make_async_copy(others, others, hub_r.at[base]).wait()

    def send_all(q, qr, base):
        def send(there):
            remote(q.at[there], qr.at[hub], sc_s.at[base], sc_r.at[base, hub], there).start()

        each_tile(send)
        qr[hub] = q[t]

    def wait_all(q, qr, base, places):
        for h, place in enumerate(places):
            @pl.when(t != place)
            def _():
                remote(q.at[0], qr.at[h], sc_s.at[base], sc_r.at[base, h], place).wait_recv()

    to_hubs_a = hub_copies(pa, pall_a, 0)
    start_to_hubs(to_hubs_a)

    @pl.when(is_hub)
    def _():
        send_all(qw, qr_w, 0)

    @pl.when(is_second)
    def _():
        send_all(qs, qr_s, 1)

    strip_copies = []
    middle = (mirror, t >= 0, inner)
    for i, (there, other, inside) in enumerate((beside[0], middle, beside[1])):
        strip_copies.append(remote(pw, pw_mir.at[i], strip_s.at[i], strip_r.at[i], there))

        @pl.when(other & inside)
        def _():
            strip_copies[i].start()

    ring_a, ring_mid = [
        [
            remote(
                halo_s.at[side, part], wh.at[1 - side, part],
                ring_s.at[2 * part + side], ring_r.at[2 * part + side], (prev, nxt)[side],
            )
            for side in range(2)
        ]
        for part in range(2)
    ]
    for copy in ring_a:
        copy.start()

    for copy in loads[5:]:
        copy.wait()
    lane = iota((LANES, LANES), 1)
    blocks = {}
    for b in range(NB):
        wide = taper(jnp.transpose(band_cols[:, b * LANES : (b + 1) * LANES]))
        wide = jnp.concatenate([wide, jnp.zeros((LANES, LANES), f32)], axis=1)
        wide = pltpu.roll(wide, 0, 1, stride=1, stride_axis=0)
        wide = pltpu.roll(wide, WIDE - HALF, 1)
        over = wide[:, LANES:]
        for c, value in (
            (b, wide[:, :LANES]),
            ((b + 1) % (NB + 1), jnp.where(lane < HALF, over, 0.0)),
            ((b + NB) % (NB + 1), jnp.where(lane >= LANES - HALF, over, 0.0)),
        ):
            blocks[b, c] = blocks[b, c] + value if (b, c) in blocks else value
    from_lane, to_lane = iota((LANES, LANES), 0), iota((LANES, LANES), 1) & 31
    rim_order = onehot(
        ((to_lane < HALF) & (from_lane == LANES - 1 - to_lane))
        | ((to_lane >= HALF) & (to_lane < 2 * HALF) & (from_lane == to_lane - HALF))
    )
    for b in range(NB):
        for c in range(NB + 1):
            value = blocks.get((b, c))
            value = jnp.zeros((LANES, LANES), bf16) if value is None else value.astype(bf16)
            if c == NB:
                value = dot(value, rim_order).astype(bf16)
            dmat[b * LANES : (b + 1) * LANES, c * LANES : (c + 1) * LANES] = value

    def skewed(taps, first):
        wide = jnp.concatenate([taps, jnp.zeros((ROWS, LANES), f32)], axis=1)
        wide = pltpu.roll(wide, first, 1, stride=1, stride_axis=0)
        return wide[:, :LANES].astype(bf16)

    skew = skewed(own_taps, ROWS - HALF)
    every = jnp.concatenate([skew] * (M * FACES), axis=0)
    tap_at, dst_at = iota((LANES, WIDE), 0), iota((LANES, WIDE), 1)
    row_at, col_at = iota((MR, WIDE), 0) >> 4, iota((MR, WIDE), 1)
    half_at = (dst_at * 171) >> 11
    step_at = dst_at - half_at * HALF

    def banded(expand, same):
        full = jnp.where(same, dot(every, onehot(expand)), 0.0)
        square = jnp.concatenate([full, jnp.zeros((WIDE - MR, WIDE), f32)], axis=0)
        return full, jnp.transpose(square)

    full, turned = banded(tap_at == ROWS + (dst_at & 15), row_at == col_at >> 4)
    bd[...] = full[:, :MR].astype(bf16)
    bdt[...] = turned[:MR, :MR].astype(bf16)
    for side, first in ((0, ROWS - HALF), (1, 2 * ROWS)):
        full, turned = banded(
            (tap_at == first + step_at) & (dst_at < MH), row_at == (col_at * 171) >> 11
        )
        bdh[side] = full[:, :MH].astype(bf16)
        bdht[side] = turned[:MH, :MR].astype(bf16)

    want_face, want_edge, want_layer, want_good = col_parts(iota((WIDE, WIDE), 1))
    want_code = jnp.where(
        want_edge == 2,
        pick_face(want_face, [peers[f][2] for f in range(FACES)]),
        pick_face(want_face, [peers[f][3] for f in range(FACES)]),
    )
    want_turn = jnp.where(
        want_edge == 2,
        pick_face(want_face, [flips[f][2] for f in range(FACES)]),
        pick_face(want_face, [flips[f][3] for f in range(FACES)]),
    )
    want = make_key(0, want_code, want_layer, want_good, -2)
    src_hub, row_face, row_layer, row_good = hub_parts(iota((WIDE, WIDE), 0))
    src_rows = make_key(0, 4 * row_face + src_hub, row_layer, row_good, -1)
    gmat[0] = onehot((src_cols == want) & (want_turn == 0))
    gmat[1] = onehot(src_rows == want)
    gmat[2] = onehot((src_cols == want) & (want_turn == 1))
    back = onehot(iota((ROWS, ROWS), 0) + iota((ROWS, ROWS), 1) == ROWS - 1)

    def hub_picks(slot, shape, parts, layer_of, cols, rows):
        def wanted(width):
            index = iota((2 * shape, width), 0)
            turned = index >= shape
            member, face, at = parts(jnp.where(turned, index - shape, index))
            layer = layer_of(at)
            good = (layer < HALF) & ((pick_face(face, hub_flips) == 1) == turned)
            return member, face, layer, good

        if cols:
            member, face, layer, good = wanted(WIDE)
            src_m, src_f, src_k, src_ok = hub_parts(iota((2 * shape, WIDE), 1))
            picks[slot, : 2 * shape] = onehot(
                make_key(member, face, layer, good, -2) == make_key(src_m, src_f, src_k, src_ok, -1)
            )
            slot += 1
        for width, source_parts, source_layer, source_edge in rows:
            member, face, layer, good = wanted(width)
            code = pick_face(face, hub_peers)
            src_m, src_f, src_at = source_parts(iota((2 * shape, width), 1))
            src_k = source_layer(src_at)
            picks[slot, : 2 * shape, :width] = onehot(
                make_key(member, code, layer, good, -2)
                == make_key(src_m, 4 * src_f + source_edge, src_k, src_k < HALF, -1)
            )
            slot += 1

    def gather_rows(slot, shape, cols, rows):
        total = None
        if cols is not None:
            total = dot_nt(picks[slot, : 2 * shape], cols)
            slot += 1
        for source in rows:
            value = dot(picks[slot, : 2 * shape, : source.shape[0]], source)
            total = value if total is None else total + value
            slot += 1
        return total[:shape] + flipped(total[shape:])

    def finish_scatter(q, base):
        others = q.at[pl.ds(0, T - 1)]
        pltpu.make_async_copy(others, others, sc_s.at[base]).wait()

    def arrive_cols(direct, mirrored, qr):
        packs = []
        for m in range(M):
            value = jnp.zeros((ROWS, WIDE), f32)
            if direct is not None:
                value = value + dot(direct[m], gmat[0])
                value = value + dot(back, dot(mirrored[m], gmat[2]).astype(bf16))
            if qr is not None:
                near = [qr[h, :, m * LANES : (m + 1) * LANES] for h in range(2)]
                value = value + dot(jnp.concatenate(near, axis=1), gmat[1])
            packs.append(value)
        return packs

    halo_near, halo_far = by_hub(forward, back_halo), by_hub(back_halo, forward)
    edge_rows = by_hub(forward, back_row)

    @pl.when(is_hub)
    def _():
        rows = ((MR, row_parts, edge_rows, hub), (MH, halo_parts, halo_far, 1 - hub))
        hub_picks(0, MH, halo_parts, halo_far, True, rows)
        hub_picks(3, MR, row_parts, edge_rows, True, ())
        rows = ((MH, halo_parts, halo_far, hub), (MH, halo_parts, halo_near, 1 - hub))
        hub_picks(4, MH, halo_parts, halo_near, False, rows)

    edge_shape = (WIDE + LANES + WIDE, WIDE)
    index = iota(edge_shape, 0)
    part_w, part_s = index < WIDE, index < WIDE + LANES
    low = jnp.where(part_w, index, index - WIDE)
    arr_m, arr_f, arr_k, arr_ok = hub_parts(index - WIDE - LANES)
    half_w, half_s = jnp.where(low >= 96, 1, 0), jnp.where(low >= 48, 1, 0)
    rest_w, rest_s = low - 96 * half_w, low - 48 * half_s
    src_mf = jnp.where(
        part_w,
        jnp.where(low < 192, FACES * half_w + (rest_w >> 4), -1),
        jnp.where(
            part_s,
            jnp.where(low < 96, FACES * half_s + (rest_s >> 3), -1),
            jnp.where(arr_ok, FACES * arr_m + arr_f, -1),
        ),
    )
    place = jnp.where(
        part_w,
        HALF + (rest_w & 15),
        jnp.where(part_s, HALF + ROWS + (rest_s & 7), HALF - 1 - arr_k),
    )
    dst_m, dst_f, dst_k, dst_ok = hub_parts(iota(edge_shape, 1))
    same = src_mf == jnp.where(dst_ok, FACES * dst_m + dst_f, -2)
    seam_mask[...] = jnp.where(same, 1.0, 0.0)
    from_place[...] = onehot(place[:, :LANES] == iota((edge_shape[0], LANES), 1))
    layer_lane = iota((ROWS, WIDE), 1) & 15
    to_layer = onehot((iota((ROWS, WIDE), 0) == layer_lane) & (layer_lane < HALF))
    turn_taps = onehot(
        (iota((LANES, LANES), 0) + iota((LANES, LANES), 1) == 2 * HALF)
    )

    wait_all(qw, qr_w, 0, (0, T - 1))
    wait_all(qs, qr_s, 1, (1, T - 2))

    def sent_taps(block):
        taps = pltpu.roll(block.astype(f32), LANES // 2, 1)
        return jnp.where(iota((ROWS, LANES), 1) <= 2 * HALF, taps, 0.0)

    for h in range(2):
        taps = sent_taps(qr_w[h, :, LANES:])
        if h == 1:
            taps = dot(dot(back, taps.astype(bf16)).astype(bf16), turn_taps)
        by_layer = dot_nt(from_place[...], skewed(taps, 0)).astype(bf16)
        seam[h] = (dot(by_layer, to_layer) * seam_mask[...]).astype(bf16)
        line = jnp.concatenate([qr_w[h], qr_s[h], pa[h]], axis=1)
        qr_b[h] = dot(line, seam[h]).astype(bf16)

    @pl.when(inner)
    def _():
        for i, (there, other, inside) in enumerate((beside[0], middle, beside[1])):
            @pl.when(other)
            def _():
                strip_copies[i].wait_recv()

            if i != 1:
                @pl.when(jnp.logical_not(other))
                def _():
                    pw_mir[i] = pw[...]

        mirror_skew = skewed(sent_taps(pw_mir[1, 0, :, LANES:]), ROWS - HALF)
        for m in range(M):
            rows = jnp.concatenate([pw_mir[0, m], pw_mir[1, m], pw_mir[2, m]], axis=0)
            pb_mir[m] = dot(mirror_skew[:, : 3 * ROWS], rows).astype(bf16)

    x = dot(bd[...], w[...])
    for copy in ring_a:
        copy.wait_recv()
    for copy in ring_mid:
        copy.start()
    side_tiles = LANES // ROWS

    @pl.when(is_hub)
    def _():
        pall_a[t] = pa[hub]
        wait_at_hub(pall_a, 0)
        near = jnp.concatenate([pall_a[:side_tiles], pall_a[T - side_tiles :]], axis=0)
        wh[hub, 0] = gather_rows(
            0, MH, near.reshape(WIDE, WIDE), (end_blocks(w[...]), wh[hub, 0])
        ).astype(bf16)

    x_ends = (end_blocks(x) + dot(bdh[0], wh[0, 0]) + dot(bdh[1], wh[1, 0])).astype(bf16)
    xs[:, :LANES] = x_ends[:, :LANES]
    xs[:, N - LANES : N] = x_ends[:, LANES:]

    for m, value in enumerate(pack_ends(xs[:, :N])):
        pb[m] = value
    mirror_b = remote(pb, pb_mir, mir_s.at[0], mir_r.at[0], mirror)

    def to_strips(member, face, at):
        return jnp.where(at < HALF, LANES * member + 16 * face + at, -1)

    @pl.when(is_hub)
    def _():
        mirror_b.start()
        mirror_b.wait_recv()

    xs[:, N:] = spread(arrive_cols(pb, pb_mir, qr_b))

    zrim = jnp.zeros((MR, LANES), f32)
    for at in (0, N - LANES):
        here = slice(at, at + LANES)
        value = jnp.concatenate([xs[:, here], xs[:, N:]], axis=1)
        weights = jnp.concatenate([dmat[here, here], dmat[here, N:]], axis=1)
        zrim = zrim + dot(dot_nt(value, weights).astype(bf16), dmat[here, N:])
    rims = pack(zrim)
    for m, value in enumerate(rims):
        pc[m] = value
    mirror_c = remote(pc, pc_mir, mir_s.at[1], mir_r.at[1], mirror)
    hub_messages(rims, pa_c)
    to_hubs_c = hub_copies(pa_c, pall_c, 1)
    start_to_hubs(to_hubs_c)
    mirror_c.start()

    for copy in ring_mid:
        copy.wait_recv()

    @pl.when(is_hub)
    def _():
        middle_cols = pall_a[side_tiles : T - side_tiles].reshape(N - WIDE, WIDE)
        wh[hub, 1] = gather_rows(
            0, MH, middle_cols, (w[:, LANES : N - LANES], wh[hub, 1])
        ).astype(bf16)

    x_mid = x[:, LANES : N - LANES] + dot(bdh[0], wh[0, 1]) + dot(bdh[1], wh[1, 1])
    xs[:, LANES : N - LANES] = x_mid.astype(bf16)
    y = dot_nt(xs[...], dmat[...]).astype(bf16)
    zacc[...] = dot(y, dmat[:, :N])

    def end_columns(flat, width):
        at, end = iota((WIDE, 2 * width), 0), iota((WIDE, 2 * width), 1)
        pick = onehot(at == jnp.where(end < width, end, end + WIDE - 2 * width))
        both = iota((2 * width, 2 * width), 0) + iota((2 * width, 2 * width), 1)
        near = jnp.concatenate([flat[:, :LANES], flat[:, N - LANES :]], axis=1)
        near = dot(near, pick).astype(bf16)
        return near, dot(near, onehot(both == 2 * width - 1)).astype(bf16)

    def near_strips(flat, width, parts, layer_of, lanes_of):
        near, far = end_columns(flat, width)
        shape = (flat.shape[0], WIDE)
        member, face, at = parts(iota(shape, 0))
        here = lanes_of(member, face, layer_of(at)) == iota(shape, 1)
        turned = pick_face(face, hub_flips) == 1
        value = dot_tn(near, onehot(here & jnp.logical_not(turned)))
        value = value + dot_tn(far, onehot(here & turned))
        return value.astype(bf16).reshape(2 * width // ROWS, ROWS, WIDE)

    @pl.when(is_hub)
    def _():
        value = turn_rows(zacc[...].astype(bf16), to_strips)
        qc[...] = value.astype(bf16).reshape(T, ROWS, WIDE)

        def send(there):
            @pl.when((there > 0) & (there < T - 1))
            def _():
                remote(qc.at[there], qr_c.at[hub], sc_s.at[2], sc_r.at[2, hub], there).start()

        each_tile(send)

    ring_d = [
        remote(sp.at[0], drh.at[1], ring_s.at[4], ring_r.at[4], prev),
        remote(sp.at[1], drh.at[0], ring_s.at[5], ring_r.at[5], nxt),
    ]
    ring_late = [
        remote(late.at[0], late_r.at[1], ring_s.at[6], ring_r.at[6], prev),
        remote(late.at[1], late_r.at[0], ring_s.at[7], ring_r.at[7], nxt),
    ]

    def start_spills(value):
        for side in range(2):
            sp[side] = dot(bdht[side], value).astype(bf16)
            ring_d[side].start()

    @pl.when(inner)
    def _():
        start_spills(zacc[...].astype(bf16))

    mirror_c.wait_recv()

    @pl.when(is_hub)
    def _():
        pall_c[t] = pa_c[hub]
        wait_at_hub(pall_c, 1)
        zacc[...] += gather_rows(3, MR, pall_c[...].reshape(N, WIDE), ())

    ends = dot_nt(spread(arrive_cols(pc, pc_mir, None)), sel)
    zacc[:, :LANES] += ends[:, :LANES]
    zacc[:, N - LANES :] += ends[:, LANES:]

    z = zacc[...].astype(bf16)
    quarter = iota((MH, LANES), 1) >> 5

    def both_ends(value):
        return dot(jnp.concatenate([value[:, :LANES], value[:, N - LANES :]], axis=1), sel)

    @pl.when(is_hub)
    def _():
        start_spills(z)

    z_ends = both_ends(z).astype(bf16)
    for side in range(2):
        value = dot(bdht[side], z_ends)
        late[side] = jnp.where(quarter == 1 - side, value, 0.0).astype(bf16)
        ring_late[side].start()

    hub_d = remote(qd.at[1 - hub], qr_d.at[hub], sc_s.at[3], sc_r.at[3, hub], mirror)

    @pl.when(is_hub)
    def _():
        qd[...] = near_strips(
            sp[hub], ROWS, halo_parts, by_hub(back_halo, forward),
            lambda member, face, at: LANES * member + 16 * face + at,
        )
        qr_d[hub] = qd[hub]
        hub_d.start()

    zacc[...] = dot(bdt[...], z)

    @pl.when(inner)
    def _():
        wait_all(qc, qr_c, 2, (0, T - 1))
        for h in range(2):
            strip = (qr_c[h].astype(f32) + pa_c[h].astype(f32)).astype(bf16)
            qr_d[h] = dot_nt(strip, seam[h, WIDE + LANES :, :]).astype(bf16)

    for copy in ring_d + ring_late:
        copy.wait_recv()

    @pl.when(is_hub)
    def _():
        arrived = gather_rows(4, MH, None, (sp[hub], drh[hub])).astype(bf16)
        drh[hub] = arrived
        late_r[hub] = jnp.where(quarter == hub, both_ends(arrived), 0.0).astype(bf16)

    spill = dot_tn(comp[0], drh[0]) + dot_tn(comp[1], drh[1])
    column = iota((MR, N), 1)
    zacc[...] += jnp.where((column >= HALF) & (column < N - HALF), spill, 0.0)
    spill_ends = dot_tn(comp[0], late_r[0]) + dot_tn(comp[1], late_r[1])
    ends = dot_nt(spill_ends.astype(bf16), sel)
    zacc[:, :LANES] += ends[:, :LANES]
    zacc[:, N - LANES :] += ends[:, LANES:]
    @pl.when(is_hub)
    def _():
        remote(qd.at[0], qr_d.at[1 - hub], sc_s.at[3], sc_r.at[3, 1 - hub], mirror).wait_recv()

    ends = dot_nt(spread(arrive_cols(None, None, qr_d)), sel)
    zacc[:, :LANES] += ends[:, :LANES]
    zacc[:, N - LANES :] += ends[:, LANES:]

    FR = FACES * ROWS
    total = jnp.zeros((FR, N), f32)
    for m in range(M):
        total = total + pert[m].astype(f32).reshape(FR, N) * zacc[m * FR : (m + 1) * FR, :]
    per_chunk = part.shape[1]
    for u in range(count * per_chunk):
        r, c = u // NB, u % NB
        part[u // per_chunk, u % per_chunk] = total[r * 8 : r * 8 + 8, c * LANES : (c + 1) * LANES]

    order = [12, 13, 14, 15, 10, 11, 8, 9, 4, 5, 6, 7, 2, 3, 1] if count == 16 else range(1, count)
    peers_of_me = [me ^ i for i in order]
    for there in peers_of_me:
        remote(part.at[there], got.at[me], mem_s.at[0], mem_r.at[0], there, "member").start()
    got[me] = part[me]
    others = got.at[pl.ds(0, count - 1)]
    pltpu.make_async_copy(others, others, mem_r.at[0]).wait()
    chunk = got[0]
    for i in range(1, count):
        chunk = chunk + got[i]
    chunk = (chunk * (1.0 / (M * count - 1.0))).reshape(8 * per_chunk, LANES)
    spare = jnp.zeros((mine.shape[0] - 8 * per_chunk, LANES), f32)
    mine[...] = jnp.concatenate([chunk, spare], axis=0).astype(bf16)
    for there in peers_of_me:
        remote(mine, done.at[me], mem_s.at[1], mem_r.at[1], there, "member").start()
    done[me] = mine[...]
    finished = done.at[pl.ds(0, count - 1)]
    pltpu.make_async_copy(finished, finished, mem_r.at[1]).wait()
    for i in range(count):
        block = done[i].astype(f32)
        for k in range(per_chunk):
            r, c = (i * per_chunk + k) // NB, (i * per_chunk + k) % NB
            out[r * 8 : r * 8 + 8, c * LANES : (c + 1) * LANES] = block[8 * k : 8 * k + 8]

    for copy in ring_a + ring_mid + ring_d + ring_late + [mirror_c]:
        copy.wait_send()
    for i, (there, other, inside) in enumerate((beside[0], middle, beside[1])):
        @pl.when(other & inside)
        def _():
            strip_copies[i].wait_send()

    finish_to_hubs(to_hubs_a)
    finish_to_hubs(to_hubs_c)

    @pl.when(is_hub)
    def _():
        finish_scatter(qw, 0)
        far = qc.at[pl.ds(0, T - 2)]
        pltpu.make_async_copy(far, far, sc_s.at[2]).wait()
        mirror_b.wait_send()
        hub_d.wait_send()

    @pl.when(is_second)
    def _():
        finish_scatter(qs, 1)

    pltpu.make_async_copy(others, others, mem_s.at[0]).wait()
    pltpu.make_async_copy(finished, finished, mem_s.at[1]).wait()


def per_device(perturbations, control, band_rows, band_cols, edge_peer, edge_flip):
    T, count = lax.axis_size("tile"), lax.axis_size("member")
    M = perturbations.shape[0]
    N = control.shape[-1]
    MR, MH = M * FACES * ROWS, M * FACES * HALF
    per_chunk = FACES * ROWS * N // (8 * LANES) // count
    vmem, hbm = pl.BlockSpec(memory_space=pltpu.VMEM), pl.BlockSpec(memory_space=pltpu.HBM)
    dma = pltpu.SemaphoreType.DMA
    args = (perturbations, control, band_rows, band_cols.T, edge_peer.T, edge_flip.T)
    result = pl.pallas_call(
        functools.partial(whole_kernel, T, M, count),
        out_shape=jax.ShapeDtypeStruct((FACES * ROWS, N), f32),
        in_specs=[hbm] * 6,
        out_specs=vmem,
        scratch_shapes=[
            pltpu.VMEM(args[0].shape, bf16),
            pltpu.VMEM(args[1].shape, f32),
            pltpu.VMEM(args[2].shape, f32),
            pltpu.VMEM(args[3].shape, f32),
            pltpu.SMEM(args[4].shape, i32),
            pltpu.SMEM(args[5].shape, i32),
            pltpu.VMEM((MR, N), bf16),
            pltpu.VMEM((2, 2, MH, WIDE), bf16),
            pltpu.VMEM((2, 2, MH, WIDE), bf16),
            pltpu.VMEM((2, ROWS, WIDE), bf16),
            pltpu.VMEM((T, ROWS, WIDE), bf16),
            pltpu.VMEM((M, ROWS, WIDE), bf16),
            pltpu.VMEM((3, M, ROWS, WIDE), bf16),
            pltpu.VMEM((T, ROWS, WIDE), bf16),
            pltpu.VMEM((2, ROWS, WIDE), bf16),
            pltpu.VMEM((T, ROWS, LANES), bf16),
            pltpu.VMEM((2, ROWS, LANES), bf16),
            pltpu.VMEM((M, ROWS, WIDE), bf16),
            pltpu.VMEM((M, ROWS, WIDE), bf16),
            pltpu.VMEM((2, ROWS, WIDE), bf16),
            pltpu.VMEM((M, ROWS, WIDE), bf16),
            pltpu.VMEM((M, ROWS, WIDE), bf16),
            pltpu.VMEM((2, ROWS, WIDE), bf16),
            pltpu.VMEM((T, ROWS, WIDE), bf16),
            pltpu.VMEM((T, ROWS, WIDE), bf16),
            pltpu.VMEM((2, ROWS, WIDE), bf16),
            pltpu.VMEM((2, MH, N), bf16),
            pltpu.VMEM((2, MH, N), bf16),
            pltpu.VMEM((2, MH, LANES), bf16),
            pltpu.VMEM((2, MH, LANES), bf16),
            pltpu.VMEM((2, ROWS, WIDE), bf16),
            pltpu.VMEM((2, ROWS, WIDE), bf16),
            pltpu.VMEM((N, N + LANES), bf16),
            pltpu.VMEM((MR, N + LANES), bf16),
            pltpu.VMEM((MR, N), f32),
            pltpu.VMEM((MR, MR), bf16),
            pltpu.VMEM((2, MR, MH), bf16),
            pltpu.VMEM((MR, MR), bf16),
            pltpu.VMEM((2, MH, MR), bf16),
            pltpu.VMEM((N, N), bf16),
            pltpu.VMEM((3, WIDE, WIDE), bf16),
            pltpu.VMEM((2, 2 * WIDE + LANES, WIDE), bf16),
            pltpu.VMEM((2 * WIDE + LANES, WIDE), f32),
            pltpu.VMEM((2 * WIDE + LANES, LANES), bf16),
            pltpu.VMEM((6, 2 * MR, WIDE), bf16),
            pltpu.VMEM((count, per_chunk, 8, LANES), f32),
            pltpu.VMEM((count, per_chunk, 8, LANES), f32),
            pltpu.VMEM((-(-per_chunk // 2) * 16 + 16 * (per_chunk % 2 == 0), LANES), bf16),
            pltpu.VMEM((count, -(-per_chunk // 2) * 16 + 16 * (per_chunk % 2 == 0), LANES), bf16),
            dma((6,)),
            dma((8,)), dma((8,)),
            dma((2, 2)), dma((2,)),
            dma((2,)), dma((2,)),
            dma((3,)), dma((3,)),
            dma((6,)), dma((4, 2)),
            dma((2,)), dma((2,)),
        ],
        compiler_params=pltpu.CompilerParams(
            collective_id=0, has_side_effects=True, vmem_limit_bytes=60 * 1024 * 1024
        ),
        name="covariance",
    )(*args)
    return result.reshape(control.shape)


def solution(mesh):
    return jax.shard_map(
        per_device,
        mesh=mesh,
        in_specs=(
            P("member", None, "tile", None),
            P(None, "tile", None),
            P("tile", None),
            P(),
            P(),
            P(),
        ),
        out_specs=P(None, "tile", None),
        check_vma=False,
    )
```
